32 devices in a mesh: section: 2 (over x), seq: 4 (over y, core), fsdp: 4 (over z).
Axes of the slice: x: 2, y: 2, z: 4, core: 2. Of those that a mesh axis runs over, the one named last changes fastest.
Arguments:
- tokens: bfloat16 [2, 4, 1024, 1536], P(None, 'fsdp', 'seq'), may hold values from -6 to 6
- in_weight: bfloat16 [2, 1536, 4608], P('section', 'fsdp'), may hold values from -0.15625 to 0.15625
- conv_kernel: bfloat16 [2, 1536, 3], P('section', 'fsdp'), may hold values from -3 to 3
- out_weight: bfloat16 [2, 1536, 1536], P('section', 'fsdp'), may hold values from -0.15625 to 0.15625
- gate_weight: bfloat16 [2, 1536, 6912], P('section', 'fsdp'), may hold values from -0.15625 to 0.15625
- up_weight: bfloat16 [2, 1536, 6912], P('section', 'fsdp'), may hold values from -0.15625 to 0.15625
- down_weight: bfloat16 [2, 6912, 1536], P('section', 'fsdp'), may hold values from -0.078125 to 0.078125
- mixer_gain: bfloat16 [2, 1536], P('section', 'fsdp'), may hold values from 0.099609375 to 1.8984375
- ffn_gain: bfloat16 [2, 1536], P('section', 'fsdp'), may hold values from 0.099609375 to 1.8984375
- cotangent: bfloat16 [2, 4, 1024, 1536], P(None, 'fsdp', 'seq'), may hold values from -6 to 6
Outputs:
- section_out: bfloat16 [2, 2, 4, 1024, 1536], P('section', None, 'fsdp', 'seq')
- section_grad: float32 [2, 2, 4, 1024, 1536], P('section', None, 'fsdp', 'seq')
- in_weight_grad: float32 [2, 1536, 4608], P('section', 'fsdp')
- conv_kernel_grad: float32 [2, 1536, 3], P('section', 'fsdp')
- out_weight_grad: float32 [2, 1536, 1536], P('section', 'fsdp')
- gate_weight_grad: float32 [2, 1536, 6912], P('section', 'fsdp')
- up_weight_grad: float32 [2, 1536, 6912], P('section', 'fsdp')
- down_weight_grad: float32 [2, 6912, 1536], P('section', 'fsdp')
- mixer_gain_grad: float32 [2, 1536], P('section', 'fsdp')
- ffn_gain_grad: float32 [2, 1536], P('section', 'fsdp')
The draws below stay inside these ranges and needn't reach their ends.
All inputs are finite; a program needn't handle non-finite values.
Results may differ from the reference program's by a relative error of at most 0.022.
Values may be sent and summed in bfloat16 or wider, within the bound.
A program may use at most 448 MiB of HBM per device.

```python
import jax
import jax.numpy as jnp
from jax import lax

D = 1536
FF = 6912
KERNEL = 3
MB = 2
SEQ_LEN = 1024
LAYERS = 2
SEQS = 4


def shard_levels(key, extent, shards, least, largest):
    level = 1.0
    for position, parts in shards:
        heights = jax.random.uniform(jax.random.fold_in(jax.random.fold_in(key, 6), position), (parts,), jnp.float32, least / len(shards), largest / len(shards))
        level = level * jnp.repeat(jnp.exp(heights), extent[position] // parts).reshape((-1,) + (1,) * (len(extent) - 1 - position))
    return level


def bell_draw(own_key, extent, scale, most, pieces=(), held_as=jnp.bfloat16):
    gain = shard_levels(own_key, extent, pieces, -0.22, 0.18) if pieces else 1.0
    array = jax.random.normal(own_key, extent, jnp.float32) * scale * gain
    return jnp.minimum(jnp.maximum(array, -most), most).astype(held_as)


def setup_inputs(seed: int = 0) -> dict:
    seeds = jax.random.split(jax.random.key(seed), 11)
    tokens = bell_draw(seeds[0], (MB, SEQS, SEQ_LEN, D), 1.0, 6.0, ((1, 4), (2, 4)))
    in_weight = bell_draw(seeds[1], (LAYERS, D, 3 * D), D ** -0.5, 0.15625, ((0, 2), (1, 4)))
    conv_kernel = bell_draw(seeds[2], (LAYERS, D, KERNEL), 0.6, 3.0, ((0, 2), (1, 4)))
    out_weight = bell_draw(seeds[3], (LAYERS, D, D), D ** -0.5, 0.15625, ((0, 2), (1, 4)))
    gate_weight = bell_draw(seeds[4], (LAYERS, D, FF), D ** -0.5, 0.15625, ((0, 2), (1, 4)))
    up_weight = bell_draw(seeds[5], (LAYERS, D, FF), D ** -0.5, 0.15625, ((0, 2), (1, 4)))
    down_weight = bell_draw(seeds[6], (LAYERS, FF, D), FF ** -0.5, 0.078125, ((0, 2), (1, 4)))
    mixer_gain = jnp.clip(1.0 + 0.18 * jax.random.normal(seeds[7], (LAYERS, D), jnp.float32), 0.099609375, 1.8984375).astype(jnp.bfloat16)
    ffn_gain = jnp.clip(1.0 + 0.18 * jax.random.normal(seeds[8], (LAYERS, D), jnp.float32), 0.099609375, 1.8984375).astype(jnp.bfloat16)
    cotangent = bell_draw(seeds[9], (MB, SEQS, SEQ_LEN, D), 1.0, 6.0, ((1, 4), (2, 4)))
    return dict(tokens=tokens, in_weight=in_weight, conv_kernel=conv_kernel, out_weight=out_weight, gate_weight=gate_weight, up_weight=up_weight, down_weight=down_weight, mixer_gain=mixer_gain, ffn_gain=ffn_gain, cotangent=cotangent)


EPSILON = 1e-05

@jax.custom_vjp
def low(v):
    return lax.optimization_barrier(v.astype(jnp.bfloat16)).astype(jnp.float32)

@jax.custom_vjp
def low_back(v):
    return v

def low_keep(v):
    return (low(v), None)

def low_pass(kept, grad):
    return (grad,)

def back_keep(v):
    return (v, None)

def back_low(kept, grad):
    return (low(grad),)
low.defvjp(low_keep, low_pass)
low_back.defvjp(back_keep, back_low)

def product(left, right):
    return jnp.einsum('...d,de->...e', left, right, precision=lax.Precision.HIGHEST)

def rms_scale(stream):
    return lax.rsqrt(lax.optimization_barrier(jnp.mean(stream * stream, -1, keepdims=True)) + EPSILON)

def block_layer(stream, layer_params):
    in_matrix, conv_taps, out_matrix, gate_matrix, up_matrix, down_matrix, mixer_scale, ffn_scale = layer_params
    model_width = stream.shape[-1]
    seq_length = stream.shape[-2]
    normed = low(stream * rms_scale(stream) * mixer_scale)
    projected = low_back(product(normed, in_matrix))
    b_gate = projected[..., :model_width]
    c_gate = projected[..., model_width:2 * model_width]
    x_value = projected[..., 2 * model_width:]
    conv_input = low(b_gate * x_value)
    padded = jnp.pad(conv_input, ((0, 0), (2, 0), (0, 0)))
    conv_out = conv_taps[:, 0] * padded[:, 0:seq_length] + conv_taps[:, 1] * padded[:, 1:seq_length + 1] + conv_taps[:, 2] * padded[:, 2:seq_length + 2]
    gated = low(c_gate * conv_out)
    middle = stream + low_back(product(gated, out_matrix))
    normed_ffn = low(middle * rms_scale(middle) * ffn_scale)
    gate_value = low_back(product(normed_ffn, gate_matrix))
    up_value = low_back(product(normed_ffn, up_matrix))
    hidden = low(jax.nn.silu(gate_value) * up_value)
    return middle + low_back(product(hidden, down_matrix))

def reference(tokens, in_weight, conv_kernel, out_weight, gate_weight, up_weight, down_weight, mixer_gain, ffn_gain, cotangent):
    params = tuple((tensor.astype(jnp.float32) for tensor in (in_weight, conv_kernel, out_weight, gate_weight, up_weight, down_weight, mixer_gain, ffn_gain)))
    inputs = tokens.astype(jnp.float32)
    layer_count = in_weight.shape[0]
    offsets = jnp.zeros((inputs.shape[0], layer_count - 1) + inputs.shape[1:], jnp.float32)

    def forward(inputs, offsets, params):

        def one_slot(unused, slot_item):
            stream, shifts = slot_item
            handed = []
            for layer_index in range(layer_count):
                layer_params = tuple((tensor[layer_index] for tensor in params))
                stream = block_layer(stream, layer_params)
                if layer_index < layer_count - 1:
                    rounded = low(stream)
                    handed.append(rounded)
                    stream = low_back(rounded) + shifts[layer_index]
            return (unused, (stream, jnp.stack(handed + [stream])))
        _, (last_out, section_values) = lax.scan(jax.checkpoint(one_slot), jnp.zeros((), jnp.float32), (inputs, offsets))
        return (last_out, section_values)
    last_out, pullback, section_values = jax.vjp(forward, inputs, offsets, params, has_aux=True)
    grad_inputs, grad_offsets, grad_params = pullback(cotangent.astype(jnp.float32))
    section_out = jnp.moveaxis(section_values, 1, 0).astype(jnp.bfloat16)
    section_grad = jnp.concatenate([grad_inputs[None], jnp.moveaxis(grad_offsets, 1, 0)], 0)
    return (section_out, section_grad, grad_params[0], grad_params[1], grad_params[2], grad_params[3], grad_params[4], grad_params[5], grad_params[6], grad_params[7])
```

```python
import jax
import jax.numpy as jnp
from jax import lax
from jax.sharding import PartitionSpec as P

EPSILON = 1e-05
PLANE = ("section", "seq")


def flip(value, bits):
    count = lax.axis_size("section") * lax.axis_size("seq")
    return lax.ppermute(value, PLANE, [(source, source ^ bits) for source in range(count)])


def flip_by_core(value, even_bits, odd_bits):
    count = lax.axis_size("section") * lax.axis_size("seq")
    pairs = [(source, source ^ (odd_bits if source & 1 else even_bits)) for source in range(count)]
    return lax.ppermute(value, PLANE, pairs)


def chip_bits():
    bits = [lax.axis_size("seq")]
    step = lax.axis_size("seq") // 2
    while step > 1:
        bits.append(step)
        step //= 2
    return bits


def half_units():
    units = [0]
    for bits in chip_bits():
        units = units + [unit | bits for unit in units]
    return units


def spread_chips(own, odd):
    bits = chip_bits()
    if len(bits) == 2:
        first = flip(own, bits[0])
        second = flip(own, bits[1])
        third = flip_by_core(jnp.where(odd, second, first), bits[1], bits[0])
        return jnp.concatenate([own, first, second, third], 0)
    held = own
    for step in bits:
        held = jnp.concatenate([held, flip(held, step)], 0)
    return held


def spread(own, odd):
    near = spread_chips(own, odd)
    return near, flip(near, 1)


def collect(near, far, odd):
    bits = chip_bits()
    if len(bits) == 2:
        rows = near.shape[0] // 4
        held = near
        third = flip_by_core(held[3 * rows :].astype(jnp.bfloat16), bits[1], bits[0]).astype(jnp.float32)
        first = held[rows : 2 * rows] + jnp.where(odd, 0.0, third)
        second = held[2 * rows : 3 * rows] + jnp.where(odd, third, 0.0)
        first = flip(first.astype(jnp.bfloat16), bits[0]).astype(jnp.float32)
        second = flip(second.astype(jnp.bfloat16), bits[1]).astype(jnp.float32)
        return held[:rows] + first + second
    held = near
    for step in reversed(bits):
        rows = held.shape[0] // 2
        held = held[:rows] + flip(held[rows:].astype(jnp.bfloat16), step).astype(jnp.float32)
    return held


def rms_scale(stream):
    return lax.rsqrt(jnp.mean(stream * stream, -1, keepdims=True) + EPSILON)


def times(left, matrix):
    return jnp.dot(left, matrix, preferred_element_type=jnp.float32)


def times_transposed(left, matrix):
    return lax.dot_general(
        left, matrix, (((1,), (1,)), ((), ())), preferred_element_type=jnp.float32
    )


def row_products(left, right):
    return lax.dot_general(
        left, right, (((0,), (0,)), ((), ())), preferred_element_type=jnp.float32
    ).astype(jnp.bfloat16)


def normed_with(stream, gain):
    return (stream * rms_scale(stream) * gain).astype(jnp.bfloat16)


def pick_columns(matrix, share, width, count):
    shards = lax.axis_size("fsdp")
    part = width // shards // count
    return jnp.concatenate(
        [
            lax.dynamic_slice(
                matrix, (0, start + shard * (width // shards) + share * part), (matrix.shape[0], part)
            )
            for start in range(0, matrix.shape[1], width)
            for shard in range(shards)
        ],
        1,
    )


def pick_rows(matrix, share, count):
    part = matrix.shape[0] // count
    return lax.dynamic_slice(matrix, (share * part, 0), (part, matrix.shape[1]))


def body(
    tokens,
    in_weight,
    conv_kernel,
    out_weight,
    gate_weight,
    up_weight,
    down_weight,
    mixer_gain,
    ffn_gain,
    cotangent,
):
    bf16, f32 = jnp.bfloat16, jnp.float32
    x_index = lax.axis_index("section")
    q_index = lax.axis_index("seq")
    seq_count = lax.axis_size("seq")
    count = lax.axis_size("section") * seq_count
    shards = lax.axis_size("fsdp")
    share = x_index * seq_count + q_index
    odd = (q_index % 2) == 1
    first_plane = x_index == 0
    width = tokens.shape[3]
    rows = tokens.shape[2]
    hidden_width = gate_weight.shape[2]
    shard_rows = width // shards
    units = half_units()
    half = len(units)

    small = jnp.concatenate(
        [mixer_gain, ffn_gain, conv_kernel[0].T], 0
    )
    small = lax.all_gather(small, ("section", "fsdp"), axis=0)
    small = small.reshape(2, shards, 5, shard_rows).transpose(0, 2, 1, 3).astype(f32)
    whole = small.reshape(2, 5, width)
    part = shard_rows // count
    taps_all = lax.dynamic_slice(
        small[:, 2:].reshape(2, 3, shards, count, part),
        (0, 0, 0, share, 0),
        (2, 3, shards, 1, part),
    ).reshape(2, 3, shards * part)

    other = share ^ seq_count

    def by_block(make):
        kept, sent = make(share), flip(make(other), seq_count)
        return jnp.where(first_plane, kept, sent), jnp.where(first_plane, sent, kept)

    def mixer_share(index):
        columns = pick_columns(in_weight[0], index, width, count)
        return jnp.concatenate(
            [columns, pick_rows(out_weight[0], index, count).reshape(shard_rows, -1)], 1
        )

    def ffn_share(index):
        return jnp.concatenate(
            [
                pick_columns(gate_weight[0], index, hidden_width, count),
                pick_columns(up_weight[0], index, hidden_width, count),
            ],
            1,
        )

    def down_share(index):
        return pick_rows(down_weight[0], index, count)

    in_columns = 3 * width // count
    ffn_columns = hidden_width // count
    mixer_parts = by_block(mixer_share)
    ffn_parts = by_block(ffn_share)
    down_parts = by_block(down_share)
    weights = []
    for block in range(2):
        mixer = lax.all_gather(mixer_parts[block], "fsdp", axis=0, tiled=True)
        pair = lax.all_gather(ffn_parts[block], "fsdp", axis=0, tiled=True)
        down = lax.all_gather(down_parts[block], "fsdp", axis=0, tiled=True)
        out = mixer[:, in_columns:].reshape(-1, width)
        weights.append((mixer[:, :in_columns], out, pair, down))

    near_ids = jnp.stack([share ^ unit for unit in units])
    far_ids = near_ids ^ 1
    ids = jnp.concatenate([near_ids, far_ids])
    has_before = (ids % seq_count) > 0
    has_after = (ids % seq_count) < seq_count - 1
    before_pick = (ids[None, :] == (ids - 1)[:, None]) & has_before[:, None]
    after_pick = (ids[None, :] == (ids + 1)[:, None]) & has_after[:, None]

    def pick_units(mask, edge):
        return jnp.sum(jnp.where(mask[:, :, None, None], edge[None].astype(f32), 0.0), 1)

    mine = lax.dynamic_index_in_dim(tokens[:, 0], x_index, 0, False)
    theirs = lax.dynamic_index_in_dim(tokens[:, 0], 1 - x_index, 0, False)

    def spread_replicated(mine, theirs):
        near = jnp.concatenate([mine, theirs], 0)
        for step in chip_bits()[1:]:
            near = jnp.concatenate([near, flip(near, step)], 0)
        return near, flip(near, 1)

    entry = spread_replicated(mine, theirs)
    stream = mine.astype(f32)
    saved = []
    outputs = []
    for block in range(2):
        in_matrix, out_matrix, pair_matrix, down_matrix = weights[block]
        mixer_scale, ffn_scale = whole[block, 0], whole[block, 1]
        taps = taps_all[block]
        if block == 0:
            normed = [normed_with(piece.astype(f32), mixer_scale) for piece in entry]
        else:
            normed = spread(normed_with(stream, mixer_scale), odd)
        projected = jnp.concatenate([times(piece, in_matrix) for piece in normed], 0)
        channels = in_columns // 3
        b_gate = projected[:, :channels]
        c_gate = projected[:, channels : 2 * channels]
        x_value = projected[:, 2 * channels :]
        conv_input = (b_gate * x_value).astype(bf16).reshape(2 * half, rows, channels)
        earlier = pick_units(before_pick, conv_input[:, -2:])
        extended = jnp.concatenate([earlier, conv_input.astype(f32)], 1)
        conv_out = (
            taps[0] * extended[:, :-2] + taps[1] * extended[:, 1:-1] + taps[2] * extended[:, 2:]
        )
        c_units = c_gate.reshape(2 * half, rows, channels)
        gated = (c_units * conv_out).astype(bf16).reshape(2, half * rows, channels)
        far = flip(times(gated[1], out_matrix).astype(bf16), 1).astype(f32)
        near = times(gated[0], out_matrix) + far
        middle = stream + collect(near, None, odd)
        scale_ffn = rms_scale(middle)
        normed_ffn = spread((middle * scale_ffn * ffn_scale).astype(bf16), odd)
        pairs = [times(piece, pair_matrix) for piece in normed_ffn]
        hidden = [
            (jax.nn.silu(piece[:, :ffn_columns]) * piece[:, ffn_columns:]).astype(bf16)
            for piece in pairs
        ]
        far = flip(times(hidden[1], down_matrix).astype(bf16), 1).astype(f32)
        near = times(hidden[0], down_matrix) + far
        result = middle + collect(near, None, odd)
        outputs.append(result.astype(bf16))
        saved.append(
            (stream, normed, projected, extended, conv_out, gated, middle, scale_ffn, normed_ffn, pairs, hidden)
        )
        stream = result.astype(bf16).astype(f32)

    mine = lax.dynamic_index_in_dim(cotangent[:, 0], x_index, 0, False)
    theirs = lax.dynamic_index_in_dim(cotangent[:, 0], 1 - x_index, 0, False)
    upstream = mine.astype(f32)
    grad_units = spread_replicated(mine, theirs)
    stream_grads = [None, None]
    small_grads = [None, None]
    matrix_grads = [None, None]

    def over_z(value):
        return lax.psum_scatter(value, "fsdp", scatter_dimension=0, tiled=True)

    for block in (1, 0):
        in_matrix, out_matrix, pair_matrix, down_matrix = weights[block]
        mixer_scale, ffn_scale = whole[block, 0], whole[block, 1]
        taps = taps_all[block]
        (stream, normed, projected, extended, conv_out, gated, middle, scale_ffn, normed_ffn, pairs, hidden) = saved[block]
        down_grad = over_z(row_products(jnp.concatenate(hidden, 0), jnp.concatenate(grad_units, 0)))
        grad_pairs = []
        for piece, grad in zip(pairs, grad_units):
            gate_value, up_value = piece[:, :ffn_columns], piece[:, ffn_columns:]
            grad_hidden = times_transposed(grad, down_matrix)
            sigmoid_gate = jax.nn.sigmoid(gate_value)
            grad_gate = (
                grad_hidden * up_value * sigmoid_gate * (1.0 + gate_value * (1.0 - sigmoid_gate))
            ).astype(bf16)
            grad_up = (grad_hidden * gate_value * sigmoid_gate).astype(bf16)
            grad_pairs.append(jnp.concatenate([grad_gate, grad_up], 1))
        far = flip(times_transposed(grad_pairs[1], pair_matrix).astype(bf16), 1).astype(f32)
        near = times_transposed(grad_pairs[0], pair_matrix) + far
        grad_normed_ffn = collect(near, None, odd)
        pair_grad = over_z(
            row_products(jnp.concatenate(normed_ffn, 0), jnp.concatenate(grad_pairs, 0))
        )
        ffn_gain_part = jnp.sum(grad_normed_ffn * middle * scale_ffn, 0)
        weighted_ffn = ffn_scale * grad_normed_ffn
        grad_middle = (
            upstream
            + scale_ffn * weighted_ffn
            - middle * scale_ffn**3 * jnp.mean(weighted_ffn * middle, -1, keepdims=True)
        )
        mixer_grad = spread(grad_middle.astype(bf16), odd)
        grad_gated = jnp.concatenate(
            [times_transposed(piece, out_matrix) for piece in mixer_grad], 0
        ).reshape(2 * half, rows, channels)
        b_gate = projected[:, :channels].reshape(2 * half, rows, channels)
        c_gate = projected[:, channels : 2 * channels].reshape(2 * half, rows, channels)
        x_value = projected[:, 2 * channels :].reshape(2 * half, rows, channels)
        grad_cgate = grad_gated * conv_out
        grad_conv = grad_gated * c_gate
        later = pick_units(after_pick, grad_conv[:, :2])
        grad_extended = jnp.concatenate([grad_conv, later], 1)
        grad_input = (
            taps[0] * grad_extended[:, 2:]
            + taps[1] * grad_extended[:, 1:-1]
            + taps[2] * grad_extended[:, :-2]
        )
        taps_part = jnp.stack(
            [jnp.sum(grad_conv * extended[:, tap : tap + rows], (0, 1)) for tap in range(3)], 0
        )
        grad_projected = (
            jnp.concatenate([grad_input * x_value, grad_cgate, grad_input * b_gate], 2)
            .astype(bf16)
            .reshape(2, half * rows, in_columns)
        )
        far = flip(times_transposed(grad_projected[1], in_matrix).astype(bf16), 1).astype(f32)
        near = times_transposed(grad_projected[0], in_matrix) + far
        grad_normed = collect(near, None, odd)
        in_grad = row_products(
            jnp.concatenate(normed, 0), grad_projected.reshape(2 * half * rows, in_columns)
        )
        out_grad = row_products(
            gated.reshape(2 * half * rows, channels), jnp.concatenate(mixer_grad, 0)
        )
        mixer_sum = over_z(jnp.concatenate([in_grad, out_grad.reshape(width, -1)], 1))
        scale_mix = rms_scale(stream)
        mixer_gain_part = jnp.sum(grad_normed * stream * scale_mix, 0)
        weighted_mix = mixer_scale * grad_normed
        grad_stream = (
            grad_middle
            + scale_mix * weighted_mix
            - stream * scale_mix**3 * jnp.mean(weighted_mix * stream, -1, keepdims=True)
        )
        stream_grads[block] = grad_stream
        own_mask = (jnp.arange(count) == share)[None, None, :, None]
        taps_placed = jnp.where(own_mask, taps_part.reshape(3, shards, 1, part), 0.0)
        small_grads[block] = jnp.concatenate(
            [mixer_gain_part[None], ffn_gain_part[None], taps_placed.reshape(3, width)], 0
        )
        matrix_grads[block] = (down_grad, pair_grad, mixer_sum)
        if block == 1:
            sent = grad_stream.astype(bf16)
            upstream = sent.astype(f32)
            grad_units = spread(sent, odd)

    section_count = lax.axis_size("section")

    def to_owners(value, block):
        over = [
            ((1 - block) * seq_count + seq, block * seq_count + seq) for seq in range(seq_count)
        ]
        units_held = jnp.stack([value, lax.ppermute(value, PLANE, over)], 0)
        step = 1
        inside = chip_bits()[1:] + [1]
        for bits in inside:
            pairs = [
                (block * seq_count + seq, block * seq_count + (seq ^ bits))
                for seq in range(seq_count)
            ]
            units_held = jnp.concatenate([units_held, lax.ppermute(units_held, PLANE, pairs)], 0)
        return units_held

    def both_owners(index):
        first = to_owners(matrix_grads[0][index], 0)
        second = to_owners(matrix_grads[1][index], 1)
        return jnp.where(first_plane, first, second)

    relative = [0, seq_count]
    for bits in chip_bits()[1:] + [1]:
        relative = relative + [unit | bits for unit in relative]
    position = {unit: place for place, unit in enumerate(relative)}
    order = jnp.stack([jnp.int32(0)] * 0 + [jnp.int32(position[unit]) for unit in range(count)])
    absolute = order[jnp.arange(count) ^ share]

    def in_order(value):
        return jnp.take(value, absolute, axis=0)

    def columns_of(value, blocks):
        piece = value.reshape(count, shard_rows, blocks, shards, -1)
        return piece.transpose(1, 2, 3, 0, 4).reshape(shard_rows, -1).astype(f32)

    down_grad = in_order(both_owners(0)).reshape(-1, width).astype(f32)
    pair_grad = in_order(both_owners(1))
    gate_grad = columns_of(pair_grad[..., :ffn_columns], 1)
    up_grad = columns_of(pair_grad[..., ffn_columns:], 1)
    mixer_sum = in_order(both_owners(2))
    in_grad = columns_of(mixer_sum[..., :in_columns], 3)
    out_grad = mixer_sum[..., in_columns:].reshape(shard_rows, width).astype(f32)

    smalls = lax.psum(jnp.stack(small_grads), ("section", "seq", "fsdp"))
    smalls = lax.dynamic_slice(
        smalls, (x_index, 0, lax.axis_index("fsdp") * shard_rows), (1, 5, shard_rows)
    )[0]

    def by_slot(values, dtype):
        kept = jnp.where(first_plane, values[0], values[1]).astype(dtype)
        sent = jnp.where(first_plane, values[1], values[0]).astype(bf16)
        other = flip(sent, seq_count).astype(dtype)
        return jnp.stack(
            [jnp.where(first_plane, kept, other), jnp.where(first_plane, other, kept)], 0
        )

    return (
        by_slot(outputs, bf16)[None, :, None],
        by_slot(stream_grads, f32)[None, :, None],
        in_grad[None],
        smalls[2:].T[None],
        out_grad[None],
        gate_grad[None],
        up_grad[None],
        down_grad[None],
        smalls[0][None],
        smalls[1][None],
    )


def solution(mesh):
    placed = (
        P(None, "fsdp", "seq", None),
        P("section", "fsdp", None),
        P("section", "fsdp", None),
        P("section", "fsdp", None),
        P("section", "fsdp", None),
        P("section", "fsdp", None),
        P("section", "fsdp", None),
        P("section", "fsdp"),
        P("section", "fsdp"),
        P(None, "fsdp", "seq", None),
    )
    return jax.shard_map(
        body,
        mesh=mesh,
        in_specs=placed,
        out_specs=(
            P("section", None, "fsdp", "seq", None),
            P("section", None, "fsdp", "seq", None),
            P("section", "fsdp", None),
            P("section", "fsdp", None),
            P("section", "fsdp", None),
            P("section", "fsdp", None),
            P("section", "fsdp", None),
            P("section", "fsdp", None),
            P("section", "fsdp"),
            P("section", "fsdp"),
        ),
        check_vma=False,
    )
```

```python
import functools

import jax
import jax.numpy as jnp
from jax import lax
from jax.experimental import pallas as pl
from jax.experimental.layout import Layout, with_layout_constraint
from jax.experimental.pallas import tpu as pltpu
from jax.sharding import PartitionSpec as P

EPSILON = 1e-05
PLANE = ("section", "seq")
MESH = pl.DeviceIdType.MESH
VMEM_BYTES = 56 * 2**20
BYTES_PER_US = 3.5e6


def lasting(us):
    return pl.CostEstimate(flops=0, bytes_accessed=int(us * BYTES_PER_US), transcendentals=0)


def tie(*values):
    return lax.optimization_barrier(values)


def kernels_fit():
    return lax.axis_size("section") == 2 and lax.axis_size("seq") == 4


def peers():
    x, q = lax.axis_index("section"), lax.axis_index("seq")
    odd = q % 2
    y = (1 - q // 2) * 2 + odd
    core = {"section": x, "seq": (q // 2) * 2 + (1 - odd)}
    across = {"section": 1 - x, "seq": q}
    beside = {"section": x, "seq": y}
    corner = {"section": x + odd * (1 - 2 * x), "seq": y * (1 - odd) + q * odd}
    return odd, core, across, beside, corner


def greet(others):
    barrier = pltpu.get_barrier_semaphore()
    for other in others:
        pl.semaphore_signal(barrier, inc=1, device_id=other, device_id_type=MESH)
    pl.semaphore_wait(barrier, len(others))


def sum_stages(partial_ref, finish_rows, scratch, chunks):
    from_core, to_corner, from_corner, to_side, from_side, send, recv = scratch
    odd, core, across, beside, corner = peers()
    f32 = jnp.float32
    step = partial_ref.shape[2] // chunks

    def part(k):
        return pl.ds(k * step, step)

    def copy(slot, k, source, target, device):
        return pltpu.make_async_remote_copy(
            src_ref=source,
            dst_ref=target,
            send_sem=send.at[slot, k],
            recv_sem=recv.at[slot, k],
            device_id=device,
            device_id_type=MESH,
        )

    def core_sum(k):
        return copy(0, k, partial_ref.at[1, :, part(k)], from_core.at[:, part(k)], core)

    def corner_sum(k):
        return copy(1, k, to_corner.at[part(k)], from_corner.at[part(k)], corner)

    def across_sum(k):
        return copy(2, k, to_side.at[0, part(k)], from_side.at[0, part(k)], across)

    def beside_sum(k):
        return copy(3, k, to_side.at[1, part(k)], from_side.at[1, part(k)], beside)

    def pair_sum(unit, k):
        return partial_ref[0, unit, part(k)].astype(f32) + from_core[unit, part(k)].astype(f32)

    def sum_corner(k):
        core_sum(k).wait_recv()
        to_corner[part(k)] = pair_sum(3, k).astype(jnp.bfloat16)
        corner_sum(k).start()

    def sum_sides(k):
        corner_sum(k).wait_recv()
        extra = from_corner[part(k)].astype(f32)
        to_side[0, part(k)] = (pair_sum(1, k) + jnp.where(odd == 0, extra, 0.0)).astype(jnp.bfloat16)
        to_side[1, part(k)] = (pair_sum(2, k) + jnp.where(odd == 0, 0.0, extra)).astype(jnp.bfloat16)
        across_sum(k).start()
        beside_sum(k).start()

    def total_rows(k):
        across_sum(k).wait_recv()
        beside_sum(k).wait_recv()
        finish_rows(
            k,
            part(k),
            pair_sum(0, k) + from_side[0, part(k)].astype(f32) + from_side[1, part(k)].astype(f32),
        )

    stages = [lambda k: core_sum(k).start(), sum_corner, sum_sides, total_rows]
    return stages, [core_sum, corner_sum, across_sum, beside_sum]


def run_stages(stages, chunks):
    for tick in range(chunks + len(stages) - 1):
        for place, stage in enumerate(stages):
            if 0 <= tick - place < chunks:
                stage(tick - place)


def sum_scratch(units, rows, width, chunks):
    bf16 = jnp.bfloat16
    return [
        pltpu.VMEM((units, rows, width), bf16),
        pltpu.VMEM((rows, width), bf16),
        pltpu.VMEM((rows, width), bf16),
        pltpu.VMEM((2, rows, width), bf16),
        pltpu.VMEM((2, rows, width), bf16),
        pltpu.SemaphoreType.DMA((4, chunks)),
        pltpu.SemaphoreType.DMA((4, chunks)),
    ]


def exchange_kernel(
    finish, row_ins, shared_ins, row_outs, sum_outs, gather, carried, extra, chunks, partial_ref, *refs
):
    refs = list(refs)
    ins = [refs.pop(0) for _ in range(row_ins)]
    shared = [refs.pop(0) for _ in range(shared_ins)]
    carried_ref = refs.pop(0) if carried else None
    extra_ref, extra_middle = (refs.pop(0), refs.pop(0)) if extra else (None, None)
    outs = [refs.pop(0) for _ in range(row_outs)]
    sums = [refs.pop(0) for _ in range(sum_outs)]
    carried_out = refs.pop(0) if carried else None
    extra_out = refs.pop(0) if extra else None
    spread_ref = refs.pop(0) if gather else None
    sum_refs, (send, recv, carry_send, carry_recv), extra_refs = refs[:7], refs[7:11], refs[11:]
    odd, core, across, beside, corner = peers()
    greet([core, across, beside])
    f32 = jnp.float32
    step = partial_ref.shape[2] // chunks

    def part(k):
        return pl.ds(k * step, step)

    def copy(slot, k, source, target, device):
        return pltpu.make_async_remote_copy(
            src_ref=source,
            dst_ref=target,
            send_sem=send.at[slot, k],
            recv_sem=recv.at[slot, k],
            device_id=device,
            device_id_type=MESH,
        )

    def across_out(k):
        return copy(0, k, spread_ref.at[0, 0, part(k)], spread_ref.at[0, 1, part(k)], across)

    def beside_out(k):
        return copy(1, k, spread_ref.at[0, 0, part(k)], spread_ref.at[0, 2, part(k)], beside)

    def corner_out(k):
        return copy(2, k, spread_ref.at[0, 1 + odd, part(k)], spread_ref.at[0, 3, part(k)], corner)

    def core_out(k):
        return copy(3, k, spread_ref.at[0, :, part(k)], spread_ref.at[1, :, part(k)], core)

    def finish_rows(k, rows, total):
        values, added, sent = finish(
            total, *[ref[rows].astype(f32) for ref in ins], *[ref[...] for ref in shared]
        )
        for ref, value in zip(outs, values):
            ref[rows] = value.astype(ref.dtype)
        for ref, value in zip(sums, added):
            ref[...] = value if k == 0 else ref[...] + value
        if gather:
            spread_ref[0, 0, rows] = sent
            across_out(k).start()
            beside_out(k).start()

    def pass_corner(k):
        across_out(k).wait_recv()
        beside_out(k).wait_recv()
        corner_out(k).start()

    def pass_core(k):
        corner_out(k).wait_recv()
        core_out(k).start()

    def arrive(k):
        core_out(k).wait_recv()

    if carried:
        carry = pltpu.make_async_remote_copy(
            src_ref=carried_ref,
            dst_ref=carried_out,
            send_sem=carry_send,
            recv_sem=carry_recv,
            device_id=across,
            device_id_type=MESH,
        )
        carry.start()
    stages, copies = sum_stages(partial_ref, finish_rows, sum_refs, chunks)
    if gather:
        stages = stages + [pass_corner, pass_core, arrive]
        copies = copies + [across_out, beside_out, corner_out, core_out]
    if extra:

        def extra_rows(k, rows, total):
            extra_out[rows] = (extra_middle[rows] + total).astype(extra_out.dtype)

        later, more = sum_stages(extra_ref, extra_rows, extra_refs, chunks)
        stages = stages[:1] + [lambda k, a=a, b=b: (a(k), b(k)) for a, b in zip(stages[1:5], later)] + stages[5:]
        copies = copies + more
    run_stages(stages, chunks)
    if carried:
        carry.wait()
    for k in range(chunks):
        for one in copies:
            one(k).wait_send()


def exchange(
    finish,
    partial,
    row_ins,
    shared_ins,
    row_outs,
    sum_outs,
    gather,
    number,
    carried=None,
    extra=None,
    chunks=4,
):
    _, units, rows, width = partial.shape
    if not kernels_fit():
        return exchange_plainly(finish, partial, row_ins, shared_ins, row_outs, gather, carried, extra)
    bf16 = jnp.bfloat16
    shapes = [jax.ShapeDtypeStruct((rows, width), dtype) for dtype in row_outs]
    shapes += [jax.ShapeDtypeStruct((1, width), jnp.float32)] * sum_outs
    shapes += [] if carried is None else [jax.ShapeDtypeStruct(carried.shape, carried.dtype)]
    shapes += [] if extra is None else [jax.ShapeDtypeStruct((rows, width), bf16)]
    shapes += [jax.ShapeDtypeStruct(partial.shape, bf16)] * gather
    more = ([] if carried is None else [carried]) + list(extra or ())
    place = pl.BlockSpec(memory_space=pltpu.VMEM)
    result = pl.pallas_call(
        functools.partial(
            exchange_kernel,
            finish,
            len(row_ins),
            len(shared_ins),
            len(row_outs),
            sum_outs,
            gather,
            carried is not None,
            extra is not None,
            chunks,
        ),
        out_shape=shapes,
        in_specs=[place] * (1 + len(row_ins) + len(shared_ins) + len(more)),
        out_specs=[place] * len(shapes),
        scratch_shapes=sum_scratch(units, rows, width, chunks)
        + [pltpu.SemaphoreType.DMA((4, chunks))] * 2
        + [pltpu.SemaphoreType.DMA] * 2
        + ([] if extra is None else sum_scratch(units, rows, width, chunks)),
        compiler_params=pltpu.CompilerParams(
            collective_id=number, has_side_effects=True, vmem_limit_bytes=VMEM_BYTES
        ),
        cost_estimate=lasting(66 if gather else 38),
        name=("exchange_%d" % number),
    )(partial, *row_ins, *shared_ins, *more)
    result = list(result)
    rows_done = [result.pop(0) for _ in row_outs]
    sums = [result.pop(0) for _ in range(sum_outs)]
    carried = None if carried is None else result.pop(0)
    extra = None if extra is None else result.pop(0)
    return rows_done, sums, (result.pop(0) if gather else None), carried, extra


def plane_total(partial):
    near = partial[0].reshape(-1, partial.shape[3]).astype(jnp.float32)
    near = near + flip(partial[1].reshape(-1, partial.shape[3]), 1).astype(jnp.float32)
    return collect(near, (lax.axis_index("seq") % 2) == 1)


def exchange_plainly(finish, partial, row_ins, shared_ins, row_outs, gather, carried, extra):
    total = plane_total(partial)
    rows, sums, sent = finish(total, *[value.astype(jnp.float32) for value in row_ins], *shared_ins)
    rows = [value.astype(dtype) for value, dtype in zip(rows, row_outs)]
    if carried is not None:
        carried = flip(carried, lax.axis_size("seq"))
    if extra is not None:
        extra = (plane_total(extra[0]) + extra[1]).astype(jnp.bfloat16)
    if gather:
        odd = (lax.axis_index("seq") % 2) == 1
        sent = jnp.stack(spread(sent, odd)).reshape(partial.shape)
    return rows, sums, sent, carried, extra


def finish_middle(total, stream, gain):
    middle = stream + total
    return [middle], [], (middle * rms_scale(middle) * gain).astype(jnp.bfloat16)


def finish_block(total, middle, gain):
    result = (middle + total).astype(jnp.bfloat16)
    stream = result.astype(jnp.float32)
    return [result], [], (stream * rms_scale(stream) * gain).astype(jnp.bfloat16)


def finish_gradient(total, upstream, stream, gain):
    scale = rms_scale(stream)
    weighted = gain * total
    grad = (
        upstream
        + scale * weighted
        - stream * scale**3 * jnp.mean(weighted * stream, -1, keepdims=True)
    )
    added = jnp.sum(total * stream * scale, 0, keepdims=True)
    return [grad], [added], grad.astype(jnp.bfloat16)


LAST_CHUNKS = 4


def last_kernel(
    partial_ref,
    upstream_ref,
    stream_ref,
    gain_ref,
    smalls_ref,
    result_ref,
    product_ref,
    mixer_ref,
    pair0_ref,
    pair1_ref,
    down0_ref,
    down1_ref,
    grad_ref,
    crossed_ref,
    smalls_out,
    pair_out,
    down_out,
    mixer_out,
    *scratch,
):
    sum_refs, scratch = scratch[:7], scratch[7:]
    pair_both, down_both, mixer_both, from_z, grad_low, gain_sum = scratch[:6]
    small_sum, small_sent, small_side, small_z = scratch[6:10]
    local, z_send, z_recv, own_send, own_recv, small_send, small_recv, cross_send, cross_recv = scratch[10:]
    x, q, z = lax.axis_index("section"), lax.axis_index("seq"), lax.axis_index("fsdp")
    shards = lax.axis_size("fsdp")
    _, core, across, beside, _ = peers()
    f32, bf16 = jnp.float32, jnp.bfloat16
    others = [{"fsdp": (z + step) % shards} for step in range(1, shards)]
    greet([core, across, beside] + others)
    share = x * 4 + q
    share_across = (1 - x) * 4 + q
    beside_q = (1 - q // 2) * 2 + q % 2
    share_beside = x * 4 + beside_q
    share_corner = (1 - x) * 4 + beside_q

    def remote(source, target, send, recv, device):
        return pltpu.make_async_remote_copy(
            src_ref=source,
            dst_ref=target,
            send_sem=send,
            recv_sem=recv,
            device_id=device,
            device_id_type=MESH,
        )

    early = remote(result_ref, crossed_ref.at[1], cross_send.at[1], cross_recv.at[1], across)
    early.start()
    z_moves = []
    for step, device in enumerate(others):
        one = remote(
            product_ref.at[(z + step + 1) % shards],
            from_z.at[step],
            z_send.at[step],
            z_recv.at[step],
            device,
        )
        one.start()
        z_moves.append(one)
    loads = [
        pltpu.make_async_copy(pair0_ref, pair_both.at[0], local.at[0]),
        pltpu.make_async_copy(pair1_ref, pair_both.at[1], local.at[1]),
        pltpu.make_async_copy(down0_ref, down_both.at[0], local.at[2]),
        pltpu.make_async_copy(down1_ref, down_both.at[1], local.at[3]),
        pltpu.make_async_copy(product_ref.at[z], from_z.at[shards - 1], local.at[4]),
        pltpu.make_async_copy(mixer_ref, mixer_both.at[1], local.at[5]),
    ]
    for one in loads:
        one.start()

    class Owners:
        def __init__(self, place, both, out):
            self.out = out

            def move(slot, source, target, device):
                return remote(source, out.at[target], own_send.at[place, slot], own_recv.at[place, slot], device)

            self.cross = move(0, both.at[1 - x], share, across)
            self.side = move(1, both.at[x], share, beside)
            self.near = move(2, both.at[x], share, core)
            self.side_across = move(3, out.at[share_across], share_across, beside)
            self.near_across = move(4, out.at[share_across], share_across, core)
            self.near_beside = move(5, out.at[share_beside], share_beside, core)
            self.near_corner = move(6, out.at[share_corner], share_corner, core)
            self.keep = pltpu.make_async_copy(both.at[x], out.at[share], local.at[6 + place])

        def first(self):
            for one in (self.cross, self.side, self.near, self.keep):
                one.start()

        def second(self):
            self.cross.wait_recv()
            self.side_across.start()
            self.near_across.start()

        def third(self):
            self.side.wait_recv()
            self.near_beside.start()

        def fourth(self):
            self.side_across.wait_recv()
            self.near_corner.start()

        def end(self):
            for one in (self.near, self.near_across, self.near_beside, self.near_corner):
                one.wait_recv()
            for one in (
                self.cross,
                self.side,
                self.near,
                self.side_across,
                self.near_across,
                self.near_beside,
                self.near_corner,
            ):
                one.wait_send()
            self.keep.wait()

    pair = Owners(0, pair_both, pair_out)
    down = Owners(1, down_both, down_out)
    mixer = Owners(2, mixer_both, mixer_out)
    loads[0].wait()
    loads[1].wait()
    pair.first()
    loads[2].wait()
    loads[3].wait()
    down.first()

    def finish_rows(k, rows, total):
        (grad,), (added,), sent = finish_gradient(
            total, upstream_ref[rows].astype(f32), stream_ref[rows].astype(f32), gain_ref[...]
        )
        grad_ref[rows] = grad
        grad_low[rows] = sent
        gain_sum[...] = added if k == 0 else gain_sum[...] + added

    stages, copies = sum_stages(partial_ref, finish_rows, sum_refs, LAST_CHUNKS)
    run_stages(stages, LAST_CHUNKS)
    pair.second()
    cross = remote(grad_low, crossed_ref.at[0], cross_send.at[0], cross_recv.at[0], across)
    cross.start()
    down.second()

    for one in z_moves:
        one.wait_recv()
    loads[4].wait()
    loads[5].wait()
    total = from_z[0].astype(f32)
    for step in range(1, shards):
        total = total + from_z[step].astype(f32)
    mixer_both[0] = total.astype(bf16)
    mixer.first()
    pair.third()
    down.third()

    small_rows = smalls_ref.shape[3]
    small_sum[...] = smalls_ref[...]
    for shard in range(shards):
        small_sum[0, shard, 0:1] += gain_sum[:, shard * small_rows : (shard + 1) * small_rows]
    for step, device in enumerate((core, across, beside)):
        small_sent[step] = small_sum[...]
        one = remote(small_sent.at[step], small_side.at[step], small_send.at[step], small_recv.at[step], device)
        one.start()
        one.wait()
        small_sum[...] += small_side[step]
    small_moves = []
    for step, device in enumerate(others):
        one = remote(
            small_sum.at[x, (z + step + 1) % shards],
            small_z.at[step],
            small_send.at[3 + step],
            small_recv.at[3 + step],
            device,
        )
        one.start()
        small_moves.append(one)
    small_total = small_sum[x, z]
    for step, one in enumerate(small_moves):
        one.wait()
        small_total = small_total + small_z[step]
    smalls_out[...] = small_total

    mixer.second()
    mixer.third()
    pair.fourth()
    down.fourth()
    mixer.fourth()
    for owners in (pair, down, mixer):
        owners.end()
    cross.wait()
    early.wait()
    for one in z_moves:
        one.wait_send()
    for k in range(LAST_CHUNKS):
        for one in copies:
            one(k).wait_send()


def last_exchange(partial, upstream, stream, gain, smalls, result, product, mixer, pairs, downs):
    _, units, rows, width = partial.shape
    shards, shard_rows, mixer_columns = product.shape
    bf16, f32 = jnp.bfloat16, jnp.float32
    count = 2 * units
    vmem = pl.BlockSpec(memory_space=pltpu.VMEM)
    anywhere = pl.BlockSpec(memory_space=pl.ANY)
    return pl.pallas_call(
        last_kernel,
        out_shape=[
            jax.ShapeDtypeStruct((rows, width), f32),
            jax.ShapeDtypeStruct((2, rows, width), bf16),
            jax.ShapeDtypeStruct(smalls.shape[2:], f32),
            jax.ShapeDtypeStruct((count, *pairs[0].shape), bf16),
            jax.ShapeDtypeStruct((count, *downs[0].shape), bf16),
            jax.ShapeDtypeStruct((count, shard_rows, mixer_columns), bf16),
        ],
        in_specs=[vmem] * 6 + [anywhere] * 6,
        out_specs=[vmem] * 3 + [anywhere] * 3,
        scratch_shapes=sum_scratch(units, rows, width, LAST_CHUNKS)
        + [
            pltpu.VMEM((2, *pairs[0].shape), bf16),
            pltpu.VMEM((2, *downs[0].shape), bf16),
            pltpu.VMEM((2, shard_rows, mixer_columns), bf16),
            pltpu.VMEM(product.shape, bf16),
            pltpu.VMEM((rows, width), bf16),
            pltpu.VMEM((1, width), f32),
            pltpu.VMEM(smalls.shape, f32),
            pltpu.VMEM((3, *smalls.shape), f32),
            pltpu.VMEM((3, *smalls.shape), f32),
            pltpu.VMEM((shards - 1, *smalls.shape[2:]), f32),
            pltpu.SemaphoreType.DMA((9,)),
            pltpu.SemaphoreType.DMA((shards - 1,)),
            pltpu.SemaphoreType.DMA((shards - 1,)),
            pltpu.SemaphoreType.DMA((3, 7)),
            pltpu.SemaphoreType.DMA((3, 7)),
            pltpu.SemaphoreType.DMA((2 + shards,)),
            pltpu.SemaphoreType.DMA((2 + shards,)),
            pltpu.SemaphoreType.DMA((2,)),
            pltpu.SemaphoreType.DMA((2,)),
        ],
        compiler_params=pltpu.CompilerParams(
            collective_id=20, has_side_effects=True, vmem_limit_bytes=VMEM_BYTES
        ),
        cost_estimate=lasting(130),
        name="last_exchange",
    )(partial, upstream, stream, gain, smalls, result, product, mixer, *pairs, *downs)


def place_kernel(blocks, width, stack_ref, *outs):
    shards = lax.axis_size("fsdp")
    count = stack_ref.shape[0]
    part = width // shards // count
    for block in range(blocks):
        pieces = []
        for shard in range(shards):
            start = (block * shards + shard) * part
            pieces += [stack_ref[share, :, start : start + part] for share in range(count)]
        value = jnp.concatenate(pieces, 1).astype(jnp.float32)
        if len(outs) == 1:
            outs[0][:, block * width : (block + 1) * width] = value
        else:
            outs[block][...] = value


def place_columns(stack, blocks, width, together):
    count, rows, columns = stack.shape
    step = 48
    widths = [blocks * width] if together else [width] * blocks
    return pl.pallas_call(
        functools.partial(place_kernel, blocks, width),
        grid=(rows // step,),
        out_shape=[jax.ShapeDtypeStruct((rows, each), jnp.float32) for each in widths],
        in_specs=[pl.BlockSpec((count, step, columns), lambda i: (0, i, 0))],
        out_specs=[pl.BlockSpec((step, each), lambda i: (i, 0)) for each in widths],
        compiler_params=pltpu.CompilerParams(vmem_limit_bytes=VMEM_BYTES),
        cost_estimate=lasting(14),
        name="place_columns",
    )(stack)


def flip(value, bits):
    count = lax.axis_size("section") * lax.axis_size("seq")
    return lax.ppermute(value, PLANE, [(source, source ^ bits) for source in range(count)])


def flip_by_core(value, even_bits, odd_bits):
    count = lax.axis_size("section") * lax.axis_size("seq")
    pairs = [(source, source ^ (odd_bits if source & 1 else even_bits)) for source in range(count)]
    return lax.ppermute(value, PLANE, pairs)


def chip_bits():
    bits = [lax.axis_size("seq")]
    step = lax.axis_size("seq") // 2
    while step > 1:
        bits.append(step)
        step //= 2
    return bits


def half_units():
    units = [0]
    for bits in chip_bits():
        units = units + [unit | bits for unit in units]
    return units


def spread_chips(own, odd):
    bits = chip_bits()
    if len(bits) == 2:
        first = flip(own, bits[0])
        second = flip(own, bits[1])
        third = flip_by_core(jnp.where(odd, second, first), bits[1], bits[0])
        return jnp.concatenate([own, first, second, third], 0)
    held = own
    for step in bits:
        held = jnp.concatenate([held, flip(held, step)], 0)
    return held


def spread(own, odd):
    near = spread_chips(own, odd)
    return near, flip(near, 1)


def collect(near, odd):
    bits = chip_bits()
    if len(bits) == 2:
        rows = near.shape[0] // 4
        held = near
        third = flip_by_core(held[3 * rows :].astype(jnp.bfloat16), bits[1], bits[0]).astype(jnp.float32)
        first = held[rows : 2 * rows] + jnp.where(odd, 0.0, third)
        second = held[2 * rows : 3 * rows] + jnp.where(odd, third, 0.0)
        first = flip(first.astype(jnp.bfloat16), bits[0]).astype(jnp.float32)
        second = flip(second.astype(jnp.bfloat16), bits[1]).astype(jnp.float32)
        return held[:rows] + first + second
    held = near
    for step in reversed(bits):
        rows = held.shape[0] // 2
        held = held[:rows] + flip(held[rows:].astype(jnp.bfloat16), step).astype(jnp.float32)
    return held


def rms_scale(stream):
    return lax.rsqrt(jnp.mean(stream * stream, -1, keepdims=True) + EPSILON)


def times(left, matrix):
    return jnp.dot(left, matrix, preferred_element_type=jnp.float32)


def times_transposed(left, matrix):
    return lax.dot_general(
        left, matrix, (((1,), (1,)), ((), ())), preferred_element_type=jnp.float32
    )


def by_rows(value):
    return with_layout_constraint(value, Layout(major_to_minor=tuple(range(value.ndim))))


def row_products(left, right):
    return lax.dot_general(
        left, right, (((0,), (0,)), ((), ())), preferred_element_type=jnp.float32
    ).astype(jnp.bfloat16)


def normed_with(stream, gain):
    return (stream * rms_scale(stream) * gain).astype(jnp.bfloat16)


def pick_columns(matrix, share, width, count):
    shards = lax.axis_size("fsdp")
    part = width // shards // count
    return jnp.concatenate(
        [
            lax.dynamic_slice(
                matrix, (0, start + shard * (width // shards) + share * part), (matrix.shape[0], part)
            )
            for start in range(0, matrix.shape[1], width)
            for shard in range(shards)
        ],
        1,
    )


def pick_rows(matrix, share, count):
    part = matrix.shape[0] // count
    return lax.dynamic_slice(matrix, (share * part, 0), (part, matrix.shape[1]))


def spread_tokens(tokens_ref, out_ref, send, recv, local, chunks):
    x = lax.axis_index("section")
    _, core, _, beside, _ = peers()
    step_rows = tokens_ref.shape[1] // chunks

    def move(source, target, number, device):
        return pltpu.make_async_remote_copy(
            src_ref=source,
            dst_ref=target,
            send_sem=send.at[number],
            recv_sem=recv.at[number],
            device_id=device,
            device_id_type=MESH,
        )

    sides = []
    for k in range(chunks):
        part = pl.ds(k * step_rows, step_rows)
        first = move(tokens_ref.at[x, part], out_ref.at[0, 2, part], 2 * k, beside)
        second = move(tokens_ref.at[1 - x, part], out_ref.at[0, 3, part], 2 * k + 1, beside)
        first.start()
        second.start()
        sides.append((first, second))
    keep = [
        pltpu.make_async_copy(tokens_ref.at[x], out_ref.at[0, 0], local.at[0]),
        pltpu.make_async_copy(tokens_ref.at[1 - x], out_ref.at[0, 1], local.at[1]),
    ]
    for one in keep:
        one.start()
    for one in keep:
        one.wait()
    near = move(out_ref.at[0, 0:2], out_ref.at[1, 0:2], 2 * chunks, core)
    near.start()

    def end():
        overs = []
        for k, (first, second) in enumerate(sides):
            part = pl.ds(k * step_rows, step_rows)
            first.wait_recv()
            second.wait_recv()
            over = move(out_ref.at[0, 2:4, part], out_ref.at[1, 2:4, part], 2 * chunks + 1 + k, core)
            over.start()
            overs.append(over)
        near.wait()
        for one in overs:
            one.wait()
        for first, second in sides:
            first.wait_send()
            second.wait_send()

    return end


SPREAD_CHUNKS = 4
FFN_CHUNKS = 4
SPREAD_MOVES = 3 * SPREAD_CHUNKS + 1


def spread_kernel(tokens_ref, out_ref, local, send, recv):
    _, core, _, beside, _ = peers()
    greet([core, beside])
    spread_tokens(tokens_ref, out_ref, send, recv, local, SPREAD_CHUNKS)()


def spread_slots(tokens, number):
    x = lax.axis_index("section")
    slots, rows, width = tokens.shape
    if not kernels_fit():
        near = jnp.concatenate(
            [
                lax.dynamic_index_in_dim(tokens, x, 0, False),
                lax.dynamic_index_in_dim(tokens, 1 - x, 0, False),
            ],
            0,
        )
        for step in chip_bits()[1:]:
            near = jnp.concatenate([near, flip(near, step)], 0)
        return jnp.stack([near, flip(near, 1)]).reshape(2, -1, rows, width)
    place = pl.BlockSpec(memory_space=pltpu.VMEM)
    return pl.pallas_call(
        spread_kernel,
        out_shape=jax.ShapeDtypeStruct((2, 4, rows, width), tokens.dtype),
        in_specs=[place],
        out_specs=place,
        scratch_shapes=[
            pltpu.SemaphoreType.DMA((2,)),
            pltpu.SemaphoreType.DMA((SPREAD_MOVES,)),
            pltpu.SemaphoreType.DMA((SPREAD_MOVES,)),
        ],
        compiler_params=pltpu.CompilerParams(
            collective_id=number, has_side_effects=True, vmem_limit_bytes=VMEM_BYTES
        ),
        cost_estimate=lasting(42),
        name="spread_slots",
    )(tokens)


def start_kernel(
    small_ref, tokens_ref, sent_ref, small_out, tokens_out, ffn_out, local, small_send, small_recv, send, recv
):
    x, z = lax.axis_index("section"), lax.axis_index("fsdp")
    shards = lax.axis_size("fsdp")
    _, core, across, beside, _ = peers()
    others = [
        {"section": (x + step // shards) % 2, "fsdp": (z + step) % shards} for step in range(1, 2 * shards)
    ]
    greet([core, beside] + others)
    ffn_rows = sent_ref.shape[0] // FFN_CHUNKS
    crossing = []
    for k in range(FFN_CHUNKS):
        part = pl.ds(k * ffn_rows, ffn_rows)
        one = pltpu.make_async_remote_copy(
            src_ref=sent_ref.at[part],
            dst_ref=ffn_out.at[part],
            send_sem=send.at[SPREAD_MOVES + k],
            recv_sem=recv.at[SPREAD_MOVES + k],
            device_id=across,
            device_id_type=MESH,
        )
        one.start()
        crossing.append(one)
    smalls = []
    for step, device in enumerate(others):
        one = pltpu.make_async_remote_copy(
            src_ref=small_ref,
            dst_ref=small_out.at[x, z],
            send_sem=small_send.at[step],
            recv_sem=small_recv.at[step],
            device_id=device,
            device_id_type=MESH,
        )
        one.start()
        smalls.append(one)
    end = spread_tokens(tokens_ref, tokens_out, send, recv, local, SPREAD_CHUNKS)
    keep = pltpu.make_async_copy(small_ref, small_out.at[x, z], local.at[2])
    keep.start()
    end()
    for one in [keep] + smalls + crossing:
        one.wait()


def start(small, tokens, sent):
    shards = lax.axis_size("fsdp")
    if not kernels_fit():
        every = lax.all_gather(small, ("section", "fsdp"), axis=0).reshape(2, shards, *small.shape)
        return every, spread_slots(tokens, 0), flip(sent, lax.axis_size("seq"))
    _, rows, width = tokens.shape
    place = pl.BlockSpec(memory_space=pltpu.VMEM)
    anywhere = pl.BlockSpec(memory_space=pl.ANY)
    return pl.pallas_call(
        start_kernel,
        out_shape=[
            jax.ShapeDtypeStruct((2, shards, *small.shape), small.dtype),
            jax.ShapeDtypeStruct((2, 4, rows, width), tokens.dtype),
            jax.ShapeDtypeStruct(sent.shape, sent.dtype),
        ],
        in_specs=[place, place, anywhere],
        out_specs=[place, place, anywhere],
        scratch_shapes=[
            pltpu.SemaphoreType.DMA((3,)),
            pltpu.SemaphoreType.DMA((2 * shards - 1,)),
            pltpu.SemaphoreType.DMA((2 * shards - 1,)),
            pltpu.SemaphoreType.DMA((SPREAD_MOVES + FFN_CHUNKS,)),
            pltpu.SemaphoreType.DMA((SPREAD_MOVES + FFN_CHUNKS,)),
        ],
        compiler_params=pltpu.CompilerParams(
            collective_id=21, has_side_effects=True, vmem_limit_bytes=VMEM_BYTES
        ),
        cost_estimate=lasting(59),
        name="start",
    )(small, tokens, sent)


def body(
    tokens,
    in_weight,
    conv_kernel,
    out_weight,
    gate_weight,
    up_weight,
    down_weight,
    mixer_gain,
    ffn_gain,
    cotangent,
):
    bf16, f32 = jnp.bfloat16, jnp.float32
    x_index = lax.axis_index("section")
    q_index = lax.axis_index("seq")
    seq_count = lax.axis_size("seq")
    count = lax.axis_size("section") * seq_count
    shards = lax.axis_size("fsdp")
    share = x_index * seq_count + q_index
    first_plane = x_index == 0
    width = tokens.shape[3]
    rows = tokens.shape[2]
    hidden_width = gate_weight.shape[2]
    shard_rows = width // shards
    in_columns = 3 * width // count
    channels = width // count
    ffn_columns = hidden_width // count
    units = half_units()
    half = len(units)
    part = shard_rows // count

    other = share ^ seq_count

    def mixer_share(index):
        columns = pick_columns(in_weight[0], index, width, count)
        return jnp.concatenate(
            [columns, pick_rows(out_weight[0], index, count).reshape(shard_rows, -1)], 1
        )

    def ffn_share(index):
        return jnp.concatenate(
            [
                pick_columns(gate_weight[0], index, hidden_width, count),
                pick_columns(up_weight[0], index, hidden_width, count),
                pick_rows(down_weight[0], index, count).reshape(shard_rows, -1),
            ],
            1,
        )

    mixer_kept = mixer_share(share)
    mixer_sent = flip(mixer_share(other), seq_count)
    ffn_kept, ffn_sent = ffn_share(share), ffn_share(other)
    mixer_sent, ffn_kept, ffn_sent = tie(mixer_sent, ffn_kept, ffn_sent)
    mixer_parts = [
        jnp.where(first_plane, mixer_kept, mixer_sent),
        jnp.where(first_plane, mixer_sent, mixer_kept),
    ]
    small = jnp.concatenate(
        [
            mixer_gain.astype(f32),
            ffn_gain.astype(f32),
            conv_kernel[0].T.astype(f32),
            jnp.zeros((3, shard_rows), f32),
        ],
        0,
    )
    small, mixer_parts = tie(small, mixer_parts)
    small, entry, ffn_sent = start(small, tokens[:, 0], ffn_sent)
    ffn_parts = [
        jnp.where(first_plane, ffn_kept, ffn_sent),
        jnp.where(first_plane, ffn_sent, ffn_kept),
    ]
    small = small.transpose(0, 2, 1, 3)
    whole = small.reshape(2, 8, width)
    taps_all = lax.dynamic_slice(
        small[:, 2:5].reshape(2, 3, shards, count, part), (0, 0, 0, share, 0), (2, 3, shards, 1, part)
    ).reshape(2, 3, shards * part)

    def over_fsdp(value):
        return lax.all_gather(value, "fsdp", axis=0, tiled=True)

    pair_columns = 2 * ffn_columns

    def mixer_weights(value):
        mixer = over_fsdp(value)
        return mixer[:, :in_columns], mixer[:, in_columns:].reshape(-1, width)

    mixer_matrices = [mixer_weights(mixer_parts[0]), None]

    def ffn_weights(value):
        return value[:, :pair_columns], value[:, pair_columns:].reshape(-1, width)

    in_matrix, out_matrix, value = tie(*mixer_matrices[0], ffn_parts[0])
    mixer_matrices[0] = (in_matrix, out_matrix)
    ffn = over_fsdp(value)
    ffn_matrices = [None, None]

    ids = jnp.stack([share ^ unit ^ side for side in (0, 1) for unit in units])
    has_before = (ids % seq_count) > 0
    has_after = (ids % seq_count) < seq_count - 1
    before_pick = (ids[None, :] == (ids - 1)[:, None]) & has_before[:, None]
    after_pick = (ids[None, :] == (ids + 1)[:, None]) & has_after[:, None]

    def pick_units(mask, edge):
        return jnp.sum(jnp.where(mask[:, :, None, None], edge[None].astype(f32), 0.0), 1)

    def flat(value):
        return value.reshape(2 * half * rows, value.shape[-1])

    def in_units(value):
        return value.reshape(2, half, rows, value.shape[-1])

    def gain_row(block, kind):
        return whole[block, kind : kind + 1]

    stream = lax.dynamic_index_in_dim(tokens[:, 0], x_index, 0, False)
    normed = normed_with(entry.astype(f32), whole[0, 0])
    saved = []
    outputs = []
    for block in range(2):
        in_matrix, out_matrix = mixer_matrices[block]
        taps = taps_all[block]
        projected = times(flat(normed), in_matrix)
        b_gate = projected[:, :channels]
        c_gate = projected[:, channels : 2 * channels]
        x_value = projected[:, 2 * channels :]
        conv_input = (b_gate * x_value).astype(bf16).reshape(2 * half, rows, channels)
        earlier = pick_units(before_pick, conv_input[:, -2:])
        extended = jnp.concatenate([earlier, conv_input.astype(f32)], 1)
        conv_out = (
            taps[0] * extended[:, :-2] + taps[1] * extended[:, 1:-1] + taps[2] * extended[:, 2:]
        )
        gated = flat((c_gate.reshape(conv_out.shape) * conv_out).astype(bf16))
        partial = in_units(times(gated, out_matrix).astype(bf16))
        (middle,), _, normed_ffn, crossed_out, _ = exchange(
            finish_middle,
            partial,
            [stream],
            [gain_row(block, 1)],
            [f32],
            0,
            True,
            1 + 2 * block,
            carried=outputs[0] if block else None,
        )
        if block == 0:
            tokens_back, normed_ffn = tie(cotangent[:, 0], normed_ffn)
            grad_units, normed_ffn = tie(spread_slots(tokens_back, 22), normed_ffn)
            ffn, normed_ffn, value = tie(ffn, normed_ffn, mixer_parts[1])
            ffn_matrices[0] = ffn_weights(ffn)
            mixer = over_fsdp(value)
        pair_matrix, down_matrix = ffn_matrices[block]
        pairs = times(flat(normed_ffn), pair_matrix)
        hidden = (jax.nn.silu(pairs[:, :ffn_columns]) * pairs[:, ffn_columns:]).astype(bf16)
        partial = in_units(times(hidden, down_matrix).astype(bf16))
        if block == 0:
            partial, mixer, value = tie(partial, mixer, ffn_parts[1])
            mixer_matrices[1] = (mixer[:, :in_columns], mixer[:, in_columns:].reshape(-1, width))
            ffn_matrices[1] = ffn_weights(over_fsdp(value))
        saved.append((stream, normed, projected, extended, conv_out, gated, middle, normed_ffn, pairs, hidden))
        if block == 0:
            (stream,), _, normed, _, _ = exchange(
                finish_block, partial, [middle], [gain_row(1, 0)], [bf16], 0, True, 2
            )
            outputs.append(stream)
        else:
            last_sum = (partial, middle)

    upstream = lax.dynamic_index_in_dim(cotangent[:, 0], x_index, 0, False)
    stream_grads = [None, None]
    small_grads = [None, None]
    matrix_grads = [None, None]

    def over_z(value):
        return lax.psum_scatter(value, "fsdp", scatter_dimension=0, tiled=True)

    def product(left, right):
        return by_rows(row_products(left, right))

    def small_rows(mixer_gain_part, ffn_gain_part, taps_placed):
        return jnp.concatenate(
            [
                mixer_gain_part.reshape(1, width),
                ffn_gain_part.reshape(1, width),
                taps_placed,
                jnp.zeros((3, width), f32),
            ],
            0,
        )

    def small_values():
        return jnp.stack(small_grads).reshape(2, 8, shards, shard_rows).transpose(0, 2, 1, 3)

    def to_section(value, block):
        over = [((1 - block) * seq_count + seq, block * seq_count + seq) for seq in range(seq_count)]
        return lax.ppermute(value, PLANE, over)

    inside = chip_bits()[1:] + [1]
    relative = [0, seq_count]
    for bits in inside:
        relative = relative + [unit | bits for unit in relative]

    def to_owners(value, block):
        held = [value, to_section(value, block)]
        for bits in inside:
            over = [
                (block * seq_count + seq, block * seq_count + (seq ^ bits)) for seq in range(seq_count)
            ]
            held = held + [lax.ppermute(unit, PLANE, over) for unit in held]
        return held

    mixer_sum = jnp.zeros((), f32)
    for block in (1, 0):
        in_matrix, out_matrix = mixer_matrices[block]
        pair_matrix, down_matrix = ffn_matrices[block]
        taps = taps_all[block]
        (stream, normed, projected, extended, conv_out, gated, middle, normed_ffn, pairs, hidden) = saved[block]
        down_product, grad_units, mixer_sum = tie(
            product(hidden, flat(grad_units)), grad_units, mixer_sum
        )
        if block == 0:
            matrix_grads[1] = (down_grad, pair_grad, mixer_sum)
        down_grad = over_z(down_product)
        gate_value, up_value = pairs[:, :ffn_columns], pairs[:, ffn_columns:]
        grad_hidden = times_transposed(flat(grad_units), down_matrix)
        sigmoid_gate = jax.nn.sigmoid(gate_value)
        grad_gate = (
            grad_hidden * up_value * sigmoid_gate * (1.0 + gate_value * (1.0 - sigmoid_gate))
        ).astype(bf16)
        grad_up = (grad_hidden * gate_value * sigmoid_gate).astype(bf16)
        grad_pairs = jnp.concatenate([grad_gate, grad_up], 1)
        partial = in_units(times_transposed(grad_pairs, pair_matrix).astype(bf16))
        partial, pair_product, down_grad = tie(
            partial, product(flat(normed_ffn), grad_pairs), down_grad
        )
        pair_grad = over_z(pair_product)
        (grad_middle,), (ffn_gain_part,), mixer_grad, crossed_grad, result = exchange(
            finish_gradient,
            partial,
            [upstream, middle],
            [gain_row(block, 1)],
            [f32],
            1,
            True,
            8 - 2 * block,
            carried=None if block else upstream,
            extra=last_sum if block else None,
        )
        if block == 1:
            outputs.append(result)
        grad_gated = times_transposed(flat(mixer_grad), out_matrix).reshape(2 * half, rows, channels)
        b_gate = projected[:, :channels].reshape(2 * half, rows, channels)
        c_gate = projected[:, channels : 2 * channels].reshape(2 * half, rows, channels)
        x_value = projected[:, 2 * channels :].reshape(2 * half, rows, channels)
        grad_cgate = grad_gated * conv_out
        grad_conv = grad_gated * c_gate
        later = pick_units(after_pick, grad_conv[:, :2])
        grad_extended = jnp.concatenate([grad_conv, later], 1)
        grad_input = (
            taps[0] * grad_extended[:, 2:]
            + taps[1] * grad_extended[:, 1:-1]
            + taps[2] * grad_extended[:, :-2]
        )
        taps_part = jnp.stack(
            [jnp.sum(grad_conv * extended[:, tap : tap + rows], (0, 1)) for tap in range(3)], 0
        )
        grad_projected = flat(
            jnp.concatenate([grad_input * x_value, grad_cgate, grad_input * b_gate], 2).astype(bf16)
        )
        partial = in_units(times_transposed(grad_projected, in_matrix).astype(bf16))
        in_grad = row_products(flat(normed), grad_projected)
        out_grad = row_products(gated, flat(mixer_grad))
        partial, mixer_product, pair_grad = tie(
            partial, by_rows(jnp.concatenate([in_grad, out_grad.reshape(width, -1)], 1)), pair_grad
        )
        if block == 1 or not kernels_fit():
            mixer_sum = over_z(mixer_product)
        own_mask = (jnp.arange(count) == share)[None, None, :, None]
        taps_placed = jnp.where(own_mask, taps_part.reshape(3, shards, 1, part), 0.0).reshape(3, width)
        if block == 0 and kernels_fit():
            break
        (grad_stream,), (mixer_gain_part,), sent, _, _ = exchange(
            finish_gradient,
            partial,
            [grad_middle, stream],
            [gain_row(block, 0)],
            [f32],
            1,
            block == 1,
            9 - 2 * block,
        )
        stream_grads[block] = grad_stream
        small_grads[block] = small_rows(mixer_gain_part, ffn_gain_part, taps_placed)
        if block == 0:
            matrix_grads[0] = (down_grad, pair_grad, mixer_sum)
        if block == 1:
            upstream = sent[0, 0]
            grad_units = sent

    def in_order(index):
        second = to_owners(matrix_grads[1][index], 1)
        first = to_owners(matrix_grads[0][index], 0)
        ordered = jnp.zeros((count, *first[0].shape), bf16)
        for unit, one, two in zip(relative, first, second):
            ordered = lax.dynamic_update_index_in_dim(
                ordered, jnp.where(first_plane, one, two), share ^ unit, 0
            )
        return ordered

    def columns_of(value, blocks):
        piece = value.reshape(count, shard_rows, blocks, shards, -1)
        return piece.transpose(1, 2, 3, 0, 4).reshape(shard_rows, -1).astype(f32)

    if kernels_fit():
        small_grads[0] = small_rows(jnp.zeros((1, width), f32), ffn_gain_part, taps_placed)
        later = matrix_grads[1]
        stream_grads[0], crossed_last, smalls, pair_grad, down_grad, mixer_sum = last_exchange(
            partial,
            grad_middle,
            stream,
            gain_row(0, 0),
            small_values(),
            outputs[1],
            mixer_product.reshape(shards, shard_rows, -1),
            later[2],
            (pair_grad, later[1]),
            (down_grad, later[0]),
        )
        gate_grad, up_grad = place_columns(pair_grad, 2, hidden_width, False)
        (in_grad,) = place_columns(mixer_sum, 3, width, True)
    else:
        crossed_last = flip(jnp.stack([stream_grads[0].astype(bf16), outputs[1]]), seq_count)
        smalls = lax.psum(small_values(), ("section", "seq", "fsdp"))
        smalls = lax.dynamic_slice(
            smalls, (x_index, lax.axis_index("fsdp"), 0, 0), (1, 1, *smalls.shape[2:])
        )[0, 0]
        down_grad, pair_grad, mixer_sum = in_order(0), in_order(1), in_order(2)
        gate_grad = columns_of(pair_grad[..., :ffn_columns], 1)
        up_grad = columns_of(pair_grad[..., ffn_columns:], 1)
        in_grad = columns_of(mixer_sum[..., :in_columns], 3)
    down_grad = down_grad.reshape(-1, width).astype(f32)
    out_grad = mixer_sum[..., in_columns:].reshape(shard_rows, width).astype(f32)

    def by_slot(values, crossed, dtype):
        kept = jnp.where(first_plane, values[0], values[1]).astype(dtype)
        other = jnp.where(first_plane, crossed[0], crossed[1]).astype(dtype)
        return jnp.stack(
            [jnp.where(first_plane, kept, other), jnp.where(first_plane, other, kept)], 0
        )

    return (
        by_slot(outputs, (crossed_out, crossed_last[1]), bf16)[None, :, None],
        by_slot(stream_grads, (crossed_last[0], crossed_grad), f32)[None, :, None],
        in_grad[None],
        smalls[2:5].T[None],
        out_grad[None],
        gate_grad[None],
        up_grad[None],
        down_grad[None],
        smalls[0][None],
        smalls[1][None],
    )


def solution(mesh):
    placed = (
        P(None, "fsdp", "seq", None),
        P("section", "fsdp", None),
        P("section", "fsdp", None),
        P("section", "fsdp", None),
        P("section", "fsdp", None),
        P("section", "fsdp", None),
        P("section", "fsdp", None),
        P("section", "fsdp"),
        P("section", "fsdp"),
        P(None, "fsdp", "seq", None),
    )
    return jax.shard_map(
        body,
        mesh=mesh,
        in_specs=placed,
        out_specs=(
            P("section", None, "fsdp", "seq", None),
            P("section", None, "fsdp", "seq", None),
            P("section", "fsdp", None),
            P("section", "fsdp", None),
            P("section", "fsdp", None),
            P("section", "fsdp", None),
            P("section", "fsdp", None),
            P("section", "fsdp", None),
            P("section", "fsdp"),
            P("section", "fsdp"),
        ),
        check_vma=False,
    )
```

```python
import functools

import jax
import jax.numpy as jnp
from jax import lax
from jax.experimental import pallas as pl
from jax.experimental.layout import Layout, with_layout_constraint
from jax.experimental.pallas import tpu as pltpu
from jax.sharding import PartitionSpec as P

EPSILON = 1e-05
PLANE = ("section", "seq")
MESH = pl.DeviceIdType.MESH
VMEM_BYTES = 56 * 2**20
BYTES_PER_US = 3.5e6


def lasting(us):
    return pl.CostEstimate(flops=0, bytes_accessed=int(us * BYTES_PER_US), transcendentals=0)


def tie(*values):
    return lax.optimization_barrier(values)


def kernels_fit():
    return lax.axis_size("section") == 2 and lax.axis_size("seq") == 4


def peers():
    x, q = lax.axis_index("section"), lax.axis_index("seq")
    odd = q % 2
    y = (1 - q // 2) * 2 + odd
    core = {"section": x, "seq": (q // 2) * 2 + (1 - odd)}
    across = {"section": 1 - x, "seq": q}
    beside = {"section": x, "seq": y}
    corner = {"section": x + odd * (1 - 2 * x), "seq": y * (1 - odd) + q * odd}
    return odd, core, across, beside, corner


def greet(others):
    barrier = pltpu.get_barrier_semaphore()
    for other in others:
        pl.semaphore_signal(barrier, inc=1, device_id=other, device_id_type=MESH)
    pl.semaphore_wait(barrier, len(others))


def remote_copy(source, target, send, recv, device):
    return pltpu.make_async_remote_copy(
        src_ref=source,
        dst_ref=target,
        send_sem=send,
        recv_sem=recv,
        device_id=device,
        device_id_type=MESH,
    )


def other_shards():
    z, shards = lax.axis_index("fsdp"), lax.axis_size("fsdp")
    return [{"fsdp": (z + step) % shards} for step in range(1, shards)]


class ShardSum:
    def __init__(self, product_ref, from_z, send, recv, local):
        z, shards = lax.axis_index("fsdp"), lax.axis_size("fsdp")
        self.from_z = from_z
        self.moves = [
            remote_copy(
                product_ref.at[(z + step) % shards],
                from_z.at[step - 1],
                send.at[step - 1],
                recv.at[step - 1],
                {"fsdp": (z + step) % shards},
            )
            for step in range(1, shards)
        ]
        self.keep = pltpu.make_async_copy(product_ref.at[z], from_z.at[shards - 1], local)

    def start(self):
        for one in self.moves + [self.keep]:
            one.start()

    def total(self):
        for one in self.moves:
            one.wait_recv()
        self.keep.wait()
        value = self.from_z[0].astype(jnp.float32)
        for step in range(1, self.from_z.shape[0]):
            value = value + self.from_z[step].astype(jnp.float32)
        return value.astype(self.from_z.dtype)

    def end(self):
        for one in self.moves:
            one.wait_send()


def shard_sum_scratch(product):
    shards = product.shape[0]
    return [
        pltpu.VMEM(product.shape, product.dtype),
        pltpu.SemaphoreType.DMA((shards - 1,)),
        pltpu.SemaphoreType.DMA((shards - 1,)),
        pltpu.SemaphoreType.DMA,
    ]


def sum_stages(left_ref, matrix_ref, turned, finish_rows, scratch, chunks):
    partial_ref, from_core, to_corner, from_corner, to_side, from_side, send, recv = scratch
    odd, core, across, beside, corner = peers()
    f32 = jnp.float32
    units, step = left_ref.shape[1], left_ref.shape[2] // chunks

    def multiply(half, k):
        left = left_ref[half, :, part(k)].reshape(units * step, left_ref.shape[3])
        right = matrix_ref[:, : left.shape[1]] if turned else matrix_ref[...]
        value = lax.dot_general(
            left, right, (((1,), (1 if turned else 0,)), ((), ())), preferred_element_type=f32
        )
        partial_ref[half, :, part(k)] = value.astype(jnp.bfloat16).reshape(units, step, value.shape[1])

    def part(k):
        return pl.ds(k * step, step)

    def copy(slot, k, source, target, device):
        return pltpu.make_async_remote_copy(
            src_ref=source,
            dst_ref=target,
            send_sem=send.at[slot, k],
            recv_sem=recv.at[slot, k],
            device_id=device,
            device_id_type=MESH,
        )

    def core_sum(k):
        return copy(0, k, partial_ref.at[1, :, part(k)], from_core.at[:, part(k)], core)

    def corner_sum(k):
        return copy(1, k, to_corner.at[part(k)], from_corner.at[part(k)], corner)

    def across_sum(k):
        return copy(2, k, to_side.at[0, part(k)], from_side.at[0, part(k)], across)

    def beside_sum(k):
        return copy(3, k, to_side.at[1, part(k)], from_side.at[1, part(k)], beside)

    def pair_sum(unit, k):
        return partial_ref[0, unit, part(k)].astype(f32) + from_core[unit, part(k)].astype(f32)

    def send_core(k):
        multiply(1, k)
        core_sum(k).start()

    def sum_corner(k):
        multiply(0, k)
        core_sum(k).wait_recv()
        to_corner[part(k)] = pair_sum(3, k).astype(jnp.bfloat16)
        corner_sum(k).start()

    def sum_sides(k):
        corner_sum(k).wait_recv()
        extra = from_corner[part(k)].astype(f32)
        to_side[0, part(k)] = (pair_sum(1, k) + jnp.where(odd == 0, extra, 0.0)).astype(jnp.bfloat16)
        to_side[1, part(k)] = (pair_sum(2, k) + jnp.where(odd == 0, 0.0, extra)).astype(jnp.bfloat16)
        across_sum(k).start()
        beside_sum(k).start()

    def total_rows(k):
        across_sum(k).wait_recv()
        beside_sum(k).wait_recv()
        finish_rows(
            k,
            part(k),
            pair_sum(0, k) + from_side[0, part(k)].astype(f32) + from_side[1, part(k)].astype(f32),
        )

    stages = [send_core, sum_corner, sum_sides, total_rows]
    return stages, [core_sum, corner_sum, across_sum, beside_sum]


STAGE_LAG = 2


def ticks_of(stages, chunks):
    return chunks + STAGE_LAG * (len(stages) - 1)


def run_tick(stages, chunks, tick):
    for place, stage in enumerate(stages):
        if 0 <= tick - STAGE_LAG * place < chunks:
            stage(tick - STAGE_LAG * place)


def run_stages(stages, chunks):
    for tick in range(ticks_of(stages, chunks)):
        run_tick(stages, chunks, tick)


def sum_scratch(units, rows, width, chunks):
    bf16 = jnp.bfloat16
    return [
        pltpu.VMEM((2, units, rows, width), bf16),
        pltpu.VMEM((units, rows, width), bf16),
        pltpu.VMEM((rows, width), bf16),
        pltpu.VMEM((rows, width), bf16),
        pltpu.VMEM((2, rows, width), bf16),
        pltpu.VMEM((2, rows, width), bf16),
        pltpu.SemaphoreType.DMA((4, chunks)),
        pltpu.SemaphoreType.DMA((4, chunks)),
    ]


def exchange_kernel(
    finish, turned, row_ins, shared_ins, row_outs, sum_outs, gather, product, extra, chunks, *refs
):
    refs = list(refs)
    left_ref, matrix_ref = refs.pop(0), refs.pop(0)
    ins = [refs.pop(0) for _ in range(row_ins)]
    shared = [refs.pop(0) for _ in range(shared_ins)]
    product_ref = refs.pop(0) if product else None
    extra_left, extra_matrix, extra_middle = [refs.pop(0) for _ in range(3)] if extra else [None] * 3
    outs = [refs.pop(0) for _ in range(row_outs)]
    sums = [refs.pop(0) for _ in range(sum_outs)]
    product_out = refs.pop(0) if product else None
    extra_out = refs.pop(0) if extra else None
    spread_ref = refs.pop(0) if gather else None
    sum_refs, (send, recv), refs = refs[:8], refs[8:10], refs[10:]
    product_refs, extra_refs = (refs[:4], refs[4:]) if product else ([], refs)
    odd, core, across, beside, corner = peers()
    greet([core, across, beside] + (other_shards() if product else []))
    f32 = jnp.float32
    step = left_ref.shape[2] // chunks

    def part(k):
        return pl.ds(k * step, step)

    def copy(slot, k, source, target, device):
        return pltpu.make_async_remote_copy(
            src_ref=source,
            dst_ref=target,
            send_sem=send.at[slot, k],
            recv_sem=recv.at[slot, k],
            device_id=device,
            device_id_type=MESH,
        )

    def across_out(k):
        return copy(0, k, spread_ref.at[0, 0, part(k)], spread_ref.at[0, 1, part(k)], across)

    def beside_out(k):
        return copy(1, k, spread_ref.at[0, 0, part(k)], spread_ref.at[0, 2, part(k)], beside)

    def corner_out(k):
        return copy(2, k, spread_ref.at[0, 1 + odd, part(k)], spread_ref.at[0, 3, part(k)], corner)

    def core_out(k):
        return copy(3, k, spread_ref.at[0, :, part(k)], spread_ref.at[1, :, part(k)], core)

    def finish_rows(k, rows, total):
        values, added, sent = finish(
            total, *[ref[rows].astype(f32) for ref in ins], *[ref[...] for ref in shared]
        )
        for ref, value in zip(outs, values):
            ref[rows] = value.astype(ref.dtype)
        for ref, value in zip(sums, added):
            ref[...] = value if k == 0 else ref[...] + value
        if gather:
            spread_ref[0, 0, rows] = sent
            across_out(k).start()
            beside_out(k).start()

    def pass_corner(k):
        across_out(k).wait_recv()
        beside_out(k).wait_recv()
        corner_out(k).start()

    def pass_core(k):
        corner_out(k).wait_recv()
        core_out(k).start()

    def arrive(k):
        core_out(k).wait_recv()

    if product:
        shard_sum = ShardSum(product_ref, *product_refs)
        shard_sum.start()
    stages, copies = sum_stages(left_ref, matrix_ref, turned, finish_rows, sum_refs, chunks)
    if gather:
        stages = stages + [pass_corner, pass_core, arrive]
        copies = copies + [across_out, beside_out, corner_out, core_out]
    if extra:

        def extra_rows(k, rows, total):
            extra_out[rows] = (extra_middle[rows] + total).astype(extra_out.dtype)

        later, more = sum_stages(extra_left, extra_matrix, False, extra_rows, extra_refs, chunks)
        stages = stages[:1] + [lambda k, a=a, b=b: (a(k), b(k)) for a, b in zip(stages[1:5], later)] + stages[5:]
        copies = copies + more
    run_stages(stages, chunks)
    if product:
        product_out[...] = shard_sum.total()
        shard_sum.end()
    for k in range(chunks):
        for one in copies:
            one(k).wait_send()


def exchange(
    finish,
    left,
    matrix,
    turned,
    row_ins,
    shared_ins,
    row_outs,
    sum_outs,
    gather,
    number,
    product=None,
    extra=None,
    chunks=4,
):
    _, units, rows, _ = left.shape
    width = matrix.shape[0] if turned else matrix.shape[1]
    if not kernels_fit():
        return exchange_plainly(
            finish, left, matrix, turned, row_ins, shared_ins, row_outs, gather, product, extra
        )
    bf16 = jnp.bfloat16
    shapes = [jax.ShapeDtypeStruct((rows, width), dtype) for dtype in row_outs]
    shapes += [jax.ShapeDtypeStruct((1, width), jnp.float32)] * sum_outs
    shapes += [] if product is None else [jax.ShapeDtypeStruct(product.shape[1:], product.dtype)]
    shapes += [] if extra is None else [jax.ShapeDtypeStruct((rows, width), bf16)]
    shapes += [jax.ShapeDtypeStruct((2, units, rows, width), bf16)] * gather
    more = ([] if product is None else [product]) + list(extra or ())
    place = pl.BlockSpec(memory_space=pltpu.VMEM)
    result = pl.pallas_call(
        functools.partial(
            exchange_kernel,
            finish,
            turned,
            len(row_ins),
            len(shared_ins),
            len(row_outs),
            sum_outs,
            gather,
            product is not None,
            extra is not None,
            chunks,
        ),
        out_shape=shapes,
        in_specs=[place] * (2 + len(row_ins) + len(shared_ins))
        + ([] if product is None else [pl.BlockSpec(memory_space=pl.ANY)])
        + [place] * len(extra or ()),
        out_specs=[place] * len(shapes),
        scratch_shapes=sum_scratch(units, rows, width, chunks)
        + [pltpu.SemaphoreType.DMA((4, chunks))] * 2
        + ([] if product is None else shard_sum_scratch(product))
        + ([] if extra is None else sum_scratch(units, rows, width, chunks)),
        compiler_params=pltpu.CompilerParams(
            collective_id=number, has_side_effects=True, vmem_limit_bytes=VMEM_BYTES
        ),
        cost_estimate=lasting(66 if gather else 38),
        name=("exchange_%d" % number),
    )(left, matrix, *row_ins, *shared_ins, *more)
    result = list(result)
    rows_done = [result.pop(0) for _ in row_outs]
    sums = [result.pop(0) for _ in range(sum_outs)]
    product = None if product is None else result.pop(0)
    extra = None if extra is None else result.pop(0)
    return rows_done, sums, (result.pop(0) if gather else None), product, extra


def plane_total(left, matrix, turned):
    multiply = times_transposed if turned else times
    matrix = matrix[:, : left.shape[3]] if turned else matrix
    near, far = [multiply(half.reshape(-1, half.shape[2]), matrix).astype(jnp.bfloat16) for half in left]
    total = near.astype(jnp.float32) + flip(far, 1).astype(jnp.float32)
    return collect(total, (lax.axis_index("seq") % 2) == 1)


def exchange_plainly(finish, left, matrix, turned, row_ins, shared_ins, row_outs, gather, product, extra):
    total = plane_total(left, matrix, turned)
    rows, sums, sent = finish(total, *[value.astype(jnp.float32) for value in row_ins], *shared_ins)
    rows = [value.astype(dtype) for value, dtype in zip(rows, row_outs)]
    if product is not None:
        product = lax.psum_scatter(
            product.reshape(-1, product.shape[2]), "fsdp", scatter_dimension=0, tiled=True
        )
    if extra is not None:
        extra = (plane_total(extra[0], extra[1], False) + extra[2]).astype(jnp.bfloat16)
    if gather:
        odd = (lax.axis_index("seq") % 2) == 1
        sent = jnp.stack(spread(sent, odd)).reshape(*left.shape[:3], -1)
    return rows, sums, sent, product, extra


def finish_middle(total, stream, gain):
    middle = stream + total
    return [middle], [], (middle * rms_scale(middle) * gain).astype(jnp.bfloat16)


def finish_block(total, middle, gain):
    result = (middle + total).astype(jnp.bfloat16)
    stream = result.astype(jnp.float32)
    return [result], [], (stream * rms_scale(stream) * gain).astype(jnp.bfloat16)


def finish_gradient(total, upstream, stream, gain):
    scale = rms_scale(stream)
    weighted = gain * total
    grad = (
        upstream
        + scale * weighted
        - stream * scale**3 * jnp.mean(weighted * stream, -1, keepdims=True)
    )
    added = jnp.sum(total * stream * scale, 0, keepdims=True)
    return [grad], [added], grad.astype(jnp.bfloat16)


LAST_CHUNKS = 4
OWNER_CHUNKS = (6, 1, 1)


def last_kernel(
    left_ref,
    matrix_ref,
    upstream_ref,
    stream_ref,
    gain_ref,
    smalls_ref,
    later_ref,
    product_ref,
    down_product_ref,
    mixer_ref,
    down_ref,
    pair0_ref,
    pair1_ref,
    grad_ref,
    crossed_ref,
    smalls_out,
    pair_out,
    down_out,
    mixer_out,
    *scratch,
):
    sum_refs, scratch = scratch[:8], scratch[8:]
    pair_both, down_both, mixer_both, grad_low, gain_sum = scratch[:5]
    small_sum, small_sent, small_side, small_z = scratch[5:9]
    local, own_send, own_recv, small_send, small_recv, cross_send, cross_recv = scratch[9:16]
    mixer_sum = ShardSum(product_ref, *scratch[16:20])
    down_sum = ShardSum(down_product_ref, *scratch[20:])
    x, q, z = lax.axis_index("section"), lax.axis_index("seq"), lax.axis_index("fsdp")
    shards = lax.axis_size("fsdp")
    _, core, across, beside, _ = peers()
    f32, bf16 = jnp.float32, jnp.bfloat16
    others = other_shards()
    greet([core, across, beside] + others)
    share = x * 4 + q
    share_across = (1 - x) * 4 + q
    beside_q = (1 - q // 2) * 2 + q % 2
    share_beside = x * 4 + beside_q
    share_corner = (1 - x) * 4 + beside_q

    def remote(source, target, send, recv, device):
        return pltpu.make_async_remote_copy(
            src_ref=source,
            dst_ref=target,
            send_sem=send,
            recv_sem=recv,
            device_id=device,
            device_id_type=MESH,
        )

    mixer_sum.start()
    loads = [
        pltpu.make_async_copy(pair0_ref, pair_both.at[0], local.at[0]),
        pltpu.make_async_copy(pair1_ref, pair_both.at[1], local.at[1]),
        pltpu.make_async_copy(down_ref, down_both.at[1], local.at[2]),
        pltpu.make_async_copy(mixer_ref, mixer_both.at[1], local.at[3]),
    ]
    for one in loads:
        one.start()

    class Owners:
        def __init__(self, place, both, out):
            self.place, self.both, self.out = place, both, out
            self.step = both.shape[1] // OWNER_CHUNKS[place]
            self.chunks = range(OWNER_CHUNKS[place])

        def move(self, slot, k, source, target, device):
            part = pl.ds(k * self.step, self.step)
            place = self.place
            return remote(
                source.at[part],
                self.out.at[target, part],
                own_send.at[place, slot, k],
                own_recv.at[place, slot, k],
                device,
            )

        def cross(self, k):
            return self.move(0, k, self.both.at[1 - x], share, across)

        def side(self, k):
            return self.move(1, k, self.both.at[x], share, beside)

        def near(self, k):
            return self.move(2, k, self.both.at[x], share, core)

        def side_across(self, k):
            return self.move(3, k, self.out.at[share_across], share_across, beside)

        def near_across(self, k):
            return self.move(4, k, self.out.at[share_across], share_across, core)

        def near_beside(self, k):
            return self.move(5, k, self.out.at[share_beside], share_beside, core)

        def near_corner(self, k):
            return self.move(6, k, self.out.at[share_corner], share_corner, core)

        def keep(self):
            return pltpu.make_async_copy(self.both.at[x], self.out.at[share], local.at[4 + self.place])

        def first(self, k):
            self.cross(k).start()
            self.side(k).start()
            self.near(k).start()

        def second(self, k):
            self.cross(k).wait_recv()
            self.side_across(k).start()
            self.near_across(k).start()

        def third(self, k):
            self.side(k).wait_recv()
            self.near_beside(k).start()

        def fourth(self, k):
            self.side_across(k).wait_recv()
            self.near_corner(k).start()

        def end(self):
            for k in self.chunks:
                for one in (self.near, self.near_across, self.near_beside, self.near_corner):
                    one(k).wait_recv()
                for one in (
                    self.cross,
                    self.side,
                    self.near,
                    self.side_across,
                    self.near_across,
                    self.near_beside,
                    self.near_corner,
                ):
                    one(k).wait_send()
            self.keep().wait()

    pair = Owners(0, pair_both, pair_out)
    down = Owners(1, down_both, down_out)
    mixer = Owners(2, mixer_both, mixer_out)
    for one in loads[:2]:
        one.wait()
    pair.keep().start()

    def finish_rows(k, rows, total):
        (grad,), (added,), sent = finish_gradient(
            total, upstream_ref[rows].astype(f32), stream_ref[rows].astype(f32), gain_ref[...]
        )
        grad_ref[rows] = grad
        grad_low[rows] = sent
        gain_sum[...] = added if k == 0 else gain_sum[...] + added

    stages, copies = sum_stages(left_ref, matrix_ref, True, finish_rows, sum_refs, LAST_CHUNKS)
    pieces = [(pair, k) for k in pair.chunks]
    for tick in range(ticks_of(stages, LAST_CHUNKS)):
        run_tick(stages, LAST_CHUNKS, tick)
        for owners, k in pieces[tick : tick + 1]:
            owners.first(k)
        if tick == 1:
            down_sum.start()
    cross = remote(grad_low, crossed_ref.at[0], cross_send.at[0], cross_recv.at[0], across)
    cross.start()
    later = remote(later_ref, crossed_ref.at[1], cross_send.at[1], cross_recv.at[1], across)
    later.start()
    for owners, k in pieces[:2]:
        owners.second(k)

    mixer_both[0] = mixer_sum.total()
    loads[3].wait()
    mixer.keep().start()
    mixer.first(0)
    for owners, k in pieces[2:]:
        owners.second(k)
    for owners, k in pieces:
        owners.third(k)

    mixer.second(0)
    mixer.third(0)
    down_both[0] = down_sum.total()
    loads[2].wait()
    down.keep().start()
    down.first(0)
    small_rows = smalls_ref.shape[3]
    small_sum[...] = smalls_ref[...]
    for shard in range(shards):
        small_sum[0, shard, 0:1] += gain_sum[:, shard * small_rows : (shard + 1) * small_rows]
    for step, device in enumerate((core, across, beside)):
        small_sent[step] = small_sum[...]
        one = remote(small_sent.at[step], small_side.at[step], small_send.at[step], small_recv.at[step], device)
        one.start()
        one.wait()
        small_sum[...] += small_side[step]
    small_moves = []
    for step, device in enumerate(others):
        one = remote(
            small_sum.at[x, (z + step + 1) % shards],
            small_z.at[step],
            small_send.at[3 + step],
            small_recv.at[3 + step],
            device,
        )
        one.start()
        small_moves.append(one)
    small_total = small_sum[x, z]
    for step, one in enumerate(small_moves):
        one.wait()
        small_total = small_total + small_z[step]
    smalls_out[...] = small_total

    for owners, k in pieces:
        owners.fourth(k)
    down.second(0)
    down.third(0)
    mixer.fourth(0)
    down.fourth(0)
    for owners in (pair, down, mixer):
        owners.end()
    cross.wait()
    later.wait()
    mixer_sum.end()
    down_sum.end()
    for k in range(LAST_CHUNKS):
        for one in copies:
            one(k).wait_send()


def last_exchange(left, matrix, upstream, stream, gain, smalls, later, product, down_product, mixer, down, pairs):
    _, units, rows, _ = left.shape
    width = matrix.shape[0]
    shards, shard_rows, mixer_columns = product.shape
    bf16, f32 = jnp.bfloat16, jnp.float32
    count = 2 * units
    vmem = pl.BlockSpec(memory_space=pltpu.VMEM)
    anywhere = pl.BlockSpec(memory_space=pl.ANY)
    return pl.pallas_call(
        last_kernel,
        out_shape=[
            jax.ShapeDtypeStruct((rows, width), f32),
            jax.ShapeDtypeStruct((2, rows, width), bf16),
            jax.ShapeDtypeStruct(smalls.shape[2:], f32),
            jax.ShapeDtypeStruct((count, *pairs[0].shape), bf16),
            jax.ShapeDtypeStruct((count, *down.shape), bf16),
            jax.ShapeDtypeStruct((count, shard_rows, mixer_columns), bf16),
        ],
        in_specs=[vmem] * 7 + [anywhere] * 6,
        out_specs=[vmem] * 3 + [anywhere] * 3,
        scratch_shapes=sum_scratch(units, rows, width, LAST_CHUNKS)
        + [
            pltpu.VMEM((2, *pairs[0].shape), bf16),
            pltpu.VMEM((2, *down.shape), bf16),
            pltpu.VMEM((2, shard_rows, mixer_columns), bf16),
            pltpu.VMEM((rows, width), bf16),
            pltpu.VMEM((1, width), f32),
            pltpu.VMEM(smalls.shape, f32),
            pltpu.VMEM((3, *smalls.shape), f32),
            pltpu.VMEM((3, *smalls.shape), f32),
            pltpu.VMEM((shards - 1, *smalls.shape[2:]), f32),
            pltpu.SemaphoreType.DMA((7,)),
            pltpu.SemaphoreType.DMA((3, 7, max(OWNER_CHUNKS))),
            pltpu.SemaphoreType.DMA((3, 7, max(OWNER_CHUNKS))),
            pltpu.SemaphoreType.DMA((2 + shards,)),
            pltpu.SemaphoreType.DMA((2 + shards,)),
            pltpu.SemaphoreType.DMA((2,)),
            pltpu.SemaphoreType.DMA((2,)),
        ]
        + shard_sum_scratch(product)
        + shard_sum_scratch(down_product),
        compiler_params=pltpu.CompilerParams(
            collective_id=20, has_side_effects=True, vmem_limit_bytes=VMEM_BYTES
        ),
        cost_estimate=lasting(130),
        name="last_exchange",
    )(left, matrix, upstream, stream, gain, smalls, later, product, down_product, mixer, down, *pairs)


def place_kernel(blocks, width, stride, stack_ref, *outs):
    shards = lax.axis_size("fsdp")
    count = stack_ref.shape[0]
    part = width // shards // count
    for block in range(blocks):
        pieces = []
        for shard in range(shards):
            start = block * stride + shard * part
            pieces += [stack_ref[share, :, start : start + part] for share in range(count)]
        value = jnp.concatenate(pieces, 1).astype(jnp.float32)
        if len(outs) == 1:
            outs[0][:, block * width : (block + 1) * width] = value
        else:
            outs[block][...] = value


def place_columns(stack, blocks, width, stride, together):
    count, rows, columns = stack.shape
    step = 48
    widths = [blocks * width] if together else [width] * blocks
    return pl.pallas_call(
        functools.partial(place_kernel, blocks, width, stride),
        grid=(rows // step,),
        out_shape=[jax.ShapeDtypeStruct((rows, each), jnp.float32) for each in widths],
        in_specs=[pl.BlockSpec((count, step, columns), lambda i: (0, i, 0))],
        out_specs=[pl.BlockSpec((step, each), lambda i: (i, 0)) for each in widths],
        compiler_params=pltpu.CompilerParams(vmem_limit_bytes=VMEM_BYTES),
        cost_estimate=lasting(14),
        name="place_columns",
    )(stack)


def local_call(kernel, outs, scratch, us, name, *operands):
    place = pl.BlockSpec(memory_space=pltpu.VMEM)
    return pl.pallas_call(
        kernel,
        out_shape=[jax.ShapeDtypeStruct(shape, dtype) for shape, dtype in outs],
        in_specs=[place] * len(operands),
        out_specs=[place] * len(outs),
        scratch_shapes=[pltpu.VMEM(shape, dtype) for shape, dtype in scratch],
        compiler_params=pltpu.CompilerParams(vmem_limit_bytes=VMEM_BYTES),
        cost_estimate=lasting(us),
        name=name,
    )(*operands)


def unit_place(difference):
    return difference // 4 + (difference // 2 % 2) * 2 + (difference % 2) * 4


def unit_bits(place):
    return (place % 2) * 4 + (place // 2 % 2) * 2 + place // 4


def either(left, right):
    total = 0
    for bit in (1, 2, 4):
        one, two = left // bit % 2, right // bit % 2
        total = total + bit * (one + two - 2 * one * two)
    return total


def neighbour(place, step):
    share = lax.axis_index("section") * 4 + lax.axis_index("seq")
    device = either(share, unit_bits(place))
    seq = device % 4 + step
    inside = jnp.where((seq >= 0) & (seq < 4), 1.0, 0.0)
    seq = (seq + 4) % 4
    return unit_place(either(share, device // 4 * 4 + seq)), inside


def conv_parts(held_ref, place):
    f32 = jnp.float32
    before, inside = neighbour(place, -1)
    here = held_ref[place]
    rows = here.shape[0]
    edge = held_ref[before, rows - 2 : rows] * inside
    whole = jnp.concatenate([edge.astype(f32), here], 0)
    return whole[:rows], whole[1 : rows + 1], here


def mixer_forward_kernel(channels, normed_ref, matrix_ref, taps_ref, projected_ref, held_ref, gated_ref):
    f32, bf16 = jnp.float32, jnp.bfloat16

    def project(place, carry):
        value = jnp.dot(
            normed_ref[place], matrix_ref[:, : 3 * channels], preferred_element_type=f32
        )
        projected_ref[place] = value
        held_ref[place] = (value[:, :channels] * value[:, 2 * channels :]).astype(bf16).astype(f32)
        return carry

    lax.fori_loop(0, 8, project, 0)

    def convolve(place, carry):
        first, second, third = conv_parts(held_ref, place)
        value = taps_ref[0:1] * first + taps_ref[1:2] * second + taps_ref[2:3] * third
        gated_ref[place] = (projected_ref[place, :, channels : 2 * channels] * value).astype(bf16)
        return carry

    lax.fori_loop(0, 8, convolve, 0)


def mixer_forward(normed, matrix, taps):
    rows = normed.shape[2]
    channels = taps.shape[1]
    f32, bf16 = jnp.float32, jnp.bfloat16
    return local_call(
        functools.partial(mixer_forward_kernel, channels),
        [((8, rows, 3 * channels), f32), ((8, rows, channels), f32), ((8, rows, channels), bf16)],
        [],
        10,
        "mixer_forward",
        normed.reshape(8, rows, -1),
        matrix,
        taps,
    )


def mixer_backward_kernel(
    channels, grad_ref, matrix_ref, projected_ref, held_ref, taps_ref, out_ref, taps_out, conv_grad, gate_grad
):
    f32, bf16 = jnp.float32, jnp.bfloat16

    def to_gates(place, carry):
        grad = lax.dot_general(
            grad_ref[place], matrix_ref[...], (((1,), (1,)), ((), ())), preferred_element_type=f32
        )
        first, second, third = conv_parts(held_ref, place)
        value = taps_ref[0:1] * first + taps_ref[1:2] * second + taps_ref[2:3] * third
        back = grad * projected_ref[place, :, channels : 2 * channels]
        gate_grad[place] = grad * value
        conv_grad[place] = back
        added = [jnp.sum(back * shifted, 0, keepdims=True) for shifted in (first, second, third)]
        return carry + jnp.concatenate(added + [jnp.zeros((5, channels), f32)], 0)

    taps_out[...] = lax.fori_loop(0, 8, to_gates, jnp.zeros((8, channels), f32))

    def to_inputs(place, carry):
        after, inside = neighbour(place, 1)
        here = conv_grad[place]
        rows = here.shape[0]
        whole = jnp.concatenate([here, conv_grad[after, 0:2] * inside], 0)
        grad = (
            taps_ref[0:1] * whole[2:] + taps_ref[1:2] * whole[1 : rows + 1] + taps_ref[2:3] * here
        )
        out_ref[place] = jnp.concatenate(
            [
                grad * projected_ref[place, :, 2 * channels :],
                gate_grad[place],
                grad * projected_ref[place, :, :channels],
            ],
            1,
        ).astype(bf16)
        return carry

    lax.fori_loop(0, 8, to_inputs, 0)


def mixer_backward(grads, matrix, projected, held, taps):
    rows = grads.shape[2]
    channels = taps.shape[1]
    f32, bf16 = jnp.float32, jnp.bfloat16
    return local_call(
        functools.partial(mixer_backward_kernel, channels),
        [((8, rows, 3 * channels), bf16), ((8, channels), f32)],
        [((8, rows, channels), f32), ((8, rows, channels), f32)],
        12,
        "mixer_backward",
        grads.reshape(8, rows, -1),
        matrix,
        projected,
        held,
        taps,
    )


def ffn_forward_kernel(pad, normed_ref, matrix_ref, pairs_ref, hidden_ref):
    pairs = jnp.dot(normed_ref[...], matrix_ref[:, : 2 * pad], preferred_element_type=jnp.float32)
    pairs_ref[...] = pairs
    gate, up = pairs[:, :pad], pairs[:, pad:]
    hidden = gate * jax.nn.sigmoid(gate) * up
    hidden_ref[...] = hidden[:, : hidden_ref.shape[1]].astype(jnp.bfloat16)


def ffn_forward(normed, matrix, pad, columns):
    count, width = normed.shape
    step = 256
    return pl.pallas_call(
        functools.partial(ffn_forward_kernel, pad),
        grid=(count // step,),
        out_shape=[
            jax.ShapeDtypeStruct((count, 2 * pad), jnp.float32),
            jax.ShapeDtypeStruct((count, columns), jnp.bfloat16),
        ],
        in_specs=[
            pl.BlockSpec((step, width), lambda i: (i, 0)),
            pl.BlockSpec(matrix.shape, lambda i: (0, 0)),
        ],
        out_specs=[
            pl.BlockSpec((step, 2 * pad), lambda i: (i, 0)),
            pl.BlockSpec((step, columns), lambda i: (i, 0)),
        ],
        compiler_params=pltpu.CompilerParams(vmem_limit_bytes=VMEM_BYTES),
        cost_estimate=lasting(16),
        name="ffn_forward",
    )(normed, matrix)


def ffn_backward_kernel(pad, grad_ref, matrix_ref, pairs_ref, out_ref):
    grad = lax.dot_general(
        grad_ref[...], matrix_ref[...], (((1,), (1,)), ((), ())), preferred_element_type=jnp.float32
    )
    extra = pad - grad.shape[1]
    if extra:
        grad = jnp.concatenate([grad, jnp.zeros((grad.shape[0], extra), jnp.float32)], 1)
    gate, up = pairs_ref[:, :pad], pairs_ref[:, pad:]
    sigmoid = jax.nn.sigmoid(gate)
    out_ref[:, :pad] = (grad * up * sigmoid * (1.0 + gate * (1.0 - sigmoid))).astype(jnp.bfloat16)
    out_ref[:, pad:] = (grad * gate * sigmoid).astype(jnp.bfloat16)


def ffn_backward(grads, matrix, pairs, pad):
    count, width = grads.shape
    step = 256
    return pl.pallas_call(
        functools.partial(ffn_backward_kernel, pad),
        grid=(count // step,),
        out_shape=jax.ShapeDtypeStruct((count, 2 * pad), jnp.bfloat16),
        in_specs=[
            pl.BlockSpec((step, width), lambda i: (i, 0)),
            pl.BlockSpec(matrix.shape, lambda i: (0, 0)),
            pl.BlockSpec((step, 2 * pad), lambda i: (i, 0)),
        ],
        out_specs=pl.BlockSpec((step, 2 * pad), lambda i: (i, 0)),
        compiler_params=pltpu.CompilerParams(vmem_limit_bytes=VMEM_BYTES),
        cost_estimate=lasting(16),
        name="ffn_backward",
    )(grads, matrix, pairs)


def mixer_product_kernel(shards, normed_ref, projected_ref, gated_ref, grad_ref, out_ref):
    f32, bf16 = jnp.float32, jnp.bfloat16
    turned = (((0,), (0,)), ((), ()))
    columns = projected_ref.shape[1]
    width, channels = normed_ref.shape[1], gated_ref.shape[1]
    step = 256
    for start in range(0, width, step):
        out_ref[start : start + step, :columns] = lax.dot_general(
            normed_ref[:, start : start + step], projected_ref[...], turned, preferred_element_type=f32
        ).astype(bf16)
    value = lax.dot_general(gated_ref[...], grad_ref[...], turned, preferred_element_type=f32)
    part = channels // shards
    blocks = width // channels
    for shard in range(shards):
        for block in range(blocks):
            row = (shard * blocks + block) * part
            out_ref[row : row + part, columns:] = value[
                shard * part : (shard + 1) * part, block * channels : (block + 1) * channels
            ].astype(bf16)


def mixer_products(normed, projected_grad, gated, grad):
    width, columns, channels = normed.shape[1], projected_grad.shape[1], gated.shape[1]
    shards = lax.axis_size("fsdp")
    (value,) = local_call(
        functools.partial(mixer_product_kernel, shards),
        [((width, columns + channels), jnp.bfloat16)],
        [],
        14,
        "mixer_products",
        normed,
        projected_grad,
        gated,
        grad,
    )
    return value


def flip(value, bits):
    count = lax.axis_size("section") * lax.axis_size("seq")
    return lax.ppermute(value, PLANE, [(source, source ^ bits) for source in range(count)])


def flip_by_core(value, even_bits, odd_bits):
    count = lax.axis_size("section") * lax.axis_size("seq")
    pairs = [(source, source ^ (odd_bits if source & 1 else even_bits)) for source in range(count)]
    return lax.ppermute(value, PLANE, pairs)


def chip_bits():
    bits = [lax.axis_size("seq")]
    step = lax.axis_size("seq") // 2
    while step > 1:
        bits.append(step)
        step //= 2
    return bits


def half_units():
    units = [0]
    for bits in chip_bits():
        units = units + [unit | bits for unit in units]
    return units


def spread_chips(own, odd):
    bits = chip_bits()
    if len(bits) == 2:
        first = flip(own, bits[0])
        second = flip(own, bits[1])
        third = flip_by_core(jnp.where(odd, second, first), bits[1], bits[0])
        return jnp.concatenate([own, first, second, third], 0)
    held = own
    for step in bits:
        held = jnp.concatenate([held, flip(held, step)], 0)
    return held


def spread(own, odd):
    near = spread_chips(own, odd)
    return near, flip(near, 1)


def collect(near, odd):
    bits = chip_bits()
    if len(bits) == 2:
        rows = near.shape[0] // 4
        held = near
        third = flip_by_core(held[3 * rows :].astype(jnp.bfloat16), bits[1], bits[0]).astype(jnp.float32)
        first = held[rows : 2 * rows] + jnp.where(odd, 0.0, third)
        second = held[2 * rows : 3 * rows] + jnp.where(odd, third, 0.0)
        first = flip(first.astype(jnp.bfloat16), bits[0]).astype(jnp.float32)
        second = flip(second.astype(jnp.bfloat16), bits[1]).astype(jnp.float32)
        return held[:rows] + first + second
    held = near
    for step in reversed(bits):
        rows = held.shape[0] // 2
        held = held[:rows] + flip(held[rows:].astype(jnp.bfloat16), step).astype(jnp.float32)
    return held


def rms_scale(stream):
    return lax.rsqrt(jnp.mean(stream * stream, -1, keepdims=True) + EPSILON)


def times(left, matrix):
    return jnp.dot(left, matrix, preferred_element_type=jnp.float32)


def times_transposed(left, matrix):
    return lax.dot_general(
        left, matrix, (((1,), (1,)), ((), ())), preferred_element_type=jnp.float32
    )


def by_rows(value):
    return with_layout_constraint(value, Layout(major_to_minor=tuple(range(value.ndim))))


def row_products(left, right):
    return lax.dot_general(
        left, right, (((0,), (0,)), ((), ())), preferred_element_type=jnp.float32
    ).astype(jnp.bfloat16)


def normed_with(stream, gain):
    return (stream * rms_scale(stream) * gain).astype(jnp.bfloat16)


def pick_columns(matrix, share, width, count):
    shards = lax.axis_size("fsdp")
    part = width // shards // count
    return jnp.concatenate(
        [
            lax.dynamic_slice(
                matrix, (0, start + shard * (width // shards) + share * part), (matrix.shape[0], part)
            )
            for start in range(0, matrix.shape[1], width)
            for shard in range(shards)
        ],
        1,
    )


def pick_rows(matrix, share, count):
    part = matrix.shape[0] // count
    return lax.dynamic_slice(matrix, (share * part, 0), (part, matrix.shape[1]))


SPREAD_CHUNKS = 4
SPREAD_MOVES = 3 * SPREAD_CHUNKS + 1
FFN_CHUNKS = 2 * SPREAD_CHUNKS


class Spread:
    def __init__(self, rows_of, out_ref, send, recv):
        self.rows_of, self.out_ref, self.send, self.recv = rows_of, out_ref, send, recv
        _, self.core, _, self.beside, _ = peers()
        step = out_ref.shape[2] // SPREAD_CHUNKS
        self.parts = [pl.ds(k * step, step) for k in range(SPREAD_CHUNKS)]

    def side(self, k, slot):
        number = 2 * k + slot
        return remote_copy(
            self.rows_of(slot, self.parts[k]),
            self.out_ref.at[0, 2 + slot, self.parts[k]],
            self.send.at[number],
            self.recv.at[number],
            self.beside,
        )

    def over(self, k):
        number = 2 * SPREAD_CHUNKS + 1 + k
        part = self.parts[k]
        return remote_copy(
            self.out_ref.at[0, 2:4, part],
            self.out_ref.at[1, 2:4, part],
            self.send.at[number],
            self.recv.at[number],
            self.core,
        )

    def near(self):
        number = 2 * SPREAD_CHUNKS
        return remote_copy(
            self.out_ref.at[0, 0:2],
            self.out_ref.at[1, 0:2],
            self.send.at[number],
            self.recv.at[number],
            self.core,
        )

    def first(self, k):
        self.side(k, 0).start()
        self.side(k, 1).start()

    def second(self, k):
        self.side(k, 0).wait_recv()
        self.side(k, 1).wait_recv()
        self.over(k).start()

    def end(self):
        self.near().wait()
        for k in range(SPREAD_CHUNKS):
            self.over(k).wait()
            self.side(k, 0).wait_send()
            self.side(k, 1).wait_send()


def start_kernel(
    small_ref,
    tokens_ref,
    ffn_sent,
    small_out,
    normed_out,
    ffn_out,
    local,
    small_send,
    small_recv,
    spread_send,
    spread_recv,
    cross_send,
    cross_recv,
):
    x, z = lax.axis_index("section"), lax.axis_index("fsdp")
    shards = lax.axis_size("fsdp")
    _, core, across, beside, _ = peers()
    others = [
        {"section": (x + step // shards) % 2, "fsdp": (z + step) % shards} for step in range(1, 2 * shards)
    ]
    greet([core, beside] + others)
    smalls = [
        remote_copy(small_ref, small_out.at[x, z], small_send.at[step], small_recv.at[step], device)
        for step, device in enumerate(others)
    ]
    step = ffn_sent.shape[0] // FFN_CHUNKS
    crossing = []
    for k in range(FFN_CHUNKS):
        part = pl.ds(k * step, step)
        crossing.append(
            remote_copy(
                ffn_sent.at[part], ffn_out.at[part], cross_send.at[k], cross_recv.at[k], across
            )
        )
    keep = pltpu.make_async_copy(small_ref, small_out.at[x, z], local.at[0])
    normed = Spread(lambda slot, part: normed_out.at[0, slot, part], normed_out, spread_send, spread_recv)
    for one in smalls + [keep]:
        one.start()
    crossing[0].start()
    for one in smalls:
        one.wait_recv()
    keep.wait()
    gain = jnp.concatenate([small_out[0, shard, 0:1] for shard in range(shards)], 1)
    for k in range(SPREAD_CHUNKS):
        for slot, place in ((x, 0), (1 - x, 1)):
            part = normed.parts[k]
            normed_out[0, place, part] = normed_with(tokens_ref[slot, part].astype(jnp.float32), gain)
        normed.first(k)
        if k >= 1:
            crossing[k].start()
    normed.near().start()
    for k in range(SPREAD_CHUNKS):
        crossing[SPREAD_CHUNKS + k].start()
        normed.second(k)
    normed.end()
    for one in crossing:
        one.wait()
    for one in smalls:
        one.wait_send()


def start(small, tokens, ffn_sent):
    shards = lax.axis_size("fsdp")
    _, rows, width = tokens.shape
    f32, bf16 = jnp.float32, jnp.bfloat16
    if not kernels_fit():
        seq_count = lax.axis_size("seq")
        every = lax.all_gather(small, ("section", "fsdp"), axis=0).reshape(2, shards, *small.shape)
        gain = every[0, :, 0].reshape(width)
        return (
            every,
            normed_with(spread_plainly(tokens).astype(f32), gain),
            flip(ffn_sent, seq_count),
        )
    place = pl.BlockSpec(memory_space=pltpu.VMEM)
    anywhere = pl.BlockSpec(memory_space=pl.ANY)
    return pl.pallas_call(
        start_kernel,
        out_shape=[
            jax.ShapeDtypeStruct((2, shards, *small.shape), f32),
            jax.ShapeDtypeStruct((2, 4, rows, width), bf16),
            jax.ShapeDtypeStruct(ffn_sent.shape, bf16),
        ],
        in_specs=[place] * 2 + [anywhere],
        out_specs=[place] * 2 + [anywhere],
        scratch_shapes=[
            pltpu.SemaphoreType.DMA((1,)),
            pltpu.SemaphoreType.DMA((2 * shards - 1,)),
            pltpu.SemaphoreType.DMA((2 * shards - 1,)),
            pltpu.SemaphoreType.DMA((SPREAD_MOVES,)),
            pltpu.SemaphoreType.DMA((SPREAD_MOVES,)),
            pltpu.SemaphoreType.DMA((FFN_CHUNKS,)),
            pltpu.SemaphoreType.DMA((FFN_CHUNKS,)),
        ],
        compiler_params=pltpu.CompilerParams(
            collective_id=21, has_side_effects=True, vmem_limit_bytes=VMEM_BYTES
        ),
        cost_estimate=lasting(55),
        name="start",
    )(small, tokens, ffn_sent)


def spread_kernel(rows_ref, out_ref, local, send, recv):
    x = lax.axis_index("section")
    _, core, _, beside, _ = peers()
    greet([core, beside])
    keeps = [
        pltpu.make_async_copy(rows_ref.at[x], out_ref.at[0, 0], local.at[0]),
        pltpu.make_async_copy(rows_ref.at[1 - x], out_ref.at[0, 1], local.at[1]),
    ]
    for one in keeps:
        one.start()
    move = Spread(lambda slot, part: rows_ref.at[x if slot == 0 else 1 - x, part], out_ref, send, recv)
    for k in range(SPREAD_CHUNKS):
        move.first(k)
    for one in keeps:
        one.wait()
    move.near().start()
    for k in range(SPREAD_CHUNKS):
        move.second(k)
    move.end()


def spread_slots(tokens):
    _, rows, width = tokens.shape
    if not kernels_fit():
        return spread_plainly(tokens)
    place = pl.BlockSpec(memory_space=pltpu.VMEM)
    return pl.pallas_call(
        spread_kernel,
        out_shape=jax.ShapeDtypeStruct((2, 4, rows, width), tokens.dtype),
        in_specs=[place],
        out_specs=place,
        scratch_shapes=[
            pltpu.SemaphoreType.DMA((2,)),
            pltpu.SemaphoreType.DMA((SPREAD_MOVES,)),
            pltpu.SemaphoreType.DMA((SPREAD_MOVES,)),
        ],
        compiler_params=pltpu.CompilerParams(
            collective_id=22, has_side_effects=True, vmem_limit_bytes=VMEM_BYTES
        ),
        cost_estimate=lasting(42),
        name="spread_slots",
    )(tokens)


def spread_plainly(tokens):
    x = lax.axis_index("section")
    _, rows, width = tokens.shape
    near = jnp.concatenate(
        [lax.dynamic_index_in_dim(tokens, x, 0, False), lax.dynamic_index_in_dim(tokens, 1 - x, 0, False)], 0
    )
    for step in chip_bits()[1:]:
        near = jnp.concatenate([near, flip(near, step)], 0)
    return jnp.stack([near, flip(near, 1)]).reshape(2, -1, rows, width)


def body(
    tokens,
    in_weight,
    conv_kernel,
    out_weight,
    gate_weight,
    up_weight,
    down_weight,
    mixer_gain,
    ffn_gain,
    cotangent,
):
    bf16, f32 = jnp.bfloat16, jnp.float32
    x_index = lax.axis_index("section")
    q_index = lax.axis_index("seq")
    seq_count = lax.axis_size("seq")
    count = lax.axis_size("section") * seq_count
    shards = lax.axis_size("fsdp")
    share = x_index * seq_count + q_index
    first_plane = x_index == 0
    width = tokens.shape[3]
    rows = tokens.shape[2]
    hidden_width = gate_weight.shape[2]
    shard_rows = width // shards
    in_columns = 3 * width // count
    channels = width // count
    ffn_columns = hidden_width // count
    ffn_pad = -(-ffn_columns // 128) * 128
    units = half_units()
    half = len(units)
    part = shard_rows // count

    other = share ^ seq_count

    def in_share(index):
        return pick_columns(in_weight[0], index, width, count)

    def out_share(index):
        return pick_rows(out_weight[0], index, count)

    def ffn_share(index):
        nothing = jnp.zeros((shard_rows, ffn_pad - ffn_columns), bf16)
        return jnp.concatenate(
            [
                pick_columns(gate_weight[0], index, hidden_width, count),
                nothing,
                pick_columns(up_weight[0], index, hidden_width, count),
                nothing,
                pick_rows(down_weight[0], index, count).reshape(shard_rows, -1),
            ],
            1,
        )

    small = jnp.concatenate(
        [
            mixer_gain.astype(f32),
            ffn_gain.astype(f32),
            conv_kernel[0].T.astype(f32),
            jnp.zeros((3, shard_rows), f32),
        ],
        0,
    )
    def over_fsdp(value):
        return lax.all_gather(value, "fsdp", axis=0, tiled=True)

    def pack_rows(value):
        return value.reshape(part, count, channels).transpose(1, 0, 2).reshape(shard_rows, channels)

    def unpack_rows(value):
        return value.reshape(-1, count, part, channels).transpose(0, 2, 1, 3).reshape(-1, width)

    def mixer_share(index):
        return jnp.concatenate([in_share(index), pack_rows(out_share(index))], 1)

    def over_mixers(value):
        value = over_fsdp(value)
        return value[:, :in_columns], unpack_rows(value[:, in_columns:])

    mixer_own = over_mixers(mixer_share(share))
    mixer_sent = flip(mixer_share(other), seq_count)
    mixer_sent, ffn_kept, ffn_sent = tie(mixer_sent, ffn_share(share), ffn_share(other))
    small, mixer_sent = tie(small, mixer_sent)
    small, normed, ffn_sent = start(small, tokens[:, 0], ffn_sent)
    mixer_across = over_mixers(mixer_sent)
    mixer_matrices = [
        [jnp.where(first_plane == kept, own, across) for own, across in zip(mixer_own, mixer_across)]
        for kept in (True, False)
    ]
    ffn_parts = [
        jnp.where(first_plane, ffn_kept, ffn_sent),
        jnp.where(first_plane, ffn_sent, ffn_kept),
    ]
    small = small.transpose(0, 2, 1, 3)
    whole = small.reshape(2, 8, width)
    taps_all = lax.dynamic_slice(
        small[:, 2:5].reshape(2, 3, shards, count, part), (0, 0, 0, share, 0), (2, 3, shards, 1, part)
    ).reshape(2, 3, shards * part)

    pair_columns = 2 * ffn_pad
    *mixer_matrices[0], pair_part, down_part = tie(
        *mixer_matrices[0], ffn_parts[0][:, :pair_columns], ffn_parts[0][:, pair_columns:]
    )
    pair = over_fsdp(pair_part)
    ids = jnp.stack([share ^ unit ^ side for side in (0, 1) for unit in units])
    has_before = (ids % seq_count) > 0
    has_after = (ids % seq_count) < seq_count - 1
    before_pick = (ids[None, :] == (ids - 1)[:, None]) & has_before[:, None]
    after_pick = (ids[None, :] == (ids + 1)[:, None]) & has_after[:, None]

    def pick_units(mask, edge):
        return jnp.sum(jnp.where(mask[:, :, None, None], edge[None].astype(f32), 0.0), 1)

    def flat(value):
        return value.reshape(2 * half * rows, value.shape[-1])

    def in_units(value):
        return value.reshape(2, half, rows, value.shape[-1])

    def gain_row(block, kind):
        return whole[block, kind : kind + 1]

    stream = lax.dynamic_index_in_dim(tokens[:, 0], x_index, 0, False)
    saved = []
    outputs = []
    for block in range(2):
        in_matrix, out_matrix = mixer_matrices[block]
        taps = taps_all[block]
        if kernels_fit():
            projected, held, gated = mixer_forward(normed, in_matrix, taps)
            gated = flat(gated)
            if block == 1:
                gated, crossed_out = tie(gated, crossed_out)
        else:
            projected = times(flat(normed), in_matrix[:, :in_columns])
            b_gate = projected[:, :channels]
            c_gate = projected[:, channels : 2 * channels]
            x_value = projected[:, 2 * channels :]
            conv_input = (b_gate * x_value).astype(bf16).reshape(2 * half, rows, channels)
            earlier = pick_units(before_pick, conv_input[:, -2:])
            held = jnp.concatenate([earlier, conv_input.astype(f32)], 1)
            conv_out = taps[0] * held[:, :-2] + taps[1] * held[:, 1:-1] + taps[2] * held[:, 2:]
            gated = flat((c_gate.reshape(conv_out.shape) * conv_out).astype(bf16))
        (middle,), _, normed_ffn, _, _ = exchange(
            finish_middle,
            in_units(gated),
            out_matrix,
            False,
            [stream],
            [gain_row(block, 1)],
            [f32],
            0,
            True,
            1 + 2 * block,
        )
        if block == 0:
            pair, normed_ffn, value = tie(pair, normed_ffn, down_part.reshape(-1, width))
            down = over_fsdp(value)
            ffn_matrices = [(pair, down), None]
        pair_matrix, down_matrix = ffn_matrices[block]
        if kernels_fit():
            pairs, hidden = ffn_forward(flat(normed_ffn), pair_matrix, ffn_pad, ffn_columns)
        else:
            pairs = times(flat(normed_ffn), pair_matrix[:, :pair_columns])
            hidden = (jax.nn.silu(pairs[:, :ffn_pad]) * pairs[:, ffn_pad:]).astype(bf16)[:, :ffn_columns]
        if block == 0:
            hidden, grad_rows = tie(hidden, cotangent[:, 0])
            hidden, grad_units = tie(hidden, spread_slots(grad_rows))
            hidden, down, value = tie(hidden, down, ffn_parts[1])
            down_matrix = down
            ffn = over_fsdp(value)
            ffn_matrices = [(pair, down), (ffn, ffn[:, pair_columns:].reshape(-1, width))]
        saved.append((stream, normed, projected, held, gated, middle, normed_ffn, pairs, hidden))
        if block == 0:
            (stream,), _, normed, _, _ = exchange(
                finish_block,
                in_units(hidden),
                down_matrix,
                False,
                [middle],
                [gain_row(1, 0)],
                [bf16],
                0,
                True,
                2,
            )
            outputs.append(stream)
            crossed_out = flip(stream, seq_count)
        else:
            last_sum = (in_units(hidden), down_matrix, middle)

    upstream = lax.dynamic_index_in_dim(cotangent[:, 0], x_index, 0, False)
    stream_grads = [None, None]
    small_grads = [None, None]
    matrix_grads = [None, None]

    def over_z(value):
        return lax.psum_scatter(value, "fsdp", scatter_dimension=0, tiled=True)

    def product(left, right):
        return by_rows(row_products(left, right))

    def small_rows(mixer_gain_part, ffn_gain_part, taps_placed):
        return jnp.concatenate(
            [
                mixer_gain_part.reshape(1, width),
                ffn_gain_part.reshape(1, width),
                taps_placed,
                jnp.zeros((3, width), f32),
            ],
            0,
        )

    def small_values():
        return jnp.stack(small_grads).reshape(2, 8, shards, shard_rows).transpose(0, 2, 1, 3)

    def to_section(value, block):
        over = [((1 - block) * seq_count + seq, block * seq_count + seq) for seq in range(seq_count)]
        return lax.ppermute(value, PLANE, over)

    inside = chip_bits()[1:] + [1]
    relative = [0, seq_count]
    for bits in inside:
        relative = relative + [unit | bits for unit in relative]

    def to_owners(value, block):
        held = [value, to_section(value, block)]
        for bits in inside:
            over = [
                (block * seq_count + seq, block * seq_count + (seq ^ bits)) for seq in range(seq_count)
            ]
            held = held + [lax.ppermute(unit, PLANE, over) for unit in held]
        return held

    mixer_sum = jnp.zeros((), f32)
    for block in (1, 0):
        in_matrix, out_matrix = mixer_matrices[block]
        pair_matrix, down_matrix = ffn_matrices[block]
        taps = taps_all[block]
        (stream, normed, projected, held, gated, middle, normed_ffn, pairs, hidden) = saved[block]
        down_product, grad_units, mixer_sum = tie(
            product(hidden, flat(grad_units)), grad_units, mixer_sum
        )
        if block == 0:
            matrix_grads[1] = (down_grad, pair_grad, mixer_sum)
        down_product = down_product.reshape(shards, -1, width)
        if kernels_fit():
            grad_pairs = ffn_backward(flat(grad_units), down_matrix, pairs, ffn_pad)
            if block == 0:
                grad_pairs, crossed = tie(grad_pairs, crossed)
        else:
            gate_value, up_value = pairs[:, :ffn_pad], pairs[:, ffn_pad:]
            grad_hidden = times_transposed(flat(grad_units), down_matrix)
            grad_hidden = jnp.pad(grad_hidden, ((0, 0), (0, ffn_pad - ffn_columns)))
            sigmoid_gate = jax.nn.sigmoid(gate_value)
            grad_gate = grad_hidden * up_value * sigmoid_gate * (1.0 + gate_value * (1.0 - sigmoid_gate))
            grad_up = grad_hidden * gate_value * sigmoid_gate
            grad_pairs = jnp.concatenate([grad_gate, grad_up], 1).astype(bf16)
        grad_pairs, pair_product = tie(grad_pairs, product(flat(normed_ffn), grad_pairs))
        pair_grad = over_z(pair_product)
        (grad_middle,), (ffn_gain_part,), mixer_grad, _, _ = exchange(
            finish_gradient,
            in_units(grad_pairs),
            pair_matrix,
            True,
            [upstream, middle],
            [gain_row(block, 1)],
            [f32],
            1,
            True,
            8 - 2 * block,
        )
        if kernels_fit():
            grad_projected, taps_part = mixer_backward(mixer_grad, out_matrix, projected, held, taps)
            grad_projected, taps_part = flat(grad_projected), taps_part[:3]
            mixer_product = mixer_products(flat(normed), grad_projected, gated, flat(mixer_grad))
        else:
            grad_gated = times_transposed(flat(mixer_grad), out_matrix).reshape(2 * half, rows, channels)
            b_gate = projected[:, :channels].reshape(2 * half, rows, channels)
            c_gate = projected[:, channels : 2 * channels].reshape(2 * half, rows, channels)
            x_value = projected[:, 2 * channels :].reshape(2 * half, rows, channels)
            conv_out = taps[0] * held[:, :-2] + taps[1] * held[:, 1:-1] + taps[2] * held[:, 2:]
            grad_cgate = grad_gated * conv_out
            grad_conv = grad_gated * c_gate
            later = pick_units(after_pick, grad_conv[:, :2])
            grad_extended = jnp.concatenate([grad_conv, later], 1)
            grad_input = (
                taps[0] * grad_extended[:, 2:]
                + taps[1] * grad_extended[:, 1:-1]
                + taps[2] * grad_extended[:, :-2]
            )
            taps_part = jnp.stack(
                [jnp.sum(grad_conv * held[:, tap : tap + rows], (0, 1)) for tap in range(3)], 0
            )
            grad_projected = flat(
                jnp.concatenate([grad_input * x_value, grad_cgate, grad_input * b_gate], 2).astype(bf16)
            )
            in_grad = row_products(flat(normed), grad_projected)
            out_grad = row_products(gated, flat(mixer_grad)).reshape(shards, part, count, channels)
            out_grad = out_grad.transpose(0, 2, 1, 3).reshape(width, channels)
            mixer_product = jnp.concatenate([in_grad, out_grad], 1)
        grad_projected, mixer_product, pair_grad = tie(
            grad_projected, mixer_product, pair_grad
        )
        if block == 1 or not kernels_fit():
            mixer_sum = over_z(mixer_product)
        own_mask = (jnp.arange(count) == share)[None, None, :, None]
        taps_placed = jnp.where(own_mask, taps_part.reshape(3, shards, 1, part), 0.0).reshape(3, width)
        if block == 0 and kernels_fit():
            break
        (grad_stream,), (mixer_gain_part,), sent, down_grad, result = exchange(
            finish_gradient,
            in_units(grad_projected),
            in_matrix,
            True,
            [grad_middle, stream],
            [gain_row(block, 0)],
            [f32],
            1,
            block == 1,
            9 - 2 * block,
            product=down_product,
            extra=last_sum if block else None,
        )
        if block == 1:
            outputs.append(result)
        stream_grads[block] = grad_stream
        small_grads[block] = small_rows(mixer_gain_part, ffn_gain_part, taps_placed)
        if block == 0:
            matrix_grads[0] = (down_grad, pair_grad, mixer_sum)
        if block == 1:
            upstream = sent[0, 0]
            grad_units = sent
            crossed = flip(result, seq_count)

    def in_order(index):
        second = to_owners(matrix_grads[1][index], 1)
        first = to_owners(matrix_grads[0][index], 0)
        ordered = jnp.zeros((count, *first[0].shape), bf16)
        for unit, one, two in zip(relative, first, second):
            ordered = lax.dynamic_update_index_in_dim(
                ordered, jnp.where(first_plane, one, two), share ^ unit, 0
            )
        return ordered

    def columns_of(value, blocks):
        piece = value.reshape(count, shard_rows, blocks, shards, -1)
        return piece.transpose(1, 2, 3, 0, 4).reshape(shard_rows, -1).astype(f32)

    if kernels_fit():
        small_grads[0] = small_rows(jnp.zeros((1, width), f32), ffn_gain_part, taps_placed)
        later = matrix_grads[1]
        stream_grads[0], crossed_last, smalls, pair_grad, down_grad, mixer_sum = last_exchange(
            in_units(grad_projected),
            in_matrix,
            grad_middle,
            stream,
            gain_row(0, 0),
            small_values(),
            upstream,
            mixer_product.reshape(shards, shard_rows, -1),
            down_product,
            later[2],
            later[0],
            (pair_grad, later[1]),
        )
        gate_grad, up_grad = place_columns(pair_grad, 2, hidden_width, ffn_pad, False)
        (in_grad,) = place_columns(mixer_sum, 3, width, channels, True)
    else:
        crossed_last = flip(jnp.stack([grad.astype(bf16) for grad in stream_grads]), seq_count)
        smalls = lax.psum(small_values(), ("section", "seq", "fsdp"))
        smalls = lax.dynamic_slice(
            smalls, (x_index, lax.axis_index("fsdp"), 0, 0), (1, 1, *smalls.shape[2:])
        )[0, 0]
        down_grad, pair_grad, mixer_sum = in_order(0), in_order(1), in_order(2)
        gate_grad = columns_of(pair_grad[..., :ffn_columns], 1)
        up_grad = columns_of(pair_grad[..., ffn_pad : ffn_pad + ffn_columns], 1)
        in_grad = columns_of(mixer_sum[..., :in_columns], 3)
    down_grad = down_grad.reshape(-1, width).astype(f32)
    out_grad = unpack_rows(mixer_sum[..., in_columns:]).astype(f32)

    def by_slot(values, crossed, dtype):
        kept = jnp.where(first_plane, values[0], values[1]).astype(dtype)
        other = jnp.where(first_plane, crossed[0], crossed[1]).astype(dtype)
        return jnp.stack(
            [jnp.where(first_plane, kept, other), jnp.where(first_plane, other, kept)], 0
        )

    return (
        by_slot(outputs, (crossed_out, crossed), bf16)[None, :, None],
        by_slot(stream_grads, (crossed_last[0], crossed_last[1]), f32)[None, :, None],
        in_grad[None],
        smalls[2:5].T[None],
        out_grad[None],
        gate_grad[None],
        up_grad[None],
        down_grad[None],
        smalls[0][None],
        smalls[1][None],
    )


def solution(mesh):
    placed = (
        P(None, "fsdp", "seq", None),
        P("section", "fsdp", None),
        P("section", "fsdp", None),
        P("section", "fsdp", None),
        P("section", "fsdp", None),
        P("section", "fsdp", None),
        P("section", "fsdp", None),
        P("section", "fsdp"),
        P("section", "fsdp"),
        P(None, "fsdp", "seq", None),
    )
    return jax.shard_map(
        body,
        mesh=mesh,
        in_specs=placed,
        out_specs=(
            P("section", None, "fsdp", "seq", None),
            P("section", None, "fsdp", "seq", None),
            P("section", "fsdp", None),
            P("section", "fsdp", None),
            P("section", "fsdp", None),
            P("section", "fsdp", None),
            P("section", "fsdp", None),
            P("section", "fsdp", None),
            P("section", "fsdp"),
            P("section", "fsdp"),
        ),
        check_vma=False,
    )
```

```python
import functools

import jax
import jax.numpy as jnp
from jax import lax
from jax.experimental import pallas as pl
from jax.experimental.layout import Layout, with_layout_constraint
from jax.experimental.pallas import tpu as pltpu
from jax.sharding import PartitionSpec as P

EPSILON = 1e-05
PLANE = ("section", "seq")
MESH = pl.DeviceIdType.MESH
VMEM_BYTES = 56 * 2**20
BYTES_PER_US = 3.5e6


def lasting(us):
    return pl.CostEstimate(flops=0, bytes_accessed=int(us * BYTES_PER_US), transcendentals=0)


def tie(*values):
    return lax.optimization_barrier(values)


def kernels_fit():
    return lax.axis_size("section") == 2 and lax.axis_size("seq") == 4


def peers():
    x, q = lax.axis_index("section"), lax.axis_index("seq")
    odd = q % 2
    y = (1 - q // 2) * 2 + odd
    core = {"section": x, "seq": (q // 2) * 2 + (1 - odd)}
    across = {"section": 1 - x, "seq": q}
    beside = {"section": x, "seq": y}
    corner = {"section": x + odd * (1 - 2 * x), "seq": y * (1 - odd) + q * odd}
    return odd, core, across, beside, corner


def greet(others):
    barrier = pltpu.get_barrier_semaphore()
    for other in others:
        pl.semaphore_signal(barrier, inc=1, device_id=other, device_id_type=MESH)
    pl.semaphore_wait(barrier, len(others))


def remote_copy(source, target, send, recv, device):
    return pltpu.make_async_remote_copy(
        src_ref=source,
        dst_ref=target,
        send_sem=send,
        recv_sem=recv,
        device_id=device,
        device_id_type=MESH,
    )


def other_shards():
    z, shards = lax.axis_index("fsdp"), lax.axis_size("fsdp")
    return [{"fsdp": (z + step) % shards} for step in range(1, shards)]


class ShardSum:
    def __init__(self, product_ref, from_z, send, recv, local):
        z, shards = lax.axis_index("fsdp"), lax.axis_size("fsdp")
        self.from_z = from_z
        self.moves = [
            remote_copy(
                product_ref.at[(z + step) % shards],
                from_z.at[step - 1],
                send.at[step - 1],
                recv.at[step - 1],
                {"fsdp": (z + step) % shards},
            )
            for step in range(1, shards)
        ]
        self.keep = pltpu.make_async_copy(product_ref.at[z], from_z.at[shards - 1], local)

    def start(self):
        for one in self.moves + [self.keep]:
            one.start()

    def total(self):
        for one in self.moves:
            one.wait_recv()
        self.keep.wait()
        value = self.from_z[0].astype(jnp.float32)
        for step in range(1, self.from_z.shape[0]):
            value = value + self.from_z[step].astype(jnp.float32)
        return value.astype(self.from_z.dtype)

    def end(self):
        for one in self.moves:
            one.wait_send()


def shard_sum_scratch(product):
    shards = product.shape[0]
    return [
        pltpu.VMEM(product.shape, product.dtype),
        pltpu.SemaphoreType.DMA((shards - 1,)),
        pltpu.SemaphoreType.DMA((shards - 1,)),
        pltpu.SemaphoreType.DMA,
    ]


def sum_stages(left_ref, matrix_ref, turned, finish_rows, scratch, chunks):
    left_held, matrix_held, partial_ref, from_core, to_corner, from_corner, to_side, from_side = scratch[:8]
    send, recv, left_load, matrix_load = scratch[8:]
    odd, core, across, beside, corner = peers()
    f32 = jnp.float32
    units, step = left_ref.shape[1], left_ref.shape[2] // chunks
    depth = left_ref.shape[3]

    def load(half, k):
        return pltpu.make_async_copy(
            left_ref.at[half, :, part(k)], left_held.at[half, :, part(k)], left_load.at[half, k]
        )

    columns = matrix_held.shape[1]
    source = matrix_ref if columns == matrix_ref.shape[1] else matrix_ref.at[:, pl.ds(0, columns)]
    load_matrix = pltpu.make_async_copy(source, matrix_held, matrix_load)

    def load_all():
        load_matrix.start()
        for k in range(chunks):
            for half in (1, 0):
                load(half, k).start()

    def multiply(half, k):
        load(half, k).wait()
        left = left_held[half, :, part(k)].reshape(units * step, depth)
        right = matrix_held[:, :depth] if turned else matrix_held[...]
        value = lax.dot_general(
            left, right, (((1,), (1 if turned else 0,)), ((), ())), preferred_element_type=f32
        )
        partial_ref[half, :, part(k)] = value.astype(jnp.bfloat16).reshape(units, step, value.shape[1])

    def part(k):
        return pl.ds(k * step, step)

    def copy(slot, k, source, target, device):
        return pltpu.make_async_remote_copy(
            src_ref=source,
            dst_ref=target,
            send_sem=send.at[slot, k],
            recv_sem=recv.at[slot, k],
            device_id=device,
            device_id_type=MESH,
        )

    def core_sum(k):
        return copy(0, k, partial_ref.at[1, :, part(k)], from_core.at[:, part(k)], core)

    def corner_sum(k):
        return copy(1, k, to_corner.at[part(k)], from_corner.at[part(k)], corner)

    def across_sum(k):
        return copy(2, k, to_side.at[0, part(k)], from_side.at[0, part(k)], across)

    def beside_sum(k):
        return copy(3, k, to_side.at[1, part(k)], from_side.at[1, part(k)], beside)

    def pair_sum(unit, k):
        return partial_ref[0, unit, part(k)].astype(f32) + from_core[unit, part(k)].astype(f32)

    def send_core(k):
        if k == 0:
            load_matrix.wait()
        multiply(1, k)
        core_sum(k).start()

    def sum_corner(k):
        multiply(0, k)
        core_sum(k).wait_recv()
        to_corner[part(k)] = pair_sum(3, k).astype(jnp.bfloat16)
        corner_sum(k).start()

    def sum_sides(k):
        corner_sum(k).wait_recv()
        extra = from_corner[part(k)].astype(f32)
        to_side[0, part(k)] = (pair_sum(1, k) + jnp.where(odd == 0, extra, 0.0)).astype(jnp.bfloat16)
        to_side[1, part(k)] = (pair_sum(2, k) + jnp.where(odd == 0, 0.0, extra)).astype(jnp.bfloat16)
        across_sum(k).start()
        beside_sum(k).start()

    def total_rows(k):
        across_sum(k).wait_recv()
        beside_sum(k).wait_recv()
        finish_rows(
            k,
            part(k),
            pair_sum(0, k) + from_side[0, part(k)].astype(f32) + from_side[1, part(k)].astype(f32),
        )

    stages = [send_core, sum_corner, sum_sides, total_rows]
    return stages, [core_sum, corner_sum, across_sum, beside_sum], load_all


def ticks_of(stages, chunks, lag):
    return chunks + lag * (len(stages) - 1)


def run_tick(stages, chunks, lag, tick):
    for place, stage in enumerate(stages):
        if 0 <= tick - lag * place < chunks:
            stage(tick - lag * place)


def run_stages(stages, chunks, lag):
    for tick in range(ticks_of(stages, chunks, lag)):
        run_tick(stages, chunks, lag, tick)


def sum_scratch(left, matrix, turned, chunks):
    bf16 = jnp.bfloat16
    _, units, rows, depth = left.shape
    width = matrix.shape[0] if turned else matrix.shape[1]
    columns = depth if turned and depth % 128 == 0 else matrix.shape[1]
    return [
        pltpu.VMEM(left.shape, bf16),
        pltpu.VMEM((matrix.shape[0], columns), bf16),
        pltpu.VMEM((2, units, rows, width), bf16),
        pltpu.VMEM((units, rows, width), bf16),
        pltpu.VMEM((rows, width), bf16),
        pltpu.VMEM((rows, width), bf16),
        pltpu.VMEM((2, rows, width), bf16),
        pltpu.VMEM((2, rows, width), bf16),
        pltpu.SemaphoreType.DMA((4, chunks)),
        pltpu.SemaphoreType.DMA((4, chunks)),
        pltpu.SemaphoreType.DMA((2, chunks)),
        pltpu.SemaphoreType.DMA,
    ]


SUM_REFS = 12


def exchange_kernel(
    finish, turned, row_ins, shared_ins, row_outs, sum_outs, gather, product, extra, chunks, *refs
):
    refs = list(refs)
    left_ref, matrix_ref = refs.pop(0), refs.pop(0)
    ins = [refs.pop(0) for _ in range(row_ins)]
    shared = [refs.pop(0) for _ in range(shared_ins)]
    product_ref = refs.pop(0) if product else None
    extra_left, extra_matrix, extra_middle = [refs.pop(0) for _ in range(3)] if extra else [None] * 3
    outs = [refs.pop(0) for _ in range(row_outs)]
    sums = [refs.pop(0) for _ in range(sum_outs)]
    product_out = refs.pop(0) if product else None
    extra_out = refs.pop(0) if extra else None
    spread_ref = refs.pop(0) if gather else None
    sum_refs, refs = refs[:SUM_REFS], refs[SUM_REFS:]
    (send, recv), refs = refs[:2], refs[2:]
    product_refs, extra_refs = (refs[:4], refs[4:]) if product else ([], refs)
    odd, core, across, beside, corner = peers()
    f32 = jnp.float32
    step = left_ref.shape[2] // chunks

    def part(k):
        return pl.ds(k * step, step)

    def copy(slot, k, source, target, device):
        return pltpu.make_async_remote_copy(
            src_ref=source,
            dst_ref=target,
            send_sem=send.at[slot, k],
            recv_sem=recv.at[slot, k],
            device_id=device,
            device_id_type=MESH,
        )

    def across_out(k):
        return copy(0, k, spread_ref.at[0, 0, part(k)], spread_ref.at[0, 1, part(k)], across)

    def beside_out(k):
        return copy(1, k, spread_ref.at[0, 0, part(k)], spread_ref.at[0, 2, part(k)], beside)

    def corner_out(k):
        return copy(2, k, spread_ref.at[0, 1 + odd, part(k)], spread_ref.at[0, 3, part(k)], corner)

    def core_out(k):
        return copy(3, k, spread_ref.at[0, :, part(k)], spread_ref.at[1, :, part(k)], core)

    def finish_rows(k, rows, total):
        values, added, sent = finish(
            total, *[ref[rows].astype(f32) for ref in ins], *[ref[...] for ref in shared]
        )
        for ref, value in zip(outs, values):
            ref[rows] = value.astype(ref.dtype)
        for ref, value in zip(sums, added):
            ref[...] = value if k == 0 else ref[...] + value
        if gather:
            spread_ref[0, 0, rows] = sent
            across_out(k).start()
            beside_out(k).start()

    def pass_corner(k):
        across_out(k).wait_recv()
        beside_out(k).wait_recv()
        corner_out(k).start()

    def pass_core(k):
        corner_out(k).wait_recv()
        core_out(k).start()

    def arrive(k):
        core_out(k).wait_recv()

    stages, copies, load_all = sum_stages(left_ref, matrix_ref, turned, finish_rows, sum_refs, chunks)
    load_all()
    if gather:
        stages = stages + [pass_corner, pass_core, arrive]
        copies = copies + [across_out, beside_out, corner_out, core_out]
    if extra:

        def extra_rows(k, rows, total):
            extra_out[rows] = (extra_middle[rows] + total).astype(extra_out.dtype)

        later, more, load_more = sum_stages(
            extra_left, extra_matrix, False, extra_rows, extra_refs, chunks
        )
        load_more()
        stages = stages[:1] + [lambda k, a=a, b=b: (a(k), b(k)) for a, b in zip(stages[1:5], later)] + stages[5:]
        copies = copies + more
    greet([core, across, beside] + (other_shards() if product else []))
    if product:
        shard_sum = ShardSum(product_ref, *product_refs)
        shard_sum.start()
    run_stages(stages, chunks, 1 if left_ref.shape[3] > 1024 else 2)
    if product:
        product_out[...] = shard_sum.total()
        shard_sum.end()
    for k in range(chunks):
        for one in copies:
            one(k).wait_send()


def exchange(
    finish,
    left,
    matrix,
    turned,
    row_ins,
    shared_ins,
    row_outs,
    sum_outs,
    gather,
    number,
    product=None,
    extra=None,
    chunks=4,
):
    _, units, rows, _ = left.shape
    width = matrix.shape[0] if turned else matrix.shape[1]
    if not kernels_fit():
        return exchange_plainly(
            finish, left, matrix, turned, row_ins, shared_ins, row_outs, gather, product, extra
        )
    bf16 = jnp.bfloat16
    shapes = [jax.ShapeDtypeStruct((rows, width), dtype) for dtype in row_outs]
    shapes += [jax.ShapeDtypeStruct((1, width), jnp.float32)] * sum_outs
    shapes += [] if product is None else [jax.ShapeDtypeStruct(product.shape[1:], product.dtype)]
    shapes += [] if extra is None else [jax.ShapeDtypeStruct((rows, width), bf16)]
    shapes += [jax.ShapeDtypeStruct((2, units, rows, width), bf16)] * gather
    more = ([] if product is None else [product]) + list(extra or ())
    place, anywhere = pl.BlockSpec(memory_space=pltpu.VMEM), pl.BlockSpec(memory_space=pl.ANY)
    result = pl.pallas_call(
        functools.partial(
            exchange_kernel,
            finish,
            turned,
            len(row_ins),
            len(shared_ins),
            len(row_outs),
            sum_outs,
            gather,
            product is not None,
            extra is not None,
            chunks,
        ),
        out_shape=shapes,
        in_specs=[anywhere] * 2
        + [place] * (len(row_ins) + len(shared_ins))
        + ([] if product is None else [anywhere])
        + ([] if extra is None else [anywhere, anywhere, place]),
        out_specs=[place] * len(shapes),
        scratch_shapes=sum_scratch(left, matrix, turned, chunks)
        + [pltpu.SemaphoreType.DMA((4, chunks))] * 2
        + ([] if product is None else shard_sum_scratch(product))
        + ([] if extra is None else sum_scratch(extra[0], extra[1], False, chunks)),
        compiler_params=pltpu.CompilerParams(
            collective_id=number, has_side_effects=True, vmem_limit_bytes=VMEM_BYTES
        ),
        cost_estimate=lasting(66 if gather else 38),
        name=("exchange_%d" % number),
    )(left, matrix, *row_ins, *shared_ins, *more)
    result = list(result)
    rows_done = [result.pop(0) for _ in row_outs]
    sums = [result.pop(0) for _ in range(sum_outs)]
    product = None if product is None else result.pop(0)
    extra = None if extra is None else result.pop(0)
    return rows_done, sums, (result.pop(0) if gather else None), product, extra


def plane_total(left, matrix, turned):
    multiply = times_transposed if turned else times
    matrix = matrix[:, : left.shape[3]] if turned else matrix
    near, far = [multiply(half.reshape(-1, half.shape[2]), matrix).astype(jnp.bfloat16) for half in left]
    total = near.astype(jnp.float32) + flip(far, 1).astype(jnp.float32)
    return collect(total, (lax.axis_index("seq") % 2) == 1)


def exchange_plainly(finish, left, matrix, turned, row_ins, shared_ins, row_outs, gather, product, extra):
    total = plane_total(left, matrix, turned)
    rows, sums, sent = finish(total, *[value.astype(jnp.float32) for value in row_ins], *shared_ins)
    rows = [value.astype(dtype) for value, dtype in zip(rows, row_outs)]
    if product is not None:
        product = lax.psum_scatter(
            product.reshape(-1, product.shape[2]), "fsdp", scatter_dimension=0, tiled=True
        )
    if extra is not None:
        extra = (plane_total(extra[0], extra[1], False) + extra[2]).astype(jnp.bfloat16)
    if gather:
        odd = (lax.axis_index("seq") % 2) == 1
        sent = jnp.stack(spread(sent, odd)).reshape(*left.shape[:3], -1)
    return rows, sums, sent, product, extra


def finish_middle(total, stream, gain):
    middle = stream + total
    return [middle], [], (middle * rms_scale(middle) * gain).astype(jnp.bfloat16)


def finish_block(total, middle, gain):
    result = (middle + total).astype(jnp.bfloat16)
    stream = result.astype(jnp.float32)
    return [result], [], (stream * rms_scale(stream) * gain).astype(jnp.bfloat16)


def finish_gradient(total, upstream, stream, gain):
    scale = rms_scale(stream)
    weighted = gain * total
    grad = (
        upstream
        + scale * weighted
        - stream * scale**3 * jnp.mean(weighted * stream, -1, keepdims=True)
    )
    added = jnp.sum(total * stream * scale, 0, keepdims=True)
    return [grad], [added], grad.astype(jnp.bfloat16)


LAST_CHUNKS = 4
OWNER_CHUNKS = (6, 1, 1)


def last_kernel(
    left_ref,
    matrix_ref,
    upstream_ref,
    stream_ref,
    gain_ref,
    smalls_ref,
    later_ref,
    product_ref,
    down_product_ref,
    mixer_ref,
    down_ref,
    pair0_ref,
    pair1_ref,
    grad_ref,
    crossed_ref,
    smalls_out,
    pair_out,
    down_out,
    mixer_out,
    *scratch,
):
    sum_refs, scratch = scratch[:SUM_REFS], scratch[SUM_REFS:]
    pair_both, down_both, mixer_both, grad_low, gain_sum = scratch[:5]
    small_sum, small_sent, small_side, small_z = scratch[5:9]
    local, own_send, own_recv, small_send, small_recv, cross_send, cross_recv = scratch[9:16]
    mixer_sum = ShardSum(product_ref, *scratch[16:20])
    down_sum = ShardSum(down_product_ref, *scratch[20:])
    x, q, z = lax.axis_index("section"), lax.axis_index("seq"), lax.axis_index("fsdp")
    shards = lax.axis_size("fsdp")
    _, core, across, beside, _ = peers()
    f32, bf16 = jnp.float32, jnp.bfloat16
    others = other_shards()
    share = x * 4 + q
    share_across = (1 - x) * 4 + q
    beside_q = (1 - q // 2) * 2 + q % 2
    share_beside = x * 4 + beside_q
    share_corner = (1 - x) * 4 + beside_q

    def remote(source, target, send, recv, device):
        return pltpu.make_async_remote_copy(
            src_ref=source,
            dst_ref=target,
            send_sem=send,
            recv_sem=recv,
            device_id=device,
            device_id_type=MESH,
        )

    class Owners:
        def __init__(self, place, both, out):
            self.place, self.both, self.out = place, both, out
            self.step = both.shape[1] // OWNER_CHUNKS[place]
            self.chunks = range(OWNER_CHUNKS[place])

        def move(self, slot, k, source, target, device):
            part = pl.ds(k * self.step, self.step)
            place = self.place
            return remote(
                source.at[part],
                self.out.at[target, part],
                own_send.at[place, slot, k],
                own_recv.at[place, slot, k],
                device,
            )

        def cross(self, k):
            return self.move(0, k, self.both.at[1 - x], share, across)

        def side(self, k):
            return self.move(1, k, self.both.at[x], share, beside)

        def near(self, k):
            return self.move(2, k, self.both.at[x], share, core)

        def side_across(self, k):
            return self.move(3, k, self.out.at[share_across], share_across, beside)

        def near_across(self, k):
            return self.move(4, k, self.out.at[share_across], share_across, core)

        def near_beside(self, k):
            return self.move(5, k, self.out.at[share_beside], share_beside, core)

        def near_corner(self, k):
            return self.move(6, k, self.out.at[share_corner], share_corner, core)

        def keep(self):
            return pltpu.make_async_copy(self.both.at[x], self.out.at[share], local.at[4 + self.place])

        def first(self, k):
            self.cross(k).start()
            self.side(k).start()
            self.near(k).start()

        def second(self, k):
            self.cross(k).wait_recv()
            self.side_across(k).start()
            self.near_across(k).start()

        def third(self, k):
            self.side(k).wait_recv()
            self.near_beside(k).start()

        def fourth(self, k):
            self.side_across(k).wait_recv()
            self.near_corner(k).start()

        def end(self):
            for k in self.chunks:
                for one in (self.near, self.near_across, self.near_beside, self.near_corner):
                    one(k).wait_recv()
                for one in (
                    self.cross,
                    self.side,
                    self.near,
                    self.side_across,
                    self.near_across,
                    self.near_beside,
                    self.near_corner,
                ):
                    one(k).wait_send()
            self.keep().wait()

    pair = Owners(0, pair_both, pair_out)
    down = Owners(1, down_both, down_out)
    mixer = Owners(2, mixer_both, mixer_out)

    def finish_rows(k, rows, total):
        (grad,), (added,), sent = finish_gradient(
            total, upstream_ref[rows].astype(f32), stream_ref[rows].astype(f32), gain_ref[...]
        )
        grad_ref[rows] = grad
        grad_low[rows] = sent
        gain_sum[...] = added if k == 0 else gain_sum[...] + added

    stages, copies, load_all = sum_stages(left_ref, matrix_ref, True, finish_rows, sum_refs, LAST_CHUNKS)
    load_all()
    loads = [
        pltpu.make_async_copy(pair0_ref, pair_both.at[0], local.at[0]),
        pltpu.make_async_copy(pair1_ref, pair_both.at[1], local.at[1]),
        pltpu.make_async_copy(down_ref, down_both.at[1], local.at[2]),
        pltpu.make_async_copy(mixer_ref, mixer_both.at[1], local.at[3]),
    ]
    for one in loads:
        one.start()
    greet([core, across, beside] + others)
    mixer_sum.start()
    later = remote(later_ref, crossed_ref.at[1], cross_send.at[1], cross_recv.at[1], across)
    later.start()
    for one in loads[:2]:
        one.wait()
    pair.keep().start()
    for tick in range(ticks_of(stages, LAST_CHUNKS, 2)):
        run_tick(stages, LAST_CHUNKS, 2, tick)
        if tick in pair.chunks:
            pair.first(tick)
        if tick == 1:
            down_sum.start()

    small_rows = smalls_ref.shape[3]
    small_sum[...] = smalls_ref[...]
    for shard in range(shards):
        small_sum[0, shard, 0:1] += gain_sum[:, shard * small_rows : (shard + 1) * small_rows]

    def small_move(step, device):
        return remote(small_sent.at[step], small_side.at[step], small_send.at[step], small_recv.at[step], device)

    for step, device in enumerate((core, across, beside)):
        small_sent[step] = small_sum[...]
        small_move(step, device).start()
        pair.second(step)
        small_move(step, device).wait()
        small_sum[...] += small_side[step]
    small_moves = [
        remote(
            small_sum.at[x, (z + step + 1) % shards],
            small_z.at[step],
            small_send.at[3 + step],
            small_recv.at[3 + step],
            device,
        )
        for step, device in enumerate(others)
    ]
    for one in small_moves:
        one.start()

    mixer_both[0] = mixer_sum.total()
    loads[3].wait()
    mixer.keep().start()
    mixer.first(0)
    for k in pair.chunks[3:]:
        pair.second(k)
    mixer.second(0)
    down_both[0] = down_sum.total()
    loads[2].wait()
    down.keep().start()
    down.first(0)
    cross = remote(grad_low, crossed_ref.at[0], cross_send.at[0], cross_recv.at[0], across)
    cross.start()
    for k in pair.chunks:
        pair.third(k)
    mixer.third(0)
    down.second(0)
    for k in pair.chunks:
        pair.fourth(k)
    mixer.fourth(0)
    down.third(0)
    down.fourth(0)
    small_total = small_sum[x, z]
    for step, one in enumerate(small_moves):
        one.wait()
        small_total = small_total + small_z[step]
    smalls_out[...] = small_total
    for owners in (pair, down, mixer):
        owners.end()
    cross.wait()
    later.wait()
    mixer_sum.end()
    down_sum.end()
    for k in range(LAST_CHUNKS):
        for one in copies:
            one(k).wait_send()


def last_exchange(left, matrix, upstream, stream, gain, smalls, later, product, down_product, mixer, down, pairs):
    _, units, rows, _ = left.shape
    width = matrix.shape[0]
    shards, shard_rows, mixer_columns = product.shape
    bf16, f32 = jnp.bfloat16, jnp.float32
    count = 2 * units
    vmem = pl.BlockSpec(memory_space=pltpu.VMEM)
    anywhere = pl.BlockSpec(memory_space=pl.ANY)
    return pl.pallas_call(
        last_kernel,
        out_shape=[
            jax.ShapeDtypeStruct((rows, width), f32),
            jax.ShapeDtypeStruct((2, rows, width), bf16),
            jax.ShapeDtypeStruct(smalls.shape[2:], f32),
            jax.ShapeDtypeStruct((count, *pairs[0].shape), bf16),
            jax.ShapeDtypeStruct((count, *down.shape), bf16),
            jax.ShapeDtypeStruct((count, shard_rows, mixer_columns), bf16),
        ],
        in_specs=[anywhere] * 2 + [vmem] * 5 + [anywhere] * 6,
        out_specs=[vmem] * 3 + [anywhere] * 3,
        scratch_shapes=sum_scratch(left, matrix, True, LAST_CHUNKS)
        + [
            pltpu.VMEM((2, *pairs[0].shape), bf16),
            pltpu.VMEM((2, *down.shape), bf16),
            pltpu.VMEM((2, shard_rows, mixer_columns), bf16),
            pltpu.VMEM((rows, width), bf16),
            pltpu.VMEM((1, width), f32),
            pltpu.VMEM(smalls.shape, f32),
            pltpu.VMEM((3, *smalls.shape), f32),
            pltpu.VMEM((3, *smalls.shape), f32),
            pltpu.VMEM((shards - 1, *smalls.shape[2:]), f32),
            pltpu.SemaphoreType.DMA((7,)),
            pltpu.SemaphoreType.DMA((3, 7, max(OWNER_CHUNKS))),
            pltpu.SemaphoreType.DMA((3, 7, max(OWNER_CHUNKS))),
            pltpu.SemaphoreType.DMA((2 + shards,)),
            pltpu.SemaphoreType.DMA((2 + shards,)),
            pltpu.SemaphoreType.DMA((2,)),
            pltpu.SemaphoreType.DMA((2,)),
        ]
        + shard_sum_scratch(product)
        + shard_sum_scratch(down_product),
        compiler_params=pltpu.CompilerParams(
            collective_id=20, has_side_effects=True, vmem_limit_bytes=VMEM_BYTES
        ),
        cost_estimate=lasting(130),
        name="last_exchange",
    )(left, matrix, upstream, stream, gain, smalls, later, product, down_product, mixer, down, *pairs)


def place_kernel(blocks, width, stride, stack_ref, *outs):
    shards = lax.axis_size("fsdp")
    count = stack_ref.shape[0]
    part = width // shards // count
    for block in range(blocks):
        pieces = []
        for shard in range(shards):
            start = block * stride + shard * part
            pieces += [stack_ref[share, :, start : start + part] for share in range(count)]
        value = jnp.concatenate(pieces, 1).astype(jnp.float32)
        if len(outs) == 1:
            outs[0][:, block * width : (block + 1) * width] = value
        else:
            outs[block][...] = value


def place_rows_kernel(stack_ref, out_ref):
    channels = stack_ref.shape[2]
    blocks = out_ref.shape[1] // channels
    part = stack_ref.shape[1] // blocks
    for share in range(stack_ref.shape[0]):
        pieces = [stack_ref[share, block * part : (block + 1) * part] for block in range(blocks)]
        out_ref[share * part : (share + 1) * part] = jnp.concatenate(pieces, 1).astype(jnp.float32)


def place_rows(stack, width):
    count, rows, _ = stack.shape
    (value,) = local_call(
        place_rows_kernel, [((rows, width), jnp.float32)], [], 5, "place_rows", stack
    )
    return value


def place_columns(stack, blocks, width, stride, together):
    count, rows, columns = stack.shape
    step = 48
    widths = [blocks * width] if together else [width] * blocks
    return pl.pallas_call(
        functools.partial(place_kernel, blocks, width, stride),
        grid=(rows // step,),
        out_shape=[jax.ShapeDtypeStruct((rows, each), jnp.float32) for each in widths],
        in_specs=[pl.BlockSpec((count, step, columns), lambda i: (0, i, 0))],
        out_specs=[pl.BlockSpec((step, each), lambda i: (i, 0)) for each in widths],
        compiler_params=pltpu.CompilerParams(vmem_limit_bytes=VMEM_BYTES),
        cost_estimate=lasting(14),
        name="place_columns",
    )(stack)


def local_call(kernel, outs, scratch, us, name, *operands, far=()):
    place = pl.BlockSpec(memory_space=pltpu.VMEM)
    places = [pl.BlockSpec(memory_space=pl.ANY) if i in far else place for i in range(len(operands))]
    return pl.pallas_call(
        kernel,
        out_shape=[jax.ShapeDtypeStruct(shape, dtype) for shape, dtype in outs],
        in_specs=places,
        out_specs=[place] * len(outs),
        scratch_shapes=scratch,
        compiler_params=pltpu.CompilerParams(vmem_limit_bytes=VMEM_BYTES),
        cost_estimate=lasting(us),
        name=name,
    )(*operands)


def unit_place(difference):
    return difference // 4 + (difference // 2 % 2) * 2 + (difference % 2) * 4


def unit_bits(place):
    return (place % 2) * 4 + (place // 2 % 2) * 2 + place // 4


def either(left, right):
    total = 0
    for bit in (1, 2, 4):
        one, two = left // bit % 2, right // bit % 2
        total = total + bit * (one + two - 2 * one * two)
    return total


def neighbour(place, step):
    share = lax.axis_index("section") * 4 + lax.axis_index("seq")
    device = either(share, unit_bits(place))
    seq = device % 4 + step
    inside = jnp.where((seq >= 0) & (seq < 4), 1.0, 0.0)
    seq = (seq + 4) % 4
    return unit_place(either(share, device // 4 * 4 + seq)), inside


def conv_parts(held_ref, place):
    f32 = jnp.float32
    before, inside = neighbour(place, -1)
    here = held_ref[place]
    rows = here.shape[0]
    edge = held_ref[before, rows - 2 : rows] * inside
    whole = jnp.concatenate([edge.astype(f32), here], 0)
    return whole[:rows], whole[1 : rows + 1], here


def load_units(source, target, sems):
    def load(place):
        return pltpu.make_async_copy(source.at[place], target.at[place], sems.at[place])

    for place in range(8):
        load(place).start()
    return lambda place: load(place).wait()


def mixer_forward_kernel(
    channels, normed_far, matrix_ref, taps_ref, projected_ref, held_ref, gated_ref, normed_ref, sems
):
    f32, bf16 = jnp.float32, jnp.bfloat16
    wait_unit = load_units(normed_far, normed_ref, sems)

    def project(place, carry):
        wait_unit(place)
        value = jnp.dot(
            normed_ref[place], matrix_ref[:, : 3 * channels], preferred_element_type=f32
        )
        projected_ref[place] = value
        held_ref[place] = (value[:, :channels] * value[:, 2 * channels :]).astype(bf16).astype(f32)
        return carry

    lax.fori_loop(0, 8, project, 0)

    def convolve(place, carry):
        first, second, third = conv_parts(held_ref, place)
        value = taps_ref[0:1] * first + taps_ref[1:2] * second + taps_ref[2:3] * third
        gated_ref[place] = (projected_ref[place, :, channels : 2 * channels] * value).astype(bf16)
        return carry

    lax.fori_loop(0, 8, convolve, 0)


def mixer_forward(normed, matrix, taps):
    rows = normed.shape[2]
    channels = taps.shape[1]
    f32, bf16 = jnp.float32, jnp.bfloat16
    return local_call(
        functools.partial(mixer_forward_kernel, channels),
        [((8, rows, 3 * channels), f32), ((8, rows, channels), f32), ((8, rows, channels), bf16)],
        [pltpu.VMEM((8, *normed.shape[2:]), bf16), pltpu.SemaphoreType.DMA((8,))],
        10,
        "mixer_forward",
        normed.reshape(8, rows, -1),
        matrix,
        taps,
        far=(0,),
    )


def mixer_backward_kernel(
    channels,
    grad_far,
    matrix_ref,
    projected_far,
    held_ref,
    taps_ref,
    out_ref,
    taps_out,
    conv_grad,
    gate_grad,
    grad_ref,
    projected_ref,
    grad_sems,
    projected_sems,
):
    f32, bf16 = jnp.float32, jnp.bfloat16
    wait_grad = load_units(grad_far, grad_ref, grad_sems)
    wait_projected = load_units(projected_far, projected_ref, projected_sems)

    def to_gates(place, carry):
        wait_grad(place)
        wait_projected(place)
        grad = lax.dot_general(
            grad_ref[place], matrix_ref[...], (((1,), (1,)), ((), ())), preferred_element_type=f32
        )
        first, second, third = conv_parts(held_ref, place)
        value = taps_ref[0:1] * first + taps_ref[1:2] * second + taps_ref[2:3] * third
        back = grad * projected_ref[place, :, channels : 2 * channels]
        gate_grad[place] = grad * value
        conv_grad[place] = back
        added = [jnp.sum(back * shifted, 0, keepdims=True) for shifted in (first, second, third)]
        return carry + jnp.concatenate(added + [jnp.zeros((5, channels), f32)], 0)

    taps_out[...] = lax.fori_loop(0, 8, to_gates, jnp.zeros((8, channels), f32))

    def to_inputs(place, carry):
        after, inside = neighbour(place, 1)
        here = conv_grad[place]
        rows = here.shape[0]
        whole = jnp.concatenate([here, conv_grad[after, 0:2] * inside], 0)
        grad = (
            taps_ref[0:1] * whole[2:] + taps_ref[1:2] * whole[1 : rows + 1] + taps_ref[2:3] * here
        )
        out_ref[place] = jnp.concatenate(
            [
                grad * projected_ref[place, :, 2 * channels :],
                gate_grad[place],
                grad * projected_ref[place, :, :channels],
            ],
            1,
        ).astype(bf16)
        return carry

    lax.fori_loop(0, 8, to_inputs, 0)


def mixer_backward(grads, matrix, projected, held, taps):
    rows = grads.shape[2]
    channels = taps.shape[1]
    f32, bf16 = jnp.float32, jnp.bfloat16
    return local_call(
        functools.partial(mixer_backward_kernel, channels),
        [((8, rows, 3 * channels), bf16), ((8, channels), f32)],
        [
            pltpu.VMEM((8, rows, channels), f32),
            pltpu.VMEM((8, rows, channels), f32),
            pltpu.VMEM((8, *grads.shape[2:]), bf16),
            pltpu.VMEM(projected.shape, f32),
            pltpu.SemaphoreType.DMA((8,)),
            pltpu.SemaphoreType.DMA((8,)),
        ],
        12,
        "mixer_backward",
        grads.reshape(8, rows, -1),
        matrix,
        projected,
        held,
        taps,
        far=(0, 2),
    )


def ffn_forward_kernel(pad, normed_ref, matrix_ref, pairs_ref, hidden_ref):
    pairs = jnp.dot(normed_ref[...], matrix_ref[:, : 2 * pad], preferred_element_type=jnp.float32)
    pairs_ref[...] = pairs
    gate, up = pairs[:, :pad], pairs[:, pad:]
    hidden = gate * jax.nn.sigmoid(gate) * up
    hidden_ref[...] = hidden[:, : hidden_ref.shape[1]].astype(jnp.bfloat16)


def ffn_forward(normed, matrix, pad, columns):
    count, width = normed.shape
    step = 256
    return pl.pallas_call(
        functools.partial(ffn_forward_kernel, pad),
        grid=(count // step,),
        out_shape=[
            jax.ShapeDtypeStruct((count, 2 * pad), jnp.float32),
            jax.ShapeDtypeStruct((count, columns), jnp.bfloat16),
        ],
        in_specs=[
            pl.BlockSpec((step, width), lambda i: (i, 0)),
            pl.BlockSpec(matrix.shape, lambda i: (0, 0)),
        ],
        out_specs=[
            pl.BlockSpec((step, 2 * pad), lambda i: (i, 0)),
            pl.BlockSpec((step, columns), lambda i: (i, 0)),
        ],
        compiler_params=pltpu.CompilerParams(vmem_limit_bytes=VMEM_BYTES),
        cost_estimate=lasting(16),
        name="ffn_forward",
    )(normed, matrix)


def ffn_backward_kernel(pad, grad_ref, matrix_ref, pairs_ref, out_ref):
    grad = lax.dot_general(
        grad_ref[...], matrix_ref[...], (((1,), (1,)), ((), ())), preferred_element_type=jnp.float32
    )
    extra = pad - grad.shape[1]
    if extra:
        grad = jnp.concatenate([grad, jnp.zeros((grad.shape[0], extra), jnp.float32)], 1)
    gate, up = pairs_ref[:, :pad], pairs_ref[:, pad:]
    sigmoid = jax.nn.sigmoid(gate)
    out_ref[:, :pad] = (grad * up * sigmoid * (1.0 + gate * (1.0 - sigmoid))).astype(jnp.bfloat16)
    out_ref[:, pad:] = (grad * gate * sigmoid).astype(jnp.bfloat16)


def ffn_backward(grads, matrix, pairs, pad):
    count, width = grads.shape
    step = 256
    return pl.pallas_call(
        functools.partial(ffn_backward_kernel, pad),
        grid=(count // step,),
        out_shape=jax.ShapeDtypeStruct((count, 2 * pad), jnp.bfloat16),
        in_specs=[
            pl.BlockSpec((step, width), lambda i: (i, 0)),
            pl.BlockSpec(matrix.shape, lambda i: (0, 0)),
            pl.BlockSpec((step, 2 * pad), lambda i: (i, 0)),
        ],
        out_specs=pl.BlockSpec((step, 2 * pad), lambda i: (i, 0)),
        compiler_params=pltpu.CompilerParams(vmem_limit_bytes=VMEM_BYTES),
        cost_estimate=lasting(16),
        name="ffn_backward",
    )(grads, matrix, pairs)


def mixer_product_kernel(
    shards, normed_far, projected_ref, gated_ref, grad_far, out_ref, normed_ref, grad_ref, sems
):
    f32, bf16 = jnp.float32, jnp.bfloat16
    blocks = normed_ref.shape[0]
    step = normed_ref.shape[2]
    loads = [
        pltpu.make_async_copy(normed_far.at[:, pl.ds(i * step, step)], normed_ref.at[i], sems.at[i])
        for i in range(blocks)
    ]
    loads.append(pltpu.make_async_copy(grad_far, grad_ref, sems.at[blocks]))
    for one in loads:
        one.start()
    turned = (((0,), (0,)), ((), ()))
    columns = projected_ref.shape[1]
    width, channels = grad_ref.shape[1], gated_ref.shape[1]
    for i in range(blocks):
        loads[i].wait()
        out_ref[i * step : (i + 1) * step, :columns] = lax.dot_general(
            normed_ref[i], projected_ref[...], turned, preferred_element_type=f32
        ).astype(bf16)
    loads[blocks].wait()
    value = lax.dot_general(gated_ref[...], grad_ref[...], turned, preferred_element_type=f32)
    part = channels // shards
    pieces = width // channels
    for shard in range(shards):
        for block in range(pieces):
            row = (shard * pieces + block) * part
            out_ref[row : row + part, columns:] = value[
                shard * part : (shard + 1) * part, block * channels : (block + 1) * channels
            ].astype(bf16)


def mixer_products(normed, projected_grad, gated, grad):
    width, columns, channels = normed.shape[1], projected_grad.shape[1], gated.shape[1]
    shards = lax.axis_size("fsdp")
    blocks = width // 256
    (value,) = local_call(
        functools.partial(mixer_product_kernel, shards),
        [((width, columns + channels), jnp.bfloat16)],
        [
            pltpu.VMEM((blocks, normed.shape[0], width // blocks), jnp.bfloat16),
            pltpu.VMEM(grad.shape, jnp.bfloat16),
            pltpu.SemaphoreType.DMA((blocks + 1,)),
        ],
        14,
        "mixer_products",
        normed,
        projected_grad,
        gated,
        grad,
        far=(0, 3),
    )
    return value


def flip(value, bits):
    count = lax.axis_size("section") * lax.axis_size("seq")
    return lax.ppermute(value, PLANE, [(source, source ^ bits) for source in range(count)])


def flip_by_core(value, even_bits, odd_bits):
    count = lax.axis_size("section") * lax.axis_size("seq")
    pairs = [(source, source ^ (odd_bits if source & 1 else even_bits)) for source in range(count)]
    return lax.ppermute(value, PLANE, pairs)


def chip_bits():
    bits = [lax.axis_size("seq")]
    step = lax.axis_size("seq") // 2
    while step > 1:
        bits.append(step)
        step //= 2
    return bits


def half_units():
    units = [0]
    for bits in chip_bits():
        units = units + [unit | bits for unit in units]
    return units


def spread_chips(own, odd):
    bits = chip_bits()
    if len(bits) == 2:
        first = flip(own, bits[0])
        second = flip(own, bits[1])
        third = flip_by_core(jnp.where(odd, second, first), bits[1], bits[0])
        return jnp.concatenate([own, first, second, third], 0)
    held = own
    for step in bits:
        held = jnp.concatenate([held, flip(held, step)], 0)
    return held


def spread(own, odd):
    near = spread_chips(own, odd)
    return near, flip(near, 1)


def collect(near, odd):
    bits = chip_bits()
    if len(bits) == 2:
        rows = near.shape[0] // 4
        held = near
        third = flip_by_core(held[3 * rows :].astype(jnp.bfloat16), bits[1], bits[0]).astype(jnp.float32)
        first = held[rows : 2 * rows] + jnp.where(odd, 0.0, third)
        second = held[2 * rows : 3 * rows] + jnp.where(odd, third, 0.0)
        first = flip(first.astype(jnp.bfloat16), bits[0]).astype(jnp.float32)
        second = flip(second.astype(jnp.bfloat16), bits[1]).astype(jnp.float32)
        return held[:rows] + first + second
    held = near
    for step in reversed(bits):
        rows = held.shape[0] // 2
        held = held[:rows] + flip(held[rows:].astype(jnp.bfloat16), step).astype(jnp.float32)
    return held


def rms_scale(stream):
    return lax.rsqrt(jnp.mean(stream * stream, -1, keepdims=True) + EPSILON)


def times(left, matrix):
    return jnp.dot(left, matrix, preferred_element_type=jnp.float32)


def times_transposed(left, matrix):
    return lax.dot_general(
        left, matrix, (((1,), (1,)), ((), ())), preferred_element_type=jnp.float32
    )


def by_rows(value):
    return with_layout_constraint(value, Layout(major_to_minor=tuple(range(value.ndim))))


def row_products(left, right):
    return lax.dot_general(
        left, right, (((0,), (0,)), ((), ())), preferred_element_type=jnp.float32
    ).astype(jnp.bfloat16)


def normed_with(stream, gain):
    return (stream * rms_scale(stream) * gain).astype(jnp.bfloat16)


def pick_columns(matrix, share, width, count):
    shards = lax.axis_size("fsdp")
    part = width // shards // count
    return jnp.concatenate(
        [
            lax.dynamic_slice(
                matrix, (0, start + shard * (width // shards) + share * part), (matrix.shape[0], part)
            )
            for start in range(0, matrix.shape[1], width)
            for shard in range(shards)
        ],
        1,
    )


def pick_rows(matrix, share, count):
    part = matrix.shape[0] // count
    return lax.dynamic_slice(matrix, (share * part, 0), (part, matrix.shape[1]))


SPREAD_CHUNKS = 4
SPREAD_MOVES = 3 * SPREAD_CHUNKS + 1
FFN_CHUNKS = 2 * SPREAD_CHUNKS


class Spread:
    def __init__(self, rows_of, out_ref, send, recv):
        self.rows_of, self.out_ref, self.send, self.recv = rows_of, out_ref, send, recv
        _, self.core, _, self.beside, _ = peers()
        step = out_ref.shape[2] // SPREAD_CHUNKS
        self.parts = [pl.ds(k * step, step) for k in range(SPREAD_CHUNKS)]

    def side(self, k, slot):
        number = 2 * k + slot
        return remote_copy(
            self.rows_of(slot, self.parts[k]),
            self.out_ref.at[0, 2 + slot, self.parts[k]],
            self.send.at[number],
            self.recv.at[number],
            self.beside,
        )

    def over(self, k):
        number = 2 * SPREAD_CHUNKS + 1 + k
        part = self.parts[k]
        return remote_copy(
            self.out_ref.at[0, 2:4, part],
            self.out_ref.at[1, 2:4, part],
            self.send.at[number],
            self.recv.at[number],
            self.core,
        )

    def near(self):
        number = 2 * SPREAD_CHUNKS
        return remote_copy(
            self.out_ref.at[0, 0:2],
            self.out_ref.at[1, 0:2],
            self.send.at[number],
            self.recv.at[number],
            self.core,
        )

    def first(self, k):
        self.side(k, 0).start()
        self.side(k, 1).start()

    def second(self, k):
        self.side(k, 0).wait_recv()
        self.side(k, 1).wait_recv()
        self.over(k).start()

    def end(self):
        self.near().wait()
        for k in range(SPREAD_CHUNKS):
            self.over(k).wait()
            self.side(k, 0).wait_send()
            self.side(k, 1).wait_send()


def start_kernel(
    small_ref,
    tokens_ref,
    ffn_sent,
    small_out,
    normed_out,
    ffn_out,
    local,
    small_send,
    small_recv,
    spread_send,
    spread_recv,
    cross_send,
    cross_recv,
):
    x, z = lax.axis_index("section"), lax.axis_index("fsdp")
    shards = lax.axis_size("fsdp")
    _, core, across, beside, _ = peers()
    others = [
        {"section": (x + step // shards) % 2, "fsdp": (z + step) % shards} for step in range(1, 2 * shards)
    ]
    greet([core, beside] + others)
    smalls = [
        remote_copy(small_ref, small_out.at[x, z], small_send.at[step], small_recv.at[step], device)
        for step, device in enumerate(others)
    ]
    step = ffn_sent.shape[0] // FFN_CHUNKS
    crossing = []
    for k in range(FFN_CHUNKS):
        part = pl.ds(k * step, step)
        crossing.append(
            remote_copy(
                ffn_sent.at[part], ffn_out.at[part], cross_send.at[k], cross_recv.at[k], across
            )
        )
    keep = pltpu.make_async_copy(small_ref, small_out.at[x, z], local.at[0])
    normed = Spread(lambda slot, part: normed_out.at[0, slot, part], normed_out, spread_send, spread_recv)
    for one in smalls + [keep]:
        one.start()
    crossing[0].start()
    for one in smalls:
        one.wait_recv()
    keep.wait()
    gain = jnp.concatenate([small_out[0, shard, 0:1] for shard in range(shards)], 1)
    for k in range(SPREAD_CHUNKS):
        for slot, place in ((x, 0), (1 - x, 1)):
            part = normed.parts[k]
            normed_out[0, place, part] = normed_with(tokens_ref[slot, part].astype(jnp.float32), gain)
        normed.first(k)
        if k >= 1:
            crossing[k].start()
    normed.near().start()
    for k in range(SPREAD_CHUNKS):
        crossing[SPREAD_CHUNKS + k].start()
        normed.second(k)
    normed.end()
    for one in crossing:
        one.wait()
    for one in smalls:
        one.wait_send()


def start(small, tokens, ffn_sent):
    shards = lax.axis_size("fsdp")
    _, rows, width = tokens.shape
    f32, bf16 = jnp.float32, jnp.bfloat16
    if not kernels_fit():
        seq_count = lax.axis_size("seq")
        every = lax.all_gather(small, ("section", "fsdp"), axis=0).reshape(2, shards, *small.shape)
        gain = every[0, :, 0].reshape(width)
        return (
            every,
            normed_with(spread_plainly(tokens).astype(f32), gain),
            flip(ffn_sent, seq_count),
        )
    place = pl.BlockSpec(memory_space=pltpu.VMEM)
    anywhere = pl.BlockSpec(memory_space=pl.ANY)
    return pl.pallas_call(
        start_kernel,
        out_shape=[
            jax.ShapeDtypeStruct((2, shards, *small.shape), f32),
            jax.ShapeDtypeStruct((2, 4, rows, width), bf16),
            jax.ShapeDtypeStruct(ffn_sent.shape, bf16),
        ],
        in_specs=[place] * 2 + [anywhere],
        out_specs=[place] * 2 + [anywhere],
        scratch_shapes=[
            pltpu.SemaphoreType.DMA((1,)),
            pltpu.SemaphoreType.DMA((2 * shards - 1,)),
            pltpu.SemaphoreType.DMA((2 * shards - 1,)),
            pltpu.SemaphoreType.DMA((SPREAD_MOVES,)),
            pltpu.SemaphoreType.DMA((SPREAD_MOVES,)),
            pltpu.SemaphoreType.DMA((FFN_CHUNKS,)),
            pltpu.SemaphoreType.DMA((FFN_CHUNKS,)),
        ],
        compiler_params=pltpu.CompilerParams(
            collective_id=21, has_side_effects=True, vmem_limit_bytes=VMEM_BYTES
        ),
        cost_estimate=lasting(55),
        name="start",
    )(small, tokens, ffn_sent)


def spread_kernel(rows_ref, out_ref, local, send, recv):
    x = lax.axis_index("section")
    _, core, _, beside, _ = peers()
    greet([core, beside])
    keeps = [
        pltpu.make_async_copy(rows_ref.at[x], out_ref.at[0, 0], local.at[0]),
        pltpu.make_async_copy(rows_ref.at[1 - x], out_ref.at[0, 1], local.at[1]),
    ]
    for one in keeps:
        one.start()
    move = Spread(lambda slot, part: rows_ref.at[x if slot == 0 else 1 - x, part], out_ref, send, recv)
    for k in range(SPREAD_CHUNKS):
        move.first(k)
    for one in keeps:
        one.wait()
    move.near().start()
    for k in range(SPREAD_CHUNKS):
        move.second(k)
    move.end()


def spread_slots(tokens):
    _, rows, width = tokens.shape
    if not kernels_fit():
        return spread_plainly(tokens)
    place = pl.BlockSpec(memory_space=pltpu.VMEM)
    return pl.pallas_call(
        spread_kernel,
        out_shape=jax.ShapeDtypeStruct((2, 4, rows, width), tokens.dtype),
        in_specs=[place],
        out_specs=place,
        scratch_shapes=[
            pltpu.SemaphoreType.DMA((2,)),
            pltpu.SemaphoreType.DMA((SPREAD_MOVES,)),
            pltpu.SemaphoreType.DMA((SPREAD_MOVES,)),
        ],
        compiler_params=pltpu.CompilerParams(
            collective_id=22, has_side_effects=True, vmem_limit_bytes=VMEM_BYTES
        ),
        cost_estimate=lasting(42),
        name="spread_slots",
    )(tokens)


def spread_plainly(tokens):
    x = lax.axis_index("section")
    _, rows, width = tokens.shape
    near = jnp.concatenate(
        [lax.dynamic_index_in_dim(tokens, x, 0, False), lax.dynamic_index_in_dim(tokens, 1 - x, 0, False)], 0
    )
    for step in chip_bits()[1:]:
        near = jnp.concatenate([near, flip(near, step)], 0)
    return jnp.stack([near, flip(near, 1)]).reshape(2, -1, rows, width)


def body(
    tokens,
    in_weight,
    conv_kernel,
    out_weight,
    gate_weight,
    up_weight,
    down_weight,
    mixer_gain,
    ffn_gain,
    cotangent,
):
    bf16, f32 = jnp.bfloat16, jnp.float32
    x_index = lax.axis_index("section")
    q_index = lax.axis_index("seq")
    seq_count = lax.axis_size("seq")
    count = lax.axis_size("section") * seq_count
    shards = lax.axis_size("fsdp")
    share = x_index * seq_count + q_index
    first_plane = x_index == 0
    width = tokens.shape[3]
    rows = tokens.shape[2]
    hidden_width = gate_weight.shape[2]
    shard_rows = width // shards
    in_columns = 3 * width // count
    channels = width // count
    ffn_columns = hidden_width // count
    ffn_pad = -(-ffn_columns // 128) * 128
    units = half_units()
    half = len(units)
    part = shard_rows // count

    other = share ^ seq_count

    def in_share(index):
        return pick_columns(in_weight[0], index, width, count)

    def out_share(index):
        return pick_rows(out_weight[0], index, count)

    def ffn_share(index):
        nothing = jnp.zeros((shard_rows, ffn_pad - ffn_columns), bf16)
        return jnp.concatenate(
            [
                pick_columns(gate_weight[0], index, hidden_width, count),
                nothing,
                pick_columns(up_weight[0], index, hidden_width, count),
                nothing,
                pick_rows(down_weight[0], index, count).reshape(shard_rows, -1),
            ],
            1,
        )

    small = jnp.concatenate(
        [
            mixer_gain.astype(f32),
            ffn_gain.astype(f32),
            conv_kernel[0].T.astype(f32),
            jnp.zeros((3, shard_rows), f32),
        ],
        0,
    )
    def over_fsdp(value):
        return lax.all_gather(value, "fsdp", axis=0, tiled=True)

    def pack_rows(value):
        return value.reshape(part, count, channels).transpose(1, 0, 2).reshape(shard_rows, channels)

    def unpack_rows(value):
        return value.reshape(-1, count, part, channels).transpose(0, 2, 1, 3).reshape(-1, width)

    def mixer_share(index):
        return jnp.concatenate([in_share(index), pack_rows(out_share(index))], 1)

    def over_mixers(value):
        value = over_fsdp(value)
        return value[:, :in_columns], unpack_rows(value[:, in_columns:])

    mixer_own = over_mixers(mixer_share(share))
    mixer_sent = flip(mixer_share(other), seq_count)
    mixer_sent, ffn_kept, ffn_sent = tie(mixer_sent, ffn_share(share), ffn_share(other))
    small, mixer_sent = tie(small, mixer_sent)
    small, normed, ffn_sent = start(small, tokens[:, 0], ffn_sent)
    mixer_across = over_mixers(mixer_sent)
    mixer_matrices = [
        [jnp.where(first_plane == kept, own, across) for own, across in zip(mixer_own, mixer_across)]
        for kept in (True, False)
    ]
    ffn_parts = [
        jnp.where(first_plane, ffn_kept, ffn_sent),
        jnp.where(first_plane, ffn_sent, ffn_kept),
    ]
    small = small.transpose(0, 2, 1, 3)
    whole = small.reshape(2, 8, width)
    taps_all = lax.dynamic_slice(
        small[:, 2:5].reshape(2, 3, shards, count, part), (0, 0, 0, share, 0), (2, 3, shards, 1, part)
    ).reshape(2, 3, shards * part)

    pair_columns = 2 * ffn_pad
    pair = over_fsdp(ffn_parts[0][:, :pair_columns])
    normed, grad_rows = tie(normed, cotangent[:, 0])
    normed, grad_units, down_part = tie(normed, spread_slots(grad_rows), ffn_parts[0][:, pair_columns:])
    down = over_fsdp(down_part.reshape(-1, width))
    ids = jnp.stack([share ^ unit ^ side for side in (0, 1) for unit in units])
    has_before = (ids % seq_count) > 0
    has_after = (ids % seq_count) < seq_count - 1
    before_pick = (ids[None, :] == (ids - 1)[:, None]) & has_before[:, None]
    after_pick = (ids[None, :] == (ids + 1)[:, None]) & has_after[:, None]

    def pick_units(mask, edge):
        return jnp.sum(jnp.where(mask[:, :, None, None], edge[None].astype(f32), 0.0), 1)

    def flat(value):
        return value.reshape(2 * half * rows, value.shape[-1])

    def in_units(value):
        return value.reshape(2, half, rows, value.shape[-1])

    def gain_row(block, kind):
        return whole[block, kind : kind + 1]

    stream = lax.dynamic_index_in_dim(tokens[:, 0], x_index, 0, False)
    saved = []
    outputs = []
    for block in range(2):
        in_matrix, out_matrix = mixer_matrices[block]
        taps = taps_all[block]
        if kernels_fit():
            projected, held, gated = mixer_forward(normed, in_matrix, taps)
            gated = flat(gated)
            if block == 1:
                gated, crossed_out = tie(gated, crossed_out)
        else:
            projected = times(flat(normed), in_matrix[:, :in_columns])
            b_gate = projected[:, :channels]
            c_gate = projected[:, channels : 2 * channels]
            x_value = projected[:, 2 * channels :]
            conv_input = (b_gate * x_value).astype(bf16).reshape(2 * half, rows, channels)
            earlier = pick_units(before_pick, conv_input[:, -2:])
            held = jnp.concatenate([earlier, conv_input.astype(f32)], 1)
            conv_out = taps[0] * held[:, :-2] + taps[1] * held[:, 1:-1] + taps[2] * held[:, 2:]
            gated = flat((c_gate.reshape(conv_out.shape) * conv_out).astype(bf16))
        (middle,), _, normed_ffn, _, _ = exchange(
            finish_middle,
            in_units(gated),
            out_matrix,
            False,
            [stream],
            [gain_row(block, 1)],
            [f32],
            0,
            True,
            1 + 2 * block,
        )
        if block == 0:
            ffn_matrices = [(pair, down), None]
        pair_matrix, down_matrix = ffn_matrices[block]
        if kernels_fit():
            pairs, hidden = ffn_forward(flat(normed_ffn), pair_matrix, ffn_pad, ffn_columns)
        else:
            pairs = times(flat(normed_ffn), pair_matrix[:, :pair_columns])
            hidden = (jax.nn.silu(pairs[:, :ffn_pad]) * pairs[:, ffn_pad:]).astype(bf16)[:, :ffn_columns]
        if block == 0:
            hidden, down, pair_value, down_value = tie(
                hidden, down, ffn_parts[1][:, :pair_columns], ffn_parts[1][:, pair_columns:].reshape(-1, width)
            )
            down_matrix = down
            ffn_matrices = [(pair, down), (over_fsdp(pair_value), over_fsdp(down_value))]
        saved.append((stream, normed, projected, held, gated, middle, normed_ffn, pairs, hidden))
        if block == 0:
            (stream,), _, normed, _, _ = exchange(
                finish_block,
                in_units(hidden),
                down_matrix,
                False,
                [middle],
                [gain_row(1, 0)],
                [bf16],
                0,
                True,
                2,
            )
            outputs.append(stream)
            crossed_out = flip(stream, seq_count)
        else:
            last_sum = (in_units(hidden), down_matrix, middle)

    upstream = lax.dynamic_index_in_dim(cotangent[:, 0], x_index, 0, False)
    stream_grads = [None, None]
    small_grads = [None, None]
    matrix_grads = [None, None]

    def over_z(value):
        return lax.psum_scatter(value, "fsdp", scatter_dimension=0, tiled=True)

    def product(left, right):
        return by_rows(row_products(left, right))

    def small_rows(mixer_gain_part, ffn_gain_part, taps_placed):
        return jnp.concatenate(
            [
                mixer_gain_part.reshape(1, width),
                ffn_gain_part.reshape(1, width),
                taps_placed,
                jnp.zeros((3, width), f32),
            ],
            0,
        )

    def small_values():
        return jnp.stack(small_grads).reshape(2, 8, shards, shard_rows).transpose(0, 2, 1, 3)

    def to_section(value, block):
        over = [((1 - block) * seq_count + seq, block * seq_count + seq) for seq in range(seq_count)]
        return lax.ppermute(value, PLANE, over)

    inside = chip_bits()[1:] + [1]
    relative = [0, seq_count]
    for bits in inside:
        relative = relative + [unit | bits for unit in relative]

    def to_owners(value, block):
        held = [value, to_section(value, block)]
        for bits in inside:
            over = [
                (block * seq_count + seq, block * seq_count + (seq ^ bits)) for seq in range(seq_count)
            ]
            held = held + [lax.ppermute(unit, PLANE, over) for unit in held]
        return held

    mixer_sum = jnp.zeros((), f32)
    for block in (1, 0):
        in_matrix, out_matrix = mixer_matrices[block]
        pair_matrix, down_matrix = ffn_matrices[block]
        taps = taps_all[block]
        (stream, normed, projected, held, gated, middle, normed_ffn, pairs, hidden) = saved[block]
        down_product, grad_units, mixer_sum = tie(
            product(hidden, flat(grad_units)), grad_units, mixer_sum
        )
        if block == 0:
            matrix_grads[1] = (down_grad, pair_grad, mixer_sum)
        down_product = down_product.reshape(shards, -1, width)
        if kernels_fit():
            grad_pairs = ffn_backward(flat(grad_units), down_matrix, pairs, ffn_pad)
            if block == 0:
                grad_pairs, crossed = tie(grad_pairs, crossed)
        else:
            gate_value, up_value = pairs[:, :ffn_pad], pairs[:, ffn_pad:]
            grad_hidden = times_transposed(flat(grad_units), down_matrix)
            grad_hidden = jnp.pad(grad_hidden, ((0, 0), (0, ffn_pad - ffn_columns)))
            sigmoid_gate = jax.nn.sigmoid(gate_value)
            grad_gate = grad_hidden * up_value * sigmoid_gate * (1.0 + gate_value * (1.0 - sigmoid_gate))
            grad_up = grad_hidden * gate_value * sigmoid_gate
            grad_pairs = jnp.concatenate([grad_gate, grad_up], 1).astype(bf16)
        grad_pairs, pair_product = tie(grad_pairs, product(flat(normed_ffn), grad_pairs))
        pair_grad = over_z(pair_product)
        (grad_middle,), (ffn_gain_part,), mixer_grad, _, _ = exchange(
            finish_gradient,
            in_units(grad_pairs),
            pair_matrix,
            True,
            [upstream, middle],
            [gain_row(block, 1)],
            [f32],
            1,
            True,
            8 - 2 * block,
        )
        if kernels_fit():
            grad_projected, taps_part = mixer_backward(mixer_grad, out_matrix, projected, held, taps)
            grad_projected, taps_part = flat(grad_projected), taps_part[:3]
            mixer_product = mixer_products(flat(normed), grad_projected, gated, flat(mixer_grad))
        else:
            grad_gated = times_transposed(flat(mixer_grad), out_matrix).reshape(2 * half, rows, channels)
            b_gate = projected[:, :channels].reshape(2 * half, rows, channels)
            c_gate = projected[:, channels : 2 * channels].reshape(2 * half, rows, channels)
            x_value = projected[:, 2 * channels :].reshape(2 * half, rows, channels)
            conv_out = taps[0] * held[:, :-2] + taps[1] * held[:, 1:-1] + taps[2] * held[:, 2:]
            grad_cgate = grad_gated * conv_out
            grad_conv = grad_gated * c_gate
            later = pick_units(after_pick, grad_conv[:, :2])
            grad_extended = jnp.concatenate([grad_conv, later], 1)
            grad_input = (
                taps[0] * grad_extended[:, 2:]
                + taps[1] * grad_extended[:, 1:-1]
                + taps[2] * grad_extended[:, :-2]
            )
            taps_part = jnp.stack(
                [jnp.sum(grad_conv * held[:, tap : tap + rows], (0, 1)) for tap in range(3)], 0
            )
            grad_projected = flat(
                jnp.concatenate([grad_input * x_value, grad_cgate, grad_input * b_gate], 2).astype(bf16)
            )
            in_grad = row_products(flat(normed), grad_projected)
            out_grad = row_products(gated, flat(mixer_grad)).reshape(shards, part, count, channels)
            out_grad = out_grad.transpose(0, 2, 1, 3).reshape(width, channels)
            mixer_product = jnp.concatenate([in_grad, out_grad], 1)
        grad_projected, mixer_product, pair_grad = tie(
            grad_projected, mixer_product, pair_grad
        )
        if block == 1 or not kernels_fit():
            mixer_sum = over_z(mixer_product)
        own_mask = (jnp.arange(count) == share)[None, None, :, None]
        taps_placed = jnp.where(own_mask, taps_part.reshape(3, shards, 1, part), 0.0).reshape(3, width)
        if block == 0 and kernels_fit():
            break
        (grad_stream,), (mixer_gain_part,), sent, down_grad, result = exchange(
            finish_gradient,
            in_units(grad_projected),
            in_matrix,
            True,
            [grad_middle, stream],
            [gain_row(block, 0)],
            [f32],
            1,
            block == 1,
            9 - 2 * block,
            product=down_product,
            extra=last_sum if block else None,
        )
        if block == 1:
            outputs.append(result)
        stream_grads[block] = grad_stream
        small_grads[block] = small_rows(mixer_gain_part, ffn_gain_part, taps_placed)
        if block == 0:
            matrix_grads[0] = (down_grad, pair_grad, mixer_sum)
        if block == 1:
            upstream = sent[0, 0]
            grad_units = sent
            crossed = flip(result, seq_count)

    def in_order(index):
        second = to_owners(matrix_grads[1][index], 1)
        first = to_owners(matrix_grads[0][index], 0)
        ordered = jnp.zeros((count, *first[0].shape), bf16)
        for unit, one, two in zip(relative, first, second):
            ordered = lax.dynamic_update_index_in_dim(
                ordered, jnp.where(first_plane, one, two), share ^ unit, 0
            )
        return ordered

    def columns_of(value, blocks):
        piece = value.reshape(count, shard_rows, blocks, shards, -1)
        return piece.transpose(1, 2, 3, 0, 4).reshape(shard_rows, -1).astype(f32)

    if kernels_fit():
        small_grads[0] = small_rows(jnp.zeros((1, width), f32), ffn_gain_part, taps_placed)
        later = matrix_grads[1]
        stream_grads[0], crossed_last, smalls, pair_grad, down_grad, mixer_sum = last_exchange(
            in_units(grad_projected),
            in_matrix,
            grad_middle,
            stream,
            gain_row(0, 0),
            small_values(),
            upstream,
            mixer_product.reshape(shards, shard_rows, -1),
            down_product,
            later[2],
            later[0],
            (pair_grad, later[1]),
        )
        gate_grad, up_grad = place_columns(pair_grad, 2, hidden_width, ffn_pad, False)
        (in_grad,) = place_columns(mixer_sum, 3, width, channels, True)
    else:
        crossed_last = flip(jnp.stack([grad.astype(bf16) for grad in stream_grads]), seq_count)
        smalls = lax.psum(small_values(), ("section", "seq", "fsdp"))
        smalls = lax.dynamic_slice(
            smalls, (x_index, lax.axis_index("fsdp"), 0, 0), (1, 1, *smalls.shape[2:])
        )[0, 0]
        down_grad, pair_grad, mixer_sum = in_order(0), in_order(1), in_order(2)
        gate_grad = columns_of(pair_grad[..., :ffn_columns], 1)
        up_grad = columns_of(pair_grad[..., ffn_pad : ffn_pad + ffn_columns], 1)
        in_grad = columns_of(mixer_sum[..., :in_columns], 3)
    down_grad = down_grad.reshape(-1, width).astype(f32)
    if kernels_fit():
        out_grad = place_rows(mixer_sum[..., in_columns:], width)
    else:
        out_grad = unpack_rows(mixer_sum[..., in_columns:]).astype(f32)

    def by_slot(values, crossed, dtype):
        kept = jnp.where(first_plane, values[0], values[1]).astype(dtype)
        other = jnp.where(first_plane, crossed[0], crossed[1]).astype(dtype)
        return jnp.stack(
            [jnp.where(first_plane, kept, other), jnp.where(first_plane, other, kept)], 0
        )

    return (
        by_slot(outputs, (crossed_out, crossed), bf16)[None, :, None],
        by_slot(stream_grads, (crossed_last[0], crossed_last[1]), f32)[None, :, None],
        in_grad[None],
        smalls[2:5].T[None],
        out_grad[None],
        gate_grad[None],
        up_grad[None],
        down_grad[None],
        smalls[0][None],
        smalls[1][None],
    )


def solution(mesh):
    placed = (
        P(None, "fsdp", "seq", None),
        P("section", "fsdp", None),
        P("section", "fsdp", None),
        P("section", "fsdp", None),
        P("section", "fsdp", None),
        P("section", "fsdp", None),
        P("section", "fsdp", None),
        P("section", "fsdp"),
        P("section", "fsdp"),
        P(None, "fsdp", "seq", None),
    )
    return jax.shard_map(
        body,
        mesh=mesh,
        in_specs=placed,
        out_specs=(
            P("section", None, "fsdp", "seq", None),
            P("section", None, "fsdp", "seq", None),
            P("section", "fsdp", None),
            P("section", "fsdp", None),
            P("section", "fsdp", None),
            P("section", "fsdp", None),
            P("section", "fsdp", None),
            P("section", "fsdp", None),
            P("section", "fsdp"),
            P("section", "fsdp"),
        ),
        check_vma=False,
    )
```

```python
import functools

import jax
import jax.numpy as jnp
from jax import lax
from jax.experimental import pallas as pl
from jax.experimental.layout import Layout, with_layout_constraint
from jax.experimental.pallas import tpu as pltpu
from jax.sharding import PartitionSpec as P

EPSILON = 1e-05
PLANE = ("section", "seq")
MESH = pl.DeviceIdType.MESH
VMEM_BYTES = 56 * 2**20
BYTES_PER_US = 3.5e6


def lasting(us):
    return pl.CostEstimate(flops=0, bytes_accessed=int(us * BYTES_PER_US), transcendentals=0)


def tie(*values):
    return lax.optimization_barrier(values)


def kernels_fit():
    return lax.axis_size("section") == 2 and lax.axis_size("seq") == 4


def peers():
    x, q = lax.axis_index("section"), lax.axis_index("seq")
    odd = q % 2
    y = (1 - q // 2) * 2 + odd
    core = {"section": x, "seq": (q // 2) * 2 + (1 - odd)}
    across = {"section": 1 - x, "seq": q}
    beside = {"section": x, "seq": y}
    corner = {"section": x + odd * (1 - 2 * x), "seq": y * (1 - odd) + q * odd}
    return odd, core, across, beside, corner


def greet(others):
    barrier = pltpu.get_barrier_semaphore()
    for other in others:
        pl.semaphore_signal(barrier, inc=1, device_id=other, device_id_type=MESH)
    pl.semaphore_wait(barrier, len(others))


def remote_copy(source, target, send, recv, device):
    return pltpu.make_async_remote_copy(
        src_ref=source,
        dst_ref=target,
        send_sem=send,
        recv_sem=recv,
        device_id=device,
        device_id_type=MESH,
    )


def other_shards():
    z, shards = lax.axis_index("fsdp"), lax.axis_size("fsdp")
    return [{"fsdp": (z + step) % shards} for step in range(1, shards)]


class ShardSum:
    def __init__(self, product_ref, from_z, send, recv, local):
        z, shards = lax.axis_index("fsdp"), lax.axis_size("fsdp")
        self.from_z = from_z
        self.moves = [
            remote_copy(
                product_ref.at[(z + step) % shards],
                from_z.at[step - 1],
                send.at[step - 1],
                recv.at[step - 1],
                {"fsdp": (z + step) % shards},
            )
            for step in range(1, shards)
        ]
        self.keep = pltpu.make_async_copy(product_ref.at[z], from_z.at[shards - 1], local)

    def start(self):
        for one in self.moves + [self.keep]:
            one.start()

    def total(self):
        for one in self.moves:
            one.wait_recv()
        self.keep.wait()
        value = self.from_z[0].astype(jnp.float32)
        for step in range(1, self.from_z.shape[0]):
            value = value + self.from_z[step].astype(jnp.float32)
        return value.astype(self.from_z.dtype)

    def end(self):
        for one in self.moves:
            one.wait_send()


def shard_sum_scratch(product):
    shards = product.shape[0]
    return [
        pltpu.VMEM(product.shape, product.dtype),
        pltpu.SemaphoreType.DMA((shards - 1,)),
        pltpu.SemaphoreType.DMA((shards - 1,)),
        pltpu.SemaphoreType.DMA,
    ]


def sum_stages(left_ref, matrix_ref, turned, finish_rows, scratch, chunks):
    left_held, matrix_held, partial_ref, from_core, to_corner, from_corner, to_side, from_side = scratch[:8]
    send, recv, left_load, matrix_load = scratch[8:]
    odd, core, across, beside, corner = peers()
    f32 = jnp.float32
    units, step = left_ref.shape[1], left_ref.shape[2] // chunks
    depth = left_ref.shape[3]

    def load(half, k):
        return pltpu.make_async_copy(
            left_ref.at[half, :, part(k)], left_held.at[half, :, part(k)], left_load.at[half, k]
        )

    columns = matrix_held.shape[1]
    source = matrix_ref if columns == matrix_ref.shape[1] else matrix_ref.at[:, pl.ds(0, columns)]
    load_matrix = pltpu.make_async_copy(source, matrix_held, matrix_load)

    def load_all():
        load_matrix.start()
        for k in range(chunks):
            for half in (1, 0):
                load(half, k).start()

    def multiply(half, k):
        load(half, k).wait()
        left = left_held[half, :, part(k)].reshape(units * step, depth)
        right = matrix_held[:, :depth] if turned else matrix_held[...]
        value = lax.dot_general(
            left, right, (((1,), (1 if turned else 0,)), ((), ())), preferred_element_type=f32
        )
        partial_ref[half, :, part(k)] = value.astype(jnp.bfloat16).reshape(units, step, value.shape[1])

    def part(k):
        return pl.ds(k * step, step)

    def copy(slot, k, source, target, device):
        return pltpu.make_async_remote_copy(
            src_ref=source,
            dst_ref=target,
            send_sem=send.at[slot, k],
            recv_sem=recv.at[slot, k],
            device_id=device,
            device_id_type=MESH,
        )

    def core_sum(k):
        return copy(0, k, partial_ref.at[1, :, part(k)], from_core.at[:, part(k)], core)

    def corner_sum(k):
        return copy(1, k, to_corner.at[part(k)], from_corner.at[part(k)], corner)

    def across_sum(k):
        return copy(2, k, to_side.at[0, part(k)], from_side.at[0, part(k)], across)

    def beside_sum(k):
        return copy(3, k, to_side.at[1, part(k)], from_side.at[1, part(k)], beside)

    def pair_sum(unit, k):
        return partial_ref[0, unit, part(k)].astype(f32) + from_core[unit, part(k)].astype(f32)

    def send_core(k):
        if k == 0:
            load_matrix.wait()
        multiply(1, k)
        core_sum(k).start()

    def sum_corner(k):
        multiply(0, k)
        core_sum(k).wait_recv()
        to_corner[part(k)] = pair_sum(3, k).astype(jnp.bfloat16)
        corner_sum(k).start()

    def sum_sides(k):
        corner_sum(k).wait_recv()
        extra = from_corner[part(k)].astype(f32)
        to_side[0, part(k)] = (pair_sum(1, k) + jnp.where(odd == 0, extra, 0.0)).astype(jnp.bfloat16)
        to_side[1, part(k)] = (pair_sum(2, k) + jnp.where(odd == 0, 0.0, extra)).astype(jnp.bfloat16)
        across_sum(k).start()
        beside_sum(k).start()

    def total_rows(k):
        across_sum(k).wait_recv()
        beside_sum(k).wait_recv()
        finish_rows(
            k,
            part(k),
            pair_sum(0, k) + from_side[0, part(k)].astype(f32) + from_side[1, part(k)].astype(f32),
        )

    stages = [send_core, sum_corner, sum_sides, total_rows]
    return stages, [core_sum, corner_sum, across_sum, beside_sum], load_all


def ticks_of(stages, chunks, lag):
    return chunks + lag * (len(stages) - 1)


def run_tick(stages, chunks, lag, tick):
    for place, stage in enumerate(stages):
        if 0 <= tick - lag * place < chunks:
            stage(tick - lag * place)


def run_stages(stages, chunks, lag):
    for tick in range(ticks_of(stages, chunks, lag)):
        run_tick(stages, chunks, lag, tick)


def sum_scratch(left, matrix, turned, chunks):
    bf16 = jnp.bfloat16
    _, units, rows, depth = left.shape
    width = matrix.shape[0] if turned else matrix.shape[1]
    columns = depth if turned and depth % 128 == 0 else matrix.shape[1]
    return [
        pltpu.VMEM(left.shape, bf16),
        pltpu.VMEM((matrix.shape[0], columns), bf16),
        pltpu.VMEM((2, units, rows, width), bf16),
        pltpu.VMEM((units, rows, width), bf16),
        pltpu.VMEM((rows, width), bf16),
        pltpu.VMEM((rows, width), bf16),
        pltpu.VMEM((2, rows, width), bf16),
        pltpu.VMEM((2, rows, width), bf16),
        pltpu.SemaphoreType.DMA((4, chunks)),
        pltpu.SemaphoreType.DMA((4, chunks)),
        pltpu.SemaphoreType.DMA((2, chunks)),
        pltpu.SemaphoreType.DMA,
    ]


SUM_REFS = 12


def exchange_kernel(
    finish, turned, row_ins, shared_ins, row_outs, sum_outs, gather, product, extra, chunks, *refs
):
    refs = list(refs)
    left_ref, matrix_ref = refs.pop(0), refs.pop(0)
    ins = [refs.pop(0) for _ in range(row_ins)]
    shared = [refs.pop(0) for _ in range(shared_ins)]
    product_ref = refs.pop(0) if product else None
    extra_left, extra_matrix, extra_middle = [refs.pop(0) for _ in range(3)] if extra else [None] * 3
    outs = [refs.pop(0) for _ in range(row_outs)]
    sums = [refs.pop(0) for _ in range(sum_outs)]
    product_out = refs.pop(0) if product else None
    extra_out = refs.pop(0) if extra else None
    spread_ref = refs.pop(0) if gather else None
    sum_refs, refs = refs[:SUM_REFS], refs[SUM_REFS:]
    (send, recv), refs = refs[:2], refs[2:]
    product_refs, extra_refs = (refs[:4], refs[4:]) if product else ([], refs)
    odd, core, across, beside, corner = peers()
    f32 = jnp.float32
    step = left_ref.shape[2] // chunks

    def part(k):
        return pl.ds(k * step, step)

    def copy(slot, k, source, target, device):
        return pltpu.make_async_remote_copy(
            src_ref=source,
            dst_ref=target,
            send_sem=send.at[slot, k],
            recv_sem=recv.at[slot, k],
            device_id=device,
            device_id_type=MESH,
        )

    def across_out(k):
        return copy(0, k, spread_ref.at[0, 0, part(k)], spread_ref.at[0, 1, part(k)], across)

    def beside_out(k):
        return copy(1, k, spread_ref.at[0, 0, part(k)], spread_ref.at[0, 2, part(k)], beside)

    def corner_out(k):
        return copy(2, k, spread_ref.at[0, 1 + odd, part(k)], spread_ref.at[0, 3, part(k)], corner)

    def core_out(k):
        return copy(3, k, spread_ref.at[0, :, part(k)], spread_ref.at[1, :, part(k)], core)

    def finish_rows(k, rows, total):
        values, added, sent = finish(
            total, *[ref[rows].astype(f32) for ref in ins], *[ref[...] for ref in shared]
        )
        for ref, value in zip(outs, values):
            ref[rows] = value.astype(ref.dtype)
        for ref, value in zip(sums, added):
            ref[...] = value if k == 0 else ref[...] + value
        if gather:
            spread_ref[0, 0, rows] = sent
            across_out(k).start()
            beside_out(k).start()

    def pass_corner(k):
        across_out(k).wait_recv()
        beside_out(k).wait_recv()
        corner_out(k).start()

    def pass_core(k):
        corner_out(k).wait_recv()
        core_out(k).start()

    def arrive(k):
        core_out(k).wait_recv()

    stages, copies, load_all = sum_stages(left_ref, matrix_ref, turned, finish_rows, sum_refs, chunks)
    load_all()
    if gather:
        stages = stages + [pass_corner, pass_core, arrive]
        copies = copies + [across_out, beside_out, corner_out, core_out]
    if extra:

        def extra_rows(k, rows, total):
            extra_out[rows] = (extra_middle[rows] + total).astype(extra_out.dtype)

        later, more, load_more = sum_stages(
            extra_left, extra_matrix, False, extra_rows, extra_refs, chunks
        )
        load_more()
        stages = stages[:1] + [lambda k, a=a, b=b: (a(k), b(k)) for a, b in zip(stages[1:5], later)] + stages[5:]
        copies = copies + more
    greet([core, across, beside] + (other_shards() if product else []))
    if product:
        shard_sum = ShardSum(product_ref, *product_refs)
        shard_sum.start()
    run_stages(stages, chunks, 1 if extra or left_ref.shape[3] > 1024 else 2)
    if product:
        product_out[...] = shard_sum.total()
        shard_sum.end()
    for k in range(chunks):
        for one in copies:
            one(k).wait_send()


def exchange(
    finish,
    left,
    matrix,
    turned,
    row_ins,
    shared_ins,
    row_outs,
    sum_outs,
    gather,
    number,
    product=None,
    extra=None,
    chunks=4,
):
    _, units, rows, _ = left.shape
    width = matrix.shape[0] if turned else matrix.shape[1]
    if not kernels_fit():
        return exchange_plainly(
            finish, left, matrix, turned, row_ins, shared_ins, row_outs, gather, product, extra
        )
    bf16 = jnp.bfloat16
    shapes = [jax.ShapeDtypeStruct((rows, width), dtype) for dtype in row_outs]
    shapes += [jax.ShapeDtypeStruct((1, width), jnp.float32)] * sum_outs
    shapes += [] if product is None else [jax.ShapeDtypeStruct(product.shape[1:], product.dtype)]
    shapes += [] if extra is None else [jax.ShapeDtypeStruct((rows, width), bf16)]
    shapes += [jax.ShapeDtypeStruct((2, units, rows, width), bf16)] * gather
    more = ([] if product is None else [product]) + list(extra or ())
    place, anywhere = pl.BlockSpec(memory_space=pltpu.VMEM), pl.BlockSpec(memory_space=pl.ANY)
    result = pl.pallas_call(
        functools.partial(
            exchange_kernel,
            finish,
            turned,
            len(row_ins),
            len(shared_ins),
            len(row_outs),
            sum_outs,
            gather,
            product is not None,
            extra is not None,
            chunks,
        ),
        out_shape=shapes,
        in_specs=[anywhere] * 2
        + [place] * (len(row_ins) + len(shared_ins))
        + ([] if product is None else [anywhere])
        + ([] if extra is None else [anywhere, anywhere, place]),
        out_specs=[place] * len(shapes),
        scratch_shapes=sum_scratch(left, matrix, turned, chunks)
        + [pltpu.SemaphoreType.DMA((4, chunks))] * 2
        + ([] if product is None else shard_sum_scratch(product))
        + ([] if extra is None else sum_scratch(extra[0], extra[1], False, chunks)),
        compiler_params=pltpu.CompilerParams(
            collective_id=number, has_side_effects=True, vmem_limit_bytes=VMEM_BYTES
        ),
        cost_estimate=lasting(66 if gather else 38),
        name=("exchange_%d" % number),
    )(left, matrix, *row_ins, *shared_ins, *more)
    result = list(result)
    rows_done = [result.pop(0) for _ in row_outs]
    sums = [result.pop(0) for _ in range(sum_outs)]
    product = None if product is None else result.pop(0)
    extra = None if extra is None else result.pop(0)
    return rows_done, sums, (result.pop(0) if gather else None), product, extra


def plane_total(left, matrix, turned):
    multiply = times_transposed if turned else times
    matrix = matrix[:, : left.shape[3]] if turned else matrix
    near, far = [multiply(half.reshape(-1, half.shape[2]), matrix).astype(jnp.bfloat16) for half in left]
    total = near.astype(jnp.float32) + flip(far, 1).astype(jnp.float32)
    return collect(total, (lax.axis_index("seq") % 2) == 1)


def exchange_plainly(finish, left, matrix, turned, row_ins, shared_ins, row_outs, gather, product, extra):
    total = plane_total(left, matrix, turned)
    rows, sums, sent = finish(total, *[value.astype(jnp.float32) for value in row_ins], *shared_ins)
    rows = [value.astype(dtype) for value, dtype in zip(rows, row_outs)]
    if product is not None:
        product = lax.psum_scatter(
            product.reshape(-1, product.shape[2]), "fsdp", scatter_dimension=0, tiled=True
        )
    if extra is not None:
        extra = (plane_total(extra[0], extra[1], False) + extra[2]).astype(jnp.bfloat16)
    if gather:
        odd = (lax.axis_index("seq") % 2) == 1
        sent = jnp.stack(spread(sent, odd)).reshape(*left.shape[:3], -1)
    return rows, sums, sent, product, extra


def finish_middle(total, stream, gain):
    middle = stream + total
    return [middle], [], (middle * rms_scale(middle) * gain).astype(jnp.bfloat16)


def finish_block(total, middle, gain):
    result = (middle + total).astype(jnp.bfloat16)
    stream = result.astype(jnp.float32)
    return [result], [], (stream * rms_scale(stream) * gain).astype(jnp.bfloat16)


def finish_gradient(total, upstream, stream, gain):
    scale = rms_scale(stream)
    weighted = gain * total
    grad = (
        upstream
        + scale * weighted
        - stream * scale**3 * jnp.mean(weighted * stream, -1, keepdims=True)
    )
    added = jnp.sum(total * stream * scale, 0, keepdims=True)
    return [grad], [added], grad.astype(jnp.bfloat16)


LAST_CHUNKS = 4
OWNER_CHUNKS = (6, 1, 1)


def last_kernel(
    left_ref,
    matrix_ref,
    upstream_ref,
    stream_ref,
    gain_ref,
    smalls_ref,
    later_ref,
    product_ref,
    down_product_ref,
    mixer_ref,
    down_ref,
    pair0_ref,
    pair1_ref,
    grad_ref,
    crossed_ref,
    smalls_out,
    pair_out,
    down_out,
    mixer_out,
    *scratch,
):
    sum_refs, scratch = scratch[:SUM_REFS], scratch[SUM_REFS:]
    pair_both, down_both, mixer_both, grad_low, gain_sum = scratch[:5]
    small_sum, small_sent, small_side, small_z = scratch[5:9]
    local, own_send, own_recv, small_send, small_recv, cross_send, cross_recv = scratch[9:16]
    mixer_sum = ShardSum(product_ref, *scratch[16:20])
    down_sum = ShardSum(down_product_ref, *scratch[20:])
    x, q, z = lax.axis_index("section"), lax.axis_index("seq"), lax.axis_index("fsdp")
    shards = lax.axis_size("fsdp")
    _, core, across, beside, _ = peers()
    f32, bf16 = jnp.float32, jnp.bfloat16
    others = other_shards()
    share = x * 4 + q
    share_across = (1 - x) * 4 + q
    beside_q = (1 - q // 2) * 2 + q % 2
    share_beside = x * 4 + beside_q
    share_corner = (1 - x) * 4 + beside_q

    def remote(source, target, send, recv, device):
        return pltpu.make_async_remote_copy(
            src_ref=source,
            dst_ref=target,
            send_sem=send,
            recv_sem=recv,
            device_id=device,
            device_id_type=MESH,
        )

    class Owners:
        def __init__(self, place, both, out):
            self.place, self.both, self.out = place, both, out
            self.step = both.shape[1] // OWNER_CHUNKS[place]
            self.chunks = range(OWNER_CHUNKS[place])

        def move(self, slot, k, source, target, device):
            part = pl.ds(k * self.step, self.step)
            place = self.place
            return remote(
                source.at[part],
                self.out.at[target, part],
                own_send.at[place, slot, k],
                own_recv.at[place, slot, k],
                device,
            )

        def cross(self, k):
            return self.move(0, k, self.both.at[1 - x], share, across)

        def side(self, k):
            return self.move(1, k, self.both.at[x], share, beside)

        def near(self, k):
            return self.move(2, k, self.both.at[x], share, core)

        def side_across(self, k):
            return self.move(3, k, self.out.at[share_across], share_across, beside)

        def near_across(self, k):
            return self.move(4, k, self.out.at[share_across], share_across, core)

        def near_beside(self, k):
            return self.move(5, k, self.out.at[share_beside], share_beside, core)

        def near_corner(self, k):
            return self.move(6, k, self.out.at[share_corner], share_corner, core)

        def keep(self):
            return pltpu.make_async_copy(self.both.at[x], self.out.at[share], local.at[4 + self.place])

        def first(self, k):
            self.cross(k).start()
            self.side(k).start()
            self.near(k).start()

        def second(self, k):
            self.cross(k).wait_recv()
            self.side_across(k).start()
            self.near_across(k).start()

        def third(self, k):
            self.side(k).wait_recv()
            self.near_beside(k).start()

        def fourth(self, k):
            self.side_across(k).wait_recv()
            self.near_corner(k).start()

        def end(self):
            for k in self.chunks:
                for one in (self.near, self.near_across, self.near_beside, self.near_corner):
                    one(k).wait_recv()
                for one in (
                    self.cross,
                    self.side,
                    self.near,
                    self.side_across,
                    self.near_across,
                    self.near_beside,
                    self.near_corner,
                ):
                    one(k).wait_send()
            self.keep().wait()

    pair = Owners(0, pair_both, pair_out)
    down = Owners(1, down_both, down_out)
    mixer = Owners(2, mixer_both, mixer_out)

    def finish_rows(k, rows, total):
        (grad,), (added,), sent = finish_gradient(
            total, upstream_ref[rows].astype(f32), stream_ref[rows].astype(f32), gain_ref[...]
        )
        grad_ref[rows] = grad
        grad_low[rows] = sent
        gain_sum[...] = added if k == 0 else gain_sum[...] + added

    stages, copies, load_all = sum_stages(left_ref, matrix_ref, True, finish_rows, sum_refs, LAST_CHUNKS)
    load_all()
    loads = [
        pltpu.make_async_copy(pair0_ref, pair_both.at[0], local.at[0]),
        pltpu.make_async_copy(pair1_ref, pair_both.at[1], local.at[1]),
        pltpu.make_async_copy(down_ref, down_both.at[1], local.at[2]),
        pltpu.make_async_copy(mixer_ref, mixer_both.at[1], local.at[3]),
    ]
    for one in loads:
        one.start()
    greet([core, across, beside] + others)
    mixer_sum.start()
    later = remote(later_ref, crossed_ref.at[1], cross_send.at[1], cross_recv.at[1], across)
    later.start()
    for one in loads[:2]:
        one.wait()
    pair.keep().start()
    for tick in range(ticks_of(stages, LAST_CHUNKS, 1)):
        run_tick(stages, LAST_CHUNKS, 1, tick)
        if tick in pair.chunks:
            pair.first(tick)
        if tick == 1:
            down_sum.start()

    small_rows = smalls_ref.shape[3]
    small_sum[...] = smalls_ref[...]
    for shard in range(shards):
        small_sum[0, shard, 0:1] += gain_sum[:, shard * small_rows : (shard + 1) * small_rows]

    def small_move(step, device):
        return remote(small_sent.at[step], small_side.at[step], small_send.at[step], small_recv.at[step], device)

    for step, device in enumerate((core, across, beside)):
        small_sent[step] = small_sum[...]
        small_move(step, device).start()
        pair.second(step)
        small_move(step, device).wait()
        small_sum[...] += small_side[step]
    small_moves = [
        remote(
            small_sum.at[x, (z + step + 1) % shards],
            small_z.at[step],
            small_send.at[3 + step],
            small_recv.at[3 + step],
            device,
        )
        for step, device in enumerate(others)
    ]
    for one in small_moves:
        one.start()

    mixer_both[0] = mixer_sum.total()
    loads[3].wait()
    mixer.keep().start()
    mixer.first(0)
    for k in pair.chunks[3:]:
        pair.second(k)
    mixer.second(0)
    down_both[0] = down_sum.total()
    loads[2].wait()
    down.keep().start()
    down.first(0)
    cross = remote(grad_low, crossed_ref.at[0], cross_send.at[0], cross_recv.at[0], across)
    cross.start()
    for k in pair.chunks:
        pair.third(k)
    mixer.third(0)
    down.second(0)
    for k in pair.chunks:
        pair.fourth(k)
    mixer.fourth(0)
    down.third(0)
    down.fourth(0)
    small_total = small_sum[x, z]
    for step, one in enumerate(small_moves):
        one.wait()
        small_total = small_total + small_z[step]
    smalls_out[...] = small_total
    for owners in (pair, down, mixer):
        owners.end()
    cross.wait()
    later.wait()
    mixer_sum.end()
    down_sum.end()
    for k in range(LAST_CHUNKS):
        for one in copies:
            one(k).wait_send()


def last_exchange(left, matrix, upstream, stream, gain, smalls, later, product, down_product, mixer, down, pairs):
    _, units, rows, _ = left.shape
    width = matrix.shape[0]
    shards, shard_rows, mixer_columns = product.shape
    bf16, f32 = jnp.bfloat16, jnp.float32
    count = 2 * units
    vmem = pl.BlockSpec(memory_space=pltpu.VMEM)
    anywhere = pl.BlockSpec(memory_space=pl.ANY)
    return pl.pallas_call(
        last_kernel,
        out_shape=[
            jax.ShapeDtypeStruct((rows, width), f32),
            jax.ShapeDtypeStruct((2, rows, width), bf16),
            jax.ShapeDtypeStruct(smalls.shape[2:], f32),
            jax.ShapeDtypeStruct((count, *pairs[0].shape), bf16),
            jax.ShapeDtypeStruct((count, *down.shape), bf16),
            jax.ShapeDtypeStruct((count, shard_rows, mixer_columns), bf16),
        ],
        in_specs=[anywhere] * 2 + [vmem] * 5 + [anywhere] * 6,
        out_specs=[vmem] * 3 + [anywhere] * 3,
        scratch_shapes=sum_scratch(left, matrix, True, LAST_CHUNKS)
        + [
            pltpu.VMEM((2, *pairs[0].shape), bf16),
            pltpu.VMEM((2, *down.shape), bf16),
            pltpu.VMEM((2, shard_rows, mixer_columns), bf16),
            pltpu.VMEM((rows, width), bf16),
            pltpu.VMEM((1, width), f32),
            pltpu.VMEM(smalls.shape, f32),
            pltpu.VMEM((3, *smalls.shape), f32),
            pltpu.VMEM((3, *smalls.shape), f32),
            pltpu.VMEM((shards - 1, *smalls.shape[2:]), f32),
            pltpu.SemaphoreType.DMA((7,)),
            pltpu.SemaphoreType.DMA((3, 7, max(OWNER_CHUNKS))),
            pltpu.SemaphoreType.DMA((3, 7, max(OWNER_CHUNKS))),
            pltpu.SemaphoreType.DMA((2 + shards,)),
            pltpu.SemaphoreType.DMA((2 + shards,)),
            pltpu.SemaphoreType.DMA((2,)),
            pltpu.SemaphoreType.DMA((2,)),
        ]
        + shard_sum_scratch(product)
        + shard_sum_scratch(down_product),
        compiler_params=pltpu.CompilerParams(
            collective_id=20, has_side_effects=True, vmem_limit_bytes=VMEM_BYTES
        ),
        cost_estimate=lasting(130),
        name="last_exchange",
    )(left, matrix, upstream, stream, gain, smalls, later, product, down_product, mixer, down, *pairs)


def place_kernel(blocks, width, stride, stack_ref, *outs):
    shards = lax.axis_size("fsdp")
    count = stack_ref.shape[0]
    part = width // shards // count
    for block in range(blocks):
        pieces = []
        for shard in range(shards):
            start = block * stride + shard * part
            pieces += [stack_ref[share, :, start : start + part] for share in range(count)]
        value = jnp.concatenate(pieces, 1).astype(jnp.float32)
        if len(outs) == 1:
            outs[0][:, block * width : (block + 1) * width] = value
        else:
            outs[block][...] = value


def place_rows_kernel(first, stack_ref, out_ref):
    channels = stack_ref.shape[2] - first
    blocks = out_ref.shape[1] // channels
    part = stack_ref.shape[1] // blocks
    for share in range(stack_ref.shape[0]):
        pieces = [stack_ref[share, block * part : (block + 1) * part, first:] for block in range(blocks)]
        out_ref[share * part : (share + 1) * part] = jnp.concatenate(pieces, 1).astype(jnp.float32)


def place_rows(stack, first, width):
    (value,) = local_call(
        functools.partial(place_rows_kernel, first),
        [((stack.shape[1], width), jnp.float32)],
        [],
        5,
        "place_rows",
        stack,
    )
    return value


def place_columns(stack, blocks, width, stride, together):
    count, rows, columns = stack.shape
    step = 96 if rows % 96 == 0 else rows
    widths = [blocks * width] if together else [width] * blocks
    return pl.pallas_call(
        functools.partial(place_kernel, blocks, width, stride),
        grid=(rows // step,),
        out_shape=[jax.ShapeDtypeStruct((rows, each), jnp.float32) for each in widths],
        in_specs=[pl.BlockSpec((count, step, columns), lambda i: (0, i, 0))],
        out_specs=[pl.BlockSpec((step, each), lambda i: (i, 0)) for each in widths],
        compiler_params=pltpu.CompilerParams(vmem_limit_bytes=VMEM_BYTES),
        cost_estimate=lasting(14),
        name="place_columns",
    )(stack)


def local_call(kernel, outs, scratch, us, name, *operands, far=()):
    place = pl.BlockSpec(memory_space=pltpu.VMEM)
    places = [pl.BlockSpec(memory_space=pl.ANY) if i in far else place for i in range(len(operands))]
    return pl.pallas_call(
        kernel,
        out_shape=[jax.ShapeDtypeStruct(shape, dtype) for shape, dtype in outs],
        in_specs=places,
        out_specs=[place] * len(outs),
        scratch_shapes=scratch,
        compiler_params=pltpu.CompilerParams(vmem_limit_bytes=VMEM_BYTES),
        cost_estimate=lasting(us),
        name=name,
    )(*operands)


def unit_place(difference):
    return difference // 4 + (difference // 2 % 2) * 2 + (difference % 2) * 4


def unit_bits(place):
    return (place % 2) * 4 + (place // 2 % 2) * 2 + place // 4


def either(left, right):
    total = 0
    for bit in (1, 2, 4):
        one, two = left // bit % 2, right // bit % 2
        total = total + bit * (one + two - 2 * one * two)
    return total


def neighbour(place, step):
    share = lax.axis_index("section") * 4 + lax.axis_index("seq")
    device = either(share, unit_bits(place))
    seq = device % 4 + step
    inside = jnp.where((seq >= 0) & (seq < 4), 1.0, 0.0)
    seq = (seq + 4) % 4
    return unit_place(either(share, device // 4 * 4 + seq)), inside


def conv_parts(held_ref, place):
    f32 = jnp.float32
    before, inside = neighbour(place, -1)
    here = held_ref[place]
    rows = here.shape[0]
    edge = held_ref[before, rows - 2 : rows] * inside
    whole = jnp.concatenate([edge.astype(f32), here], 0)
    return whole[:rows], whole[1 : rows + 1], here


def load_units(source, target, sems):
    def load(place):
        return pltpu.make_async_copy(source.at[place], target.at[place], sems.at[place])

    for place in range(8):
        load(place).start()
    return lambda place: load(place).wait()


def mixer_forward_kernel(
    channels, normed_far, matrix_ref, taps_ref, projected_ref, held_ref, gated_ref, normed_ref, sems
):
    f32, bf16 = jnp.float32, jnp.bfloat16
    wait_unit = load_units(normed_far, normed_ref, sems)

    def project(place, carry):
        wait_unit(place)
        value = jnp.dot(
            normed_ref[place], matrix_ref[:, : 3 * channels], preferred_element_type=f32
        )
        projected_ref[place] = value
        held_ref[place] = (value[:, :channels] * value[:, 2 * channels :]).astype(bf16).astype(f32)
        return carry

    lax.fori_loop(0, 8, project, 0)

    def convolve(place, carry):
        first, second, third = conv_parts(held_ref, place)
        value = taps_ref[0:1] * first + taps_ref[1:2] * second + taps_ref[2:3] * third
        gated_ref[place] = (projected_ref[place, :, channels : 2 * channels] * value).astype(bf16)
        return carry

    lax.fori_loop(0, 8, convolve, 0)


def mixer_forward(normed, matrix, taps):
    rows = normed.shape[2]
    channels = taps.shape[1]
    f32, bf16 = jnp.float32, jnp.bfloat16
    return local_call(
        functools.partial(mixer_forward_kernel, channels),
        [((8, rows, 3 * channels), f32), ((8, rows, channels), f32), ((8, rows, channels), bf16)],
        [pltpu.VMEM((8, *normed.shape[2:]), bf16), pltpu.SemaphoreType.DMA((8,))],
        10,
        "mixer_forward",
        normed.reshape(8, rows, -1),
        matrix,
        taps,
        far=(0,),
    )


def mixer_backward_kernel(
    channels,
    grad_far,
    matrix_ref,
    projected_far,
    held_ref,
    taps_ref,
    out_ref,
    taps_out,
    conv_grad,
    gate_grad,
    grad_ref,
    projected_ref,
    grad_sems,
    projected_sems,
):
    f32, bf16 = jnp.float32, jnp.bfloat16
    wait_grad = load_units(grad_far, grad_ref, grad_sems)
    wait_projected = load_units(projected_far, projected_ref, projected_sems)

    def to_gates(place, carry):
        wait_grad(place)
        wait_projected(place)
        grad = lax.dot_general(
            grad_ref[place], matrix_ref[...], (((1,), (1,)), ((), ())), preferred_element_type=f32
        )
        first, second, third = conv_parts(held_ref, place)
        value = taps_ref[0:1] * first + taps_ref[1:2] * second + taps_ref[2:3] * third
        back = grad * projected_ref[place, :, channels : 2 * channels]
        gate_grad[place] = grad * value
        conv_grad[place] = back
        added = [jnp.sum(back * shifted, 0, keepdims=True) for shifted in (first, second, third)]
        return carry + jnp.concatenate(added + [jnp.zeros((5, channels), f32)], 0)

    taps_out[...] = lax.fori_loop(0, 8, to_gates, jnp.zeros((8, channels), f32))

    def to_inputs(place, carry):
        after, inside = neighbour(place, 1)
        here = conv_grad[place]
        rows = here.shape[0]
        whole = jnp.concatenate([here, conv_grad[after, 0:2] * inside], 0)
        grad = (
            taps_ref[0:1] * whole[2:] + taps_ref[1:2] * whole[1 : rows + 1] + taps_ref[2:3] * here
        )
        out_ref[place] = jnp.concatenate(
            [
                grad * projected_ref[place, :, 2 * channels :],
                gate_grad[place],
                grad * projected_ref[place, :, :channels],
            ],
            1,
        ).astype(bf16)
        return carry

    lax.fori_loop(0, 8, to_inputs, 0)


def mixer_backward(grads, matrix, projected, held, taps):
    rows = grads.shape[2]
    channels = taps.shape[1]
    f32, bf16 = jnp.float32, jnp.bfloat16
    return local_call(
        functools.partial(mixer_backward_kernel, channels),
        [((8, rows, 3 * channels), bf16), ((8, channels), f32)],
        [
            pltpu.VMEM((8, rows, channels), f32),
            pltpu.VMEM((8, rows, channels), f32),
            pltpu.VMEM((8, *grads.shape[2:]), bf16),
            pltpu.VMEM(projected.shape, f32),
            pltpu.SemaphoreType.DMA((8,)),
            pltpu.SemaphoreType.DMA((8,)),
        ],
        12,
        "mixer_backward",
        grads.reshape(8, rows, -1),
        matrix,
        projected,
        held,
        taps,
        far=(0, 2),
    )


def ffn_forward_kernel(pad, normed_ref, matrix_ref, pairs_ref, hidden_ref):
    pairs = jnp.dot(normed_ref[...], matrix_ref[:, : 2 * pad], preferred_element_type=jnp.float32)
    pairs_ref[...] = pairs
    gate, up = pairs[:, :pad], pairs[:, pad:]
    hidden = gate * jax.nn.sigmoid(gate) * up
    hidden_ref[...] = hidden[:, : hidden_ref.shape[1]].astype(jnp.bfloat16)


def ffn_forward(normed, matrix, pad, columns):
    count, width = normed.shape
    step = 256
    return pl.pallas_call(
        functools.partial(ffn_forward_kernel, pad),
        grid=(count // step,),
        out_shape=[
            jax.ShapeDtypeStruct((count, 2 * pad), jnp.float32),
            jax.ShapeDtypeStruct((count, columns), jnp.bfloat16),
        ],
        in_specs=[
            pl.BlockSpec((step, width), lambda i: (i, 0)),
            pl.BlockSpec(matrix.shape, lambda i: (0, 0)),
        ],
        out_specs=[
            pl.BlockSpec((step, 2 * pad), lambda i: (i, 0)),
            pl.BlockSpec((step, columns), lambda i: (i, 0)),
        ],
        compiler_params=pltpu.CompilerParams(vmem_limit_bytes=VMEM_BYTES),
        cost_estimate=lasting(16),
        name="ffn_forward",
    )(normed, matrix)


def ffn_backward_kernel(pad, grad_ref, matrix_ref, pairs_ref, out_ref):
    grad = lax.dot_general(
        grad_ref[...], matrix_ref[...], (((1,), (1,)), ((), ())), preferred_element_type=jnp.float32
    )
    extra = pad - grad.shape[1]
    if extra:
        grad = jnp.concatenate([grad, jnp.zeros((grad.shape[0], extra), jnp.float32)], 1)
    gate, up = pairs_ref[:, :pad], pairs_ref[:, pad:]
    sigmoid = jax.nn.sigmoid(gate)
    out_ref[:, :pad] = (grad * up * sigmoid * (1.0 + gate * (1.0 - sigmoid))).astype(jnp.bfloat16)
    out_ref[:, pad:] = (grad * gate * sigmoid).astype(jnp.bfloat16)


def ffn_backward(grads, matrix, pairs, pad):
    count, width = grads.shape
    step = 256
    return pl.pallas_call(
        functools.partial(ffn_backward_kernel, pad),
        grid=(count // step,),
        out_shape=jax.ShapeDtypeStruct((count, 2 * pad), jnp.bfloat16),
        in_specs=[
            pl.BlockSpec((step, width), lambda i: (i, 0)),
            pl.BlockSpec(matrix.shape, lambda i: (0, 0)),
            pl.BlockSpec((step, 2 * pad), lambda i: (i, 0)),
        ],
        out_specs=pl.BlockSpec((step, 2 * pad), lambda i: (i, 0)),
        compiler_params=pltpu.CompilerParams(vmem_limit_bytes=VMEM_BYTES),
        cost_estimate=lasting(16),
        name="ffn_backward",
    )(grads, matrix, pairs)


def mixer_product_kernel(
    shards, normed_far, projected_ref, gated_ref, grad_far, out_ref, normed_ref, grad_ref, sems
):
    f32, bf16 = jnp.float32, jnp.bfloat16
    blocks = normed_ref.shape[0]
    step = normed_ref.shape[2]
    loads = [
        pltpu.make_async_copy(normed_far.at[:, pl.ds(i * step, step)], normed_ref.at[i], sems.at[i])
        for i in range(blocks)
    ]
    loads.append(pltpu.make_async_copy(grad_far, grad_ref, sems.at[blocks]))
    for one in loads:
        one.start()
    turned = (((0,), (0,)), ((), ()))
    columns = projected_ref.shape[1]
    width, channels = grad_ref.shape[1], gated_ref.shape[1]
    for i in range(blocks):
        loads[i].wait()
        out_ref[i * step : (i + 1) * step, :columns] = lax.dot_general(
            normed_ref[i], projected_ref[...], turned, preferred_element_type=f32
        ).astype(bf16)
    loads[blocks].wait()
    value = lax.dot_general(gated_ref[...], grad_ref[...], turned, preferred_element_type=f32)
    part = channels // shards
    pieces = width // channels
    for shard in range(shards):
        for block in range(pieces):
            row = (shard * pieces + block) * part
            out_ref[row : row + part, columns:] = value[
                shard * part : (shard + 1) * part, block * channels : (block + 1) * channels
            ].astype(bf16)


def mixer_products(normed, projected_grad, gated, grad):
    width, columns, channels = normed.shape[1], projected_grad.shape[1], gated.shape[1]
    shards = lax.axis_size("fsdp")
    blocks = width // 256
    (value,) = local_call(
        functools.partial(mixer_product_kernel, shards),
        [((width, columns + channels), jnp.bfloat16)],
        [
            pltpu.VMEM((blocks, normed.shape[0], width // blocks), jnp.bfloat16),
            pltpu.VMEM(grad.shape, jnp.bfloat16),
            pltpu.SemaphoreType.DMA((blocks + 1,)),
        ],
        14,
        "mixer_products",
        normed,
        projected_grad,
        gated,
        grad,
        far=(0, 3),
    )
    return value


def flip(value, bits):
    count = lax.axis_size("section") * lax.axis_size("seq")
    return lax.ppermute(value, PLANE, [(source, source ^ bits) for source in range(count)])


def flip_by_core(value, even_bits, odd_bits):
    count = lax.axis_size("section") * lax.axis_size("seq")
    pairs = [(source, source ^ (odd_bits if source & 1 else even_bits)) for source in range(count)]
    return lax.ppermute(value, PLANE, pairs)


def chip_bits():
    bits = [lax.axis_size("seq")]
    step = lax.axis_size("seq") // 2
    while step > 1:
        bits.append(step)
        step //= 2
    return bits


def half_units():
    units = [0]
    for bits in chip_bits():
        units = units + [unit | bits for unit in units]
    return units


def spread_chips(own, odd):
    bits = chip_bits()
    if len(bits) == 2:
        first = flip(own, bits[0])
        second = flip(own, bits[1])
        third = flip_by_core(jnp.where(odd, second, first), bits[1], bits[0])
        return jnp.concatenate([own, first, second, third], 0)
    held = own
    for step in bits:
        held = jnp.concatenate([held, flip(held, step)], 0)
    return held


def spread(own, odd):
    near = spread_chips(own, odd)
    return near, flip(near, 1)


def collect(near, odd):
    bits = chip_bits()
    if len(bits) == 2:
        rows = near.shape[0] // 4
        held = near
        third = flip_by_core(held[3 * rows :].astype(jnp.bfloat16), bits[1], bits[0]).astype(jnp.float32)
        first = held[rows : 2 * rows] + jnp.where(odd, 0.0, third)
        second = held[2 * rows : 3 * rows] + jnp.where(odd, third, 0.0)
        first = flip(first.astype(jnp.bfloat16), bits[0]).astype(jnp.float32)
        second = flip(second.astype(jnp.bfloat16), bits[1]).astype(jnp.float32)
        return held[:rows] + first + second
    held = near
    for step in reversed(bits):
        rows = held.shape[0] // 2
        held = held[:rows] + flip(held[rows:].astype(jnp.bfloat16), step).astype(jnp.float32)
    return held


def rms_scale(stream):
    return lax.rsqrt(jnp.mean(stream * stream, -1, keepdims=True) + EPSILON)


def times(left, matrix):
    return jnp.dot(left, matrix, preferred_element_type=jnp.float32)


def times_transposed(left, matrix):
    return lax.dot_general(
        left, matrix, (((1,), (1,)), ((), ())), preferred_element_type=jnp.float32
    )


def by_rows(value):
    return with_layout_constraint(value, Layout(major_to_minor=tuple(range(value.ndim))))


def row_products(left, right):
    return lax.dot_general(
        left, right, (((0,), (0,)), ((), ())), preferred_element_type=jnp.float32
    ).astype(jnp.bfloat16)


def normed_with(stream, gain):
    return (stream * rms_scale(stream) * gain).astype(jnp.bfloat16)


def pick_columns(matrix, share, width, count):
    shards = lax.axis_size("fsdp")
    part = width // shards // count
    return jnp.concatenate(
        [
            lax.dynamic_slice(
                matrix, (0, start + shard * (width // shards) + share * part), (matrix.shape[0], part)
            )
            for start in range(0, matrix.shape[1], width)
            for shard in range(shards)
        ],
        1,
    )


def pick_rows(matrix, share, count):
    part = matrix.shape[0] // count
    return lax.dynamic_slice(matrix, (share * part, 0), (part, matrix.shape[1]))


SPREAD_CHUNKS = 4
SPREAD_MOVES = 3 * SPREAD_CHUNKS + 1
FFN_CHUNKS = 2 * SPREAD_CHUNKS


class Spread:
    def __init__(self, rows_of, out_ref, send, recv):
        self.rows_of, self.out_ref, self.send, self.recv = rows_of, out_ref, send, recv
        _, self.core, _, self.beside, _ = peers()
        step = out_ref.shape[2] // SPREAD_CHUNKS
        self.parts = [pl.ds(k * step, step) for k in range(SPREAD_CHUNKS)]

    def side(self, k, slot):
        number = 2 * k + slot
        return remote_copy(
            self.rows_of(slot, self.parts[k]),
            self.out_ref.at[0, 2 + slot, self.parts[k]],
            self.send.at[number],
            self.recv.at[number],
            self.beside,
        )

    def over(self, k):
        number = 2 * SPREAD_CHUNKS + 1 + k
        part = self.parts[k]
        return remote_copy(
            self.out_ref.at[0, 2:4, part],
            self.out_ref.at[1, 2:4, part],
            self.send.at[number],
            self.recv.at[number],
            self.core,
        )

    def near(self):
        number = 2 * SPREAD_CHUNKS
        return remote_copy(
            self.out_ref.at[0, 0:2],
            self.out_ref.at[1, 0:2],
            self.send.at[number],
            self.recv.at[number],
            self.core,
        )

    def first(self, k):
        self.side(k, 0).start()
        self.side(k, 1).start()

    def second(self, k):
        self.side(k, 0).wait_recv()
        self.side(k, 1).wait_recv()
        self.over(k).start()

    def end(self):
        self.near().wait()
        for k in range(SPREAD_CHUNKS):
            self.over(k).wait()
            self.side(k, 0).wait_send()
            self.side(k, 1).wait_send()


def start_kernel(
    small_ref,
    tokens_ref,
    ffn_sent,
    small_out,
    normed_out,
    ffn_out,
    local,
    small_send,
    small_recv,
    spread_send,
    spread_recv,
    cross_send,
    cross_recv,
):
    x, z = lax.axis_index("section"), lax.axis_index("fsdp")
    shards = lax.axis_size("fsdp")
    _, core, across, beside, _ = peers()
    others = [
        {"section": (x + step // shards) % 2, "fsdp": (z + step) % shards} for step in range(1, 2 * shards)
    ]
    greet([core, beside] + others)
    smalls = [
        remote_copy(small_ref, small_out.at[x, z], small_send.at[step], small_recv.at[step], device)
        for step, device in enumerate(others)
    ]
    step = ffn_sent.shape[0] // FFN_CHUNKS
    crossing = []
    for k in range(FFN_CHUNKS):
        part = pl.ds(k * step, step)
        crossing.append(
            remote_copy(
                ffn_sent.at[part], ffn_out.at[part], cross_send.at[k], cross_recv.at[k], across
            )
        )
    keep = pltpu.make_async_copy(small_ref, small_out.at[x, z], local.at[0])
    normed = Spread(lambda slot, part: normed_out.at[0, slot, part], normed_out, spread_send, spread_recv)
    for one in smalls + [keep]:
        one.start()
    crossing[0].start()
    for one in smalls:
        one.wait_recv()
    keep.wait()
    gain = jnp.concatenate([small_out[0, shard, 0:1] for shard in range(shards)], 1)
    for k in range(SPREAD_CHUNKS):
        for slot, place in ((x, 0), (1 - x, 1)):
            part = normed.parts[k]
            normed_out[0, place, part] = normed_with(tokens_ref[slot, part].astype(jnp.float32), gain)
        normed.first(k)
        if k >= 1:
            crossing[k].start()
    normed.near().start()
    for k in range(SPREAD_CHUNKS):
        crossing[SPREAD_CHUNKS + k].start()
        normed.second(k)
    normed.end()
    for one in crossing:
        one.wait()
    for one in smalls:
        one.wait_send()


def start(small, tokens, ffn_sent):
    shards = lax.axis_size("fsdp")
    _, rows, width = tokens.shape
    f32, bf16 = jnp.float32, jnp.bfloat16
    if not kernels_fit():
        seq_count = lax.axis_size("seq")
        every = lax.all_gather(small, ("section", "fsdp"), axis=0).reshape(2, shards, *small.shape)
        gain = every[0, :, 0].reshape(width)
        return (
            every,
            normed_with(spread_plainly(tokens).astype(f32), gain),
            flip(ffn_sent, seq_count),
        )
    place = pl.BlockSpec(memory_space=pltpu.VMEM)
    anywhere = pl.BlockSpec(memory_space=pl.ANY)
    return pl.pallas_call(
        start_kernel,
        out_shape=[
            jax.ShapeDtypeStruct((2, shards, *small.shape), f32),
            jax.ShapeDtypeStruct((2, 4, rows, width), bf16),
            jax.ShapeDtypeStruct(ffn_sent.shape, bf16),
        ],
        in_specs=[place] * 2 + [anywhere],
        out_specs=[place] * 2 + [anywhere],
        scratch_shapes=[
            pltpu.SemaphoreType.DMA((1,)),
            pltpu.SemaphoreType.DMA((2 * shards - 1,)),
            pltpu.SemaphoreType.DMA((2 * shards - 1,)),
            pltpu.SemaphoreType.DMA((SPREAD_MOVES,)),
            pltpu.SemaphoreType.DMA((SPREAD_MOVES,)),
            pltpu.SemaphoreType.DMA((FFN_CHUNKS,)),
            pltpu.SemaphoreType.DMA((FFN_CHUNKS,)),
        ],
        compiler_params=pltpu.CompilerParams(
            collective_id=21, has_side_effects=True, vmem_limit_bytes=VMEM_BYTES
        ),
        cost_estimate=lasting(55),
        name="start",
    )(small, tokens, ffn_sent)


def spread_kernel(rows_ref, out_ref, local, send, recv):
    x = lax.axis_index("section")
    _, core, _, beside, _ = peers()
    greet([core, beside])
    keeps = [
        pltpu.make_async_copy(rows_ref.at[x], out_ref.at[0, 0], local.at[0]),
        pltpu.make_async_copy(rows_ref.at[1 - x], out_ref.at[0, 1], local.at[1]),
    ]
    for one in keeps:
        one.start()
    move = Spread(lambda slot, part: rows_ref.at[x if slot == 0 else 1 - x, part], out_ref, send, recv)
    for k in range(SPREAD_CHUNKS):
        move.first(k)
    for one in keeps:
        one.wait()
    move.near().start()
    for k in range(SPREAD_CHUNKS):
        move.second(k)
    move.end()


def spread_slots(tokens):
    _, rows, width = tokens.shape
    if not kernels_fit():
        return spread_plainly(tokens)
    place = pl.BlockSpec(memory_space=pltpu.VMEM)
    return pl.pallas_call(
        spread_kernel,
        out_shape=jax.ShapeDtypeStruct((2, 4, rows, width), tokens.dtype),
        in_specs=[place],
        out_specs=place,
        scratch_shapes=[
            pltpu.SemaphoreType.DMA((2,)),
            pltpu.SemaphoreType.DMA((SPREAD_MOVES,)),
            pltpu.SemaphoreType.DMA((SPREAD_MOVES,)),
        ],
        compiler_params=pltpu.CompilerParams(
            collective_id=22, has_side_effects=True, vmem_limit_bytes=VMEM_BYTES
        ),
        cost_estimate=lasting(42),
        name="spread_slots",
    )(tokens)


def spread_plainly(tokens):
    x = lax.axis_index("section")
    _, rows, width = tokens.shape
    near = jnp.concatenate(
        [lax.dynamic_index_in_dim(tokens, x, 0, False), lax.dynamic_index_in_dim(tokens, 1 - x, 0, False)], 0
    )
    for step in chip_bits()[1:]:
        near = jnp.concatenate([near, flip(near, step)], 0)
    return jnp.stack([near, flip(near, 1)]).reshape(2, -1, rows, width)


def body(
    tokens,
    in_weight,
    conv_kernel,
    out_weight,
    gate_weight,
    up_weight,
    down_weight,
    mixer_gain,
    ffn_gain,
    cotangent,
):
    bf16, f32 = jnp.bfloat16, jnp.float32
    x_index = lax.axis_index("section")
    q_index = lax.axis_index("seq")
    seq_count = lax.axis_size("seq")
    count = lax.axis_size("section") * seq_count
    shards = lax.axis_size("fsdp")
    share = x_index * seq_count + q_index
    first_plane = x_index == 0
    width = tokens.shape[3]
    rows = tokens.shape[2]
    hidden_width = gate_weight.shape[2]
    shard_rows = width // shards
    in_columns = 3 * width // count
    channels = width // count
    ffn_columns = hidden_width // count
    ffn_pad = -(-ffn_columns // 128) * 128
    units = half_units()
    half = len(units)
    part = shard_rows // count

    other = share ^ seq_count

    def in_share(index):
        return pick_columns(in_weight[0], index, width, count)

    def out_share(index):
        return pick_rows(out_weight[0], index, count)

    def ffn_share(index):
        nothing = jnp.zeros((shard_rows, ffn_pad - ffn_columns), bf16)
        return jnp.concatenate(
            [
                pick_columns(gate_weight[0], index, hidden_width, count),
                nothing,
                pick_columns(up_weight[0], index, hidden_width, count),
                nothing,
                pick_rows(down_weight[0], index, count).reshape(shard_rows, -1),
            ],
            1,
        )

    small = jnp.concatenate(
        [
            mixer_gain.astype(f32),
            ffn_gain.astype(f32),
            conv_kernel[0].T.astype(f32),
            jnp.zeros((3, shard_rows), f32),
        ],
        0,
    )
    def over_fsdp(value):
        return lax.all_gather(value, "fsdp", axis=0, tiled=True)

    def pack_rows(value):
        return value.reshape(part, count, channels).transpose(1, 0, 2).reshape(shard_rows, channels)

    def unpack_rows(value):
        return value.reshape(-1, count, part, channels).transpose(0, 2, 1, 3).reshape(-1, width)

    def mixer_share(index):
        return jnp.concatenate([in_share(index), pack_rows(out_share(index))], 1)

    def over_mixers(value):
        value = over_fsdp(value)
        return value[:, :in_columns], unpack_rows(value[:, in_columns:])

    mixer_own = over_mixers(mixer_share(share))
    mixer_sent = flip(mixer_share(other), seq_count)
    mixer_sent, ffn_kept, ffn_sent = tie(mixer_sent, ffn_share(share), ffn_share(other))
    small, mixer_sent = tie(small, mixer_sent)
    small, normed, ffn_sent = start(small, tokens[:, 0], ffn_sent)
    mixer_across = over_mixers(mixer_sent)
    mixer_matrices = [
        [jnp.where(first_plane == kept, own, across) for own, across in zip(mixer_own, mixer_across)]
        for kept in (True, False)
    ]
    ffn_parts = [
        jnp.where(first_plane, ffn_kept, ffn_sent),
        jnp.where(first_plane, ffn_sent, ffn_kept),
    ]
    small = small.transpose(0, 2, 1, 3)
    whole = small.reshape(2, 8, width)
    taps_all = lax.dynamic_slice(
        small[:, 2:5].reshape(2, 3, shards, count, part), (0, 0, 0, share, 0), (2, 3, shards, 1, part)
    ).reshape(2, 3, shards * part)

    pair_columns = 2 * ffn_pad
    pair = over_fsdp(ffn_parts[0][:, :pair_columns])
    normed, grad_rows = tie(normed, cotangent[:, 0])
    normed, grad_units, down_part = tie(normed, spread_slots(grad_rows), ffn_parts[0][:, pair_columns:])
    down = over_fsdp(down_part.reshape(-1, width))
    ids = jnp.stack([share ^ unit ^ side for side in (0, 1) for unit in units])
    has_before = (ids % seq_count) > 0
    has_after = (ids % seq_count) < seq_count - 1
    before_pick = (ids[None, :] == (ids - 1)[:, None]) & has_before[:, None]
    after_pick = (ids[None, :] == (ids + 1)[:, None]) & has_after[:, None]

    def pick_units(mask, edge):
        return jnp.sum(jnp.where(mask[:, :, None, None], edge[None].astype(f32), 0.0), 1)

    def flat(value):
        return value.reshape(2 * half * rows, value.shape[-1])

    def in_units(value):
        return value.reshape(2, half, rows, value.shape[-1])

    def gain_row(block, kind):
        return whole[block, kind : kind + 1]

    stream = lax.dynamic_index_in_dim(tokens[:, 0], x_index, 0, False)
    saved = []
    outputs = []
    for block in range(2):
        in_matrix, out_matrix = mixer_matrices[block]
        taps = taps_all[block]
        if kernels_fit():
            projected, held, gated = mixer_forward(normed, in_matrix, taps)
            gated = flat(gated)
            if block == 1:
                gated, crossed_out = tie(gated, crossed_out)
        else:
            projected = times(flat(normed), in_matrix[:, :in_columns])
            b_gate = projected[:, :channels]
            c_gate = projected[:, channels : 2 * channels]
            x_value = projected[:, 2 * channels :]
            conv_input = (b_gate * x_value).astype(bf16).reshape(2 * half, rows, channels)
            earlier = pick_units(before_pick, conv_input[:, -2:])
            held = jnp.concatenate([earlier, conv_input.astype(f32)], 1)
            conv_out = taps[0] * held[:, :-2] + taps[1] * held[:, 1:-1] + taps[2] * held[:, 2:]
            gated = flat((c_gate.reshape(conv_out.shape) * conv_out).astype(bf16))
        (middle,), _, normed_ffn, _, _ = exchange(
            finish_middle,
            in_units(gated),
            out_matrix,
            False,
            [stream],
            [gain_row(block, 1)],
            [f32],
            0,
            True,
            1 + 2 * block,
        )
        if block == 0:
            ffn_matrices = [(pair, down), None]
        pair_matrix, down_matrix = ffn_matrices[block]
        if kernels_fit():
            pairs, hidden = ffn_forward(flat(normed_ffn), pair_matrix, ffn_pad, ffn_columns)
        else:
            pairs = times(flat(normed_ffn), pair_matrix[:, :pair_columns])
            hidden = (jax.nn.silu(pairs[:, :ffn_pad]) * pairs[:, ffn_pad:]).astype(bf16)[:, :ffn_columns]
        if block == 0:
            hidden, down, pair_value, down_value = tie(
                hidden, down, ffn_parts[1][:, :pair_columns], ffn_parts[1][:, pair_columns:].reshape(-1, width)
            )
            down_matrix = down
            ffn_matrices = [(pair, down), (over_fsdp(pair_value), over_fsdp(down_value))]
        saved.append((stream, normed, projected, held, gated, middle, normed_ffn, pairs, hidden))
        if block == 0:
            (stream,), _, normed, _, _ = exchange(
                finish_block,
                in_units(hidden),
                down_matrix,
                False,
                [middle],
                [gain_row(1, 0)],
                [bf16],
                0,
                True,
                2,
            )
            outputs.append(stream)
            crossed_out = flip(stream, seq_count)
        else:
            last_sum = (in_units(hidden), down_matrix, middle)

    upstream = lax.dynamic_index_in_dim(cotangent[:, 0], x_index, 0, False)
    stream_grads = [None, None]
    small_grads = [None, None]
    matrix_grads = [None, None]

    def over_z(value):
        return lax.psum_scatter(value, "fsdp", scatter_dimension=0, tiled=True)

    def product(left, right):
        return by_rows(row_products(left, right))

    def small_rows(mixer_gain_part, ffn_gain_part, taps_placed):
        return jnp.concatenate(
            [
                mixer_gain_part.reshape(1, width),
                ffn_gain_part.reshape(1, width),
                taps_placed,
                jnp.zeros((3, width), f32),
            ],
            0,
        )

    def small_values():
        return jnp.stack(small_grads).reshape(2, 8, shards, shard_rows).transpose(0, 2, 1, 3)

    def to_section(value, block):
        over = [((1 - block) * seq_count + seq, block * seq_count + seq) for seq in range(seq_count)]
        return lax.ppermute(value, PLANE, over)

    inside = chip_bits()[1:] + [1]
    relative = [0, seq_count]
    for bits in inside:
        relative = relative + [unit | bits for unit in relative]

    def to_owners(value, block):
        held = [value, to_section(value, block)]
        for bits in inside:
            over = [
                (block * seq_count + seq, block * seq_count + (seq ^ bits)) for seq in range(seq_count)
            ]
            held = held + [lax.ppermute(unit, PLANE, over) for unit in held]
        return held

    mixer_sum = jnp.zeros((), f32)
    for block in (1, 0):
        in_matrix, out_matrix = mixer_matrices[block]
        pair_matrix, down_matrix = ffn_matrices[block]
        taps = taps_all[block]
        (stream, normed, projected, held, gated, middle, normed_ffn, pairs, hidden) = saved[block]
        down_product = product(hidden, flat(grad_units))
        if block == 1:
            down_product, grad_units = tie(down_product, grad_units)
        else:
            grad_units, mixer_sum = tie(grad_units, mixer_sum)
        if block == 0:
            matrix_grads[1] = (down_grad, pair_grad, mixer_sum)
        down_product = down_product.reshape(shards, -1, width)
        if kernels_fit():
            grad_pairs = ffn_backward(flat(grad_units), down_matrix, pairs, ffn_pad)
            if block == 0:
                grad_pairs, crossed = tie(grad_pairs, crossed)
        else:
            gate_value, up_value = pairs[:, :ffn_pad], pairs[:, ffn_pad:]
            grad_hidden = times_transposed(flat(grad_units), down_matrix)
            grad_hidden = jnp.pad(grad_hidden, ((0, 0), (0, ffn_pad - ffn_columns)))
            sigmoid_gate = jax.nn.sigmoid(gate_value)
            grad_gate = grad_hidden * up_value * sigmoid_gate * (1.0 + gate_value * (1.0 - sigmoid_gate))
            grad_up = grad_hidden * gate_value * sigmoid_gate
            grad_pairs = jnp.concatenate([grad_gate, grad_up], 1).astype(bf16)
        grad_pairs, pair_product = tie(grad_pairs, product(flat(normed_ffn), grad_pairs))
        pair_grad = over_z(pair_product)
        (grad_middle,), (ffn_gain_part,), mixer_grad, _, _ = exchange(
            finish_gradient,
            in_units(grad_pairs),
            pair_matrix,
            True,
            [upstream, middle],
            [gain_row(block, 1)],
            [f32],
            1,
            True,
            8 - 2 * block,
        )
        if kernels_fit():
            grad_projected, taps_part = mixer_backward(mixer_grad, out_matrix, projected, held, taps)
            grad_projected, taps_part = flat(grad_projected), taps_part[:3]
            mixer_product = mixer_products(flat(normed), grad_projected, gated, flat(mixer_grad))
        else:
            grad_gated = times_transposed(flat(mixer_grad), out_matrix).reshape(2 * half, rows, channels)
            b_gate = projected[:, :channels].reshape(2 * half, rows, channels)
            c_gate = projected[:, channels : 2 * channels].reshape(2 * half, rows, channels)
            x_value = projected[:, 2 * channels :].reshape(2 * half, rows, channels)
            conv_out = taps[0] * held[:, :-2] + taps[1] * held[:, 1:-1] + taps[2] * held[:, 2:]
            grad_cgate = grad_gated * conv_out
            grad_conv = grad_gated * c_gate
            later = pick_units(after_pick, grad_conv[:, :2])
            grad_extended = jnp.concatenate([grad_conv, later], 1)
            grad_input = (
                taps[0] * grad_extended[:, 2:]
                + taps[1] * grad_extended[:, 1:-1]
                + taps[2] * grad_extended[:, :-2]
            )
            taps_part = jnp.stack(
                [jnp.sum(grad_conv * held[:, tap : tap + rows], (0, 1)) for tap in range(3)], 0
            )
            grad_projected = flat(
                jnp.concatenate([grad_input * x_value, grad_cgate, grad_input * b_gate], 2).astype(bf16)
            )
            in_grad = row_products(flat(normed), grad_projected)
            out_grad = row_products(gated, flat(mixer_grad)).reshape(shards, part, count, channels)
            out_grad = out_grad.transpose(0, 2, 1, 3).reshape(width, channels)
            mixer_product = jnp.concatenate([in_grad, out_grad], 1)
        grad_projected, mixer_product, pair_grad = tie(
            grad_projected, mixer_product, pair_grad
        )
        if block == 1 or not kernels_fit():
            mixer_sum = over_z(mixer_product)
        own_mask = (jnp.arange(count) == share)[None, None, :, None]
        taps_placed = jnp.where(own_mask, taps_part.reshape(3, shards, 1, part), 0.0).reshape(3, width)
        if block == 0 and kernels_fit():
            break
        (grad_stream,), (mixer_gain_part,), sent, down_grad, result = exchange(
            finish_gradient,
            in_units(grad_projected),
            in_matrix,
            True,
            [grad_middle, stream],
            [gain_row(block, 0)],
            [f32],
            1,
            block == 1,
            9 - 2 * block,
            product=down_product,
            extra=last_sum if block else None,
        )
        if block == 1:
            outputs.append(result)
        stream_grads[block] = grad_stream
        small_grads[block] = small_rows(mixer_gain_part, ffn_gain_part, taps_placed)
        if block == 0:
            matrix_grads[0] = (down_grad, pair_grad, mixer_sum)
        if block == 1:
            upstream = sent[0, 0]
            grad_units = sent
            crossed = flip(result, seq_count)

    def in_order(index):
        second = to_owners(matrix_grads[1][index], 1)
        first = to_owners(matrix_grads[0][index], 0)
        ordered = jnp.zeros((count, *first[0].shape), bf16)
        for unit, one, two in zip(relative, first, second):
            ordered = lax.dynamic_update_index_in_dim(
                ordered, jnp.where(first_plane, one, two), share ^ unit, 0
            )
        return ordered

    def columns_of(value, blocks):
        piece = value.reshape(count, shard_rows, blocks, shards, -1)
        return piece.transpose(1, 2, 3, 0, 4).reshape(shard_rows, -1).astype(f32)

    if kernels_fit():
        small_grads[0] = small_rows(jnp.zeros((1, width), f32), ffn_gain_part, taps_placed)
        later = matrix_grads[1]
        stream_grads[0], crossed_last, smalls, pair_grad, down_grad, mixer_sum = last_exchange(
            in_units(grad_projected),
            in_matrix,
            grad_middle,
            stream,
            gain_row(0, 0),
            small_values(),
            upstream,
            mixer_product.reshape(shards, shard_rows, -1),
            down_product,
            later[2],
            later[0],
            (pair_grad, later[1]),
        )
        gate_grad, up_grad = place_columns(pair_grad, 2, hidden_width, ffn_pad, False)
        (in_grad,) = place_columns(mixer_sum, 3, width, channels, True)
    else:
        crossed_last = flip(jnp.stack([grad.astype(bf16) for grad in stream_grads]), seq_count)
        smalls = lax.psum(small_values(), ("section", "seq", "fsdp"))
        smalls = lax.dynamic_slice(
            smalls, (x_index, lax.axis_index("fsdp"), 0, 0), (1, 1, *smalls.shape[2:])
        )[0, 0]
        down_grad, pair_grad, mixer_sum = in_order(0), in_order(1), in_order(2)
        gate_grad = columns_of(pair_grad[..., :ffn_columns], 1)
        up_grad = columns_of(pair_grad[..., ffn_pad : ffn_pad + ffn_columns], 1)
        in_grad = columns_of(mixer_sum[..., :in_columns], 3)
    down_grad = down_grad.reshape(-1, width).astype(f32)
    if kernels_fit():
        out_grad = place_rows(mixer_sum, in_columns, width)
    else:
        out_grad = unpack_rows(mixer_sum[..., in_columns:]).astype(f32)

    def by_slot(values, crossed, dtype):
        kept = jnp.where(first_plane, values[0], values[1]).astype(dtype)
        other = jnp.where(first_plane, crossed[0], crossed[1]).astype(dtype)
        return jnp.stack(
            [jnp.where(first_plane, kept, other), jnp.where(first_plane, other, kept)], 0
        )

    return (
        by_slot(outputs, (crossed_out, crossed), bf16)[None, :, None],
        by_slot(stream_grads, (crossed_last[0], crossed_last[1]), f32)[None, :, None],
        in_grad[None],
        smalls[2:5].T[None],
        out_grad[None],
        gate_grad[None],
        up_grad[None],
        down_grad[None],
        smalls[0][None],
        smalls[1][None],
    )


def solution(mesh):
    placed = (
        P(None, "fsdp", "seq", None),
        P("section", "fsdp", None),
        P("section", "fsdp", None),
        P("section", "fsdp", None),
        P("section", "fsdp", None),
        P("section", "fsdp", None),
        P("section", "fsdp", None),
        P("section", "fsdp"),
        P("section", "fsdp"),
        P(None, "fsdp", "seq", None),
    )
    return jax.shard_map(
        body,
        mesh=mesh,
        in_specs=placed,
        out_specs=(
            P("section", None, "fsdp", "seq", None),
            P("section", None, "fsdp", "seq", None),
            P("section", "fsdp", None),
            P("section", "fsdp", None),
            P("section", "fsdp", None),
            P("section", "fsdp", None),
            P("section", "fsdp", None),
            P("section", "fsdp", None),
            P("section", "fsdp"),
            P("section", "fsdp"),
        ),
        check_vma=False,
    )
```

```python
import functools

import jax
import jax.numpy as jnp
from jax import lax
from jax.experimental import pallas as pl
from jax.experimental.layout import Layout, with_layout_constraint
from jax.experimental.pallas import tpu as pltpu
from jax.sharding import PartitionSpec as P

EPSILON = 1e-05
PLANE = ("section", "seq")
MESH = pl.DeviceIdType.MESH
VMEM_BYTES = 56 * 2**20
BYTES_PER_US = 3.5e6


def lasting(us):
    return pl.CostEstimate(flops=0, bytes_accessed=int(us * BYTES_PER_US), transcendentals=0)


def tie(*values):
    return lax.optimization_barrier(values)


def kernels_fit():
    return lax.axis_size("section") == 2 and lax.axis_size("seq") == 4


def peers():
    x, q = lax.axis_index("section"), lax.axis_index("seq")
    odd = q % 2
    y = (1 - q // 2) * 2 + odd
    core = {"section": x, "seq": (q // 2) * 2 + (1 - odd)}
    across = {"section": 1 - x, "seq": q}
    beside = {"section": x, "seq": y}
    corner = {"section": x + odd * (1 - 2 * x), "seq": y * (1 - odd) + q * odd}
    return odd, core, across, beside, corner


def greet(others):
    barrier = pltpu.get_barrier_semaphore()
    for other in others:
        pl.semaphore_signal(barrier, inc=1, device_id=other, device_id_type=MESH)
    pl.semaphore_wait(barrier, len(others))


def remote_copy(source, target, send, recv, device):
    return pltpu.make_async_remote_copy(
        src_ref=source,
        dst_ref=target,
        send_sem=send,
        recv_sem=recv,
        device_id=device,
        device_id_type=MESH,
    )


def other_shards():
    z, shards = lax.axis_index("fsdp"), lax.axis_size("fsdp")
    return [{"fsdp": (z + step) % shards} for step in range(1, shards)]


class ShardSum:
    def __init__(self, product_ref, from_z, send, recv, local):
        z, shards = lax.axis_index("fsdp"), lax.axis_size("fsdp")
        self.from_z = from_z
        self.moves = [
            remote_copy(
                product_ref.at[(z + step) % shards],
                from_z.at[step - 1],
                send.at[step - 1],
                recv.at[step - 1],
                {"fsdp": (z + step) % shards},
            )
            for step in range(1, shards)
        ]
        self.keep = pltpu.make_async_copy(product_ref.at[z], from_z.at[shards - 1], local)

    def start(self):
        for one in self.moves + [self.keep]:
            one.start()

    def total(self):
        for one in self.moves:
            one.wait_recv()
        self.keep.wait()
        value = self.from_z[0].astype(jnp.float32)
        for step in range(1, self.from_z.shape[0]):
            value = value + self.from_z[step].astype(jnp.float32)
        return value.astype(self.from_z.dtype)

    def end(self):
        for one in self.moves:
            one.wait_send()


def shard_sum_scratch(product):
    shards = product.shape[0]
    return [
        pltpu.VMEM(product.shape, product.dtype),
        pltpu.SemaphoreType.DMA((shards - 1,)),
        pltpu.SemaphoreType.DMA((shards - 1,)),
        pltpu.SemaphoreType.DMA,
    ]


def sum_stages(left_ref, matrix_ref, turned, finish_rows, scratch, chunks):
    left_held, matrix_held, partial_ref, from_core, to_corner, from_corner, to_side, from_side = scratch[:8]
    send, recv, left_load, matrix_load = scratch[8:]
    odd, core, across, beside, corner = peers()
    f32 = jnp.float32
    units, step = left_ref.shape[1], left_ref.shape[2] // chunks
    depth = left_ref.shape[3]

    def load(half, k):
        return pltpu.make_async_copy(
            left_ref.at[half, :, part(k)], left_held.at[half, :, part(k)], left_load.at[half, k]
        )

    columns = matrix_held.shape[1]
    source = matrix_ref if columns == matrix_ref.shape[1] else matrix_ref.at[:, pl.ds(0, columns)]
    load_matrix = pltpu.make_async_copy(source, matrix_held, matrix_load)

    def load_all():
        load_matrix.start()
        for k in range(chunks):
            for half in (1, 0):
                load(half, k).start()

    def multiply(half, k):
        load(half, k).wait()
        left = left_held[half, :, part(k)].reshape(units * step, depth)
        right = matrix_held[:, :depth] if turned else matrix_held[...]
        value = lax.dot_general(
            left, right, (((1,), (1 if turned else 0,)), ((), ())), preferred_element_type=f32
        )
        partial_ref[half, :, part(k)] = value.astype(jnp.bfloat16).reshape(units, step, value.shape[1])

    def part(k):
        return pl.ds(k * step, step)

    def copy(slot, k, source, target, device):
        return pltpu.make_async_remote_copy(
            src_ref=source,
            dst_ref=target,
            send_sem=send.at[slot, k],
            recv_sem=recv.at[slot, k],
            device_id=device,
            device_id_type=MESH,
        )

    def core_sum(k):
        return copy(0, k, partial_ref.at[1, :, part(k)], from_core.at[:, part(k)], core)

    def corner_sum(k):
        return copy(1, k, to_corner.at[part(k)], from_corner.at[part(k)], corner)

    def across_sum(k):
        return copy(2, k, to_side.at[0, part(k)], from_side.at[0, part(k)], across)

    def beside_sum(k):
        return copy(3, k, to_side.at[1, part(k)], from_side.at[1, part(k)], beside)

    def pair_sum(unit, k):
        return partial_ref[0, unit, part(k)].astype(f32) + from_core[unit, part(k)].astype(f32)

    def send_core(k):
        if k == 0:
            load_matrix.wait()
        multiply(1, k)
        core_sum(k).start()

    def sum_corner(k):
        multiply(0, k)
        core_sum(k).wait_recv()
        to_corner[part(k)] = pair_sum(3, k).astype(jnp.bfloat16)
        corner_sum(k).start()

    def sum_sides(k):
        corner_sum(k).wait_recv()
        extra = from_corner[part(k)].astype(f32)
        to_side[0, part(k)] = (pair_sum(1, k) + jnp.where(odd == 0, extra, 0.0)).astype(jnp.bfloat16)
        to_side[1, part(k)] = (pair_sum(2, k) + jnp.where(odd == 0, 0.0, extra)).astype(jnp.bfloat16)
        across_sum(k).start()
        beside_sum(k).start()

    def total_rows(k):
        across_sum(k).wait_recv()
        beside_sum(k).wait_recv()
        finish_rows(
            k,
            part(k),
            pair_sum(0, k) + from_side[0, part(k)].astype(f32) + from_side[1, part(k)].astype(f32),
        )

    stages = [send_core, sum_corner, sum_sides, total_rows]
    return stages, [core_sum, corner_sum, across_sum, beside_sum], load_all


def ticks_of(stages, chunks, lag):
    return chunks + lag * (len(stages) - 1)


def run_tick(stages, chunks, lag, tick):
    for place, stage in enumerate(stages):
        if 0 <= tick - lag * place < chunks:
            stage(tick - lag * place)


def run_stages(stages, chunks, lag):
    for tick in range(ticks_of(stages, chunks, lag)):
        run_tick(stages, chunks, lag, tick)


def sum_scratch(left, matrix, turned, chunks):
    bf16 = jnp.bfloat16
    _, units, rows, depth = left.shape
    width = matrix.shape[0] if turned else matrix.shape[1]
    columns = depth if turned and depth % 128 == 0 else matrix.shape[1]
    return [
        pltpu.VMEM(left.shape, bf16),
        pltpu.VMEM((matrix.shape[0], columns), bf16),
        pltpu.VMEM((2, units, rows, width), bf16),
        pltpu.VMEM((units, rows, width), bf16),
        pltpu.VMEM((rows, width), bf16),
        pltpu.VMEM((rows, width), bf16),
        pltpu.VMEM((2, rows, width), bf16),
        pltpu.VMEM((2, rows, width), bf16),
        pltpu.SemaphoreType.DMA((4, chunks)),
        pltpu.SemaphoreType.DMA((4, chunks)),
        pltpu.SemaphoreType.DMA((2, chunks)),
        pltpu.SemaphoreType.DMA,
    ]


SUM_REFS = 12


def exchange_kernel(
    finish, turned, row_ins, shared_ins, row_outs, sum_outs, gather, product, extra, chunks, *refs
):
    refs = list(refs)
    left_ref, matrix_ref = refs.pop(0), refs.pop(0)
    ins = [refs.pop(0) for _ in range(row_ins)]
    shared = [refs.pop(0) for _ in range(shared_ins)]
    product_ref = refs.pop(0) if product else None
    extra_left, extra_matrix, extra_middle = [refs.pop(0) for _ in range(3)] if extra else [None] * 3
    outs = [refs.pop(0) for _ in range(row_outs)]
    sums = [refs.pop(0) for _ in range(sum_outs)]
    product_out = refs.pop(0) if product else None
    extra_out = refs.pop(0) if extra else None
    spread_ref = refs.pop(0) if gather else None
    sum_refs, refs = refs[:SUM_REFS], refs[SUM_REFS:]
    (send, recv), refs = refs[:2], refs[2:]
    product_refs, extra_refs = (refs[:4], refs[4:]) if product else ([], refs)
    odd, core, across, beside, corner = peers()
    f32 = jnp.float32
    step = left_ref.shape[2] // chunks

    def part(k):
        return pl.ds(k * step, step)

    def copy(slot, k, source, target, device):
        return pltpu.make_async_remote_copy(
            src_ref=source,
            dst_ref=target,
            send_sem=send.at[slot, k],
            recv_sem=recv.at[slot, k],
            device_id=device,
            device_id_type=MESH,
        )

    def across_out(k):
        return copy(0, k, spread_ref.at[0, 0, part(k)], spread_ref.at[0, 1, part(k)], across)

    def beside_out(k):
        return copy(1, k, spread_ref.at[0, 0, part(k)], spread_ref.at[0, 2, part(k)], beside)

    def corner_out(k):
        return copy(2, k, spread_ref.at[0, 1 + odd, part(k)], spread_ref.at[0, 3, part(k)], corner)

    def core_out(k):
        return copy(3, k, spread_ref.at[0, :, part(k)], spread_ref.at[1, :, part(k)], core)

    def finish_rows(k, rows, total):
        values, added, sent = finish(
            total, *[ref[rows].astype(f32) for ref in ins], *[ref[...] for ref in shared]
        )
        for ref, value in zip(outs, values):
            ref[rows] = value.astype(ref.dtype)
        for ref, value in zip(sums, added):
            ref[...] = value if k == 0 else ref[...] + value
        if gather:
            spread_ref[0, 0, rows] = sent
            across_out(k).start()
            beside_out(k).start()

    def pass_corner(k):
        across_out(k).wait_recv()
        beside_out(k).wait_recv()
        corner_out(k).start()

    def pass_core(k):
        corner_out(k).wait_recv()
        core_out(k).start()

    def arrive(k):
        core_out(k).wait_recv()

    stages, copies, load_all = sum_stages(left_ref, matrix_ref, turned, finish_rows, sum_refs, chunks)
    load_all()
    if gather:
        stages = stages + [pass_corner, pass_core, arrive]
        copies = copies + [across_out, beside_out, corner_out, core_out]
    if extra:

        def extra_rows(k, rows, total):
            extra_out[rows] = (extra_middle[rows] + total).astype(extra_out.dtype)

        later, more, load_more = sum_stages(
            extra_left, extra_matrix, False, extra_rows, extra_refs, chunks
        )
        load_more()
        stages = stages[:1] + [lambda k, a=a, b=b: (a(k), b(k)) for a, b in zip(stages[1:5], later)] + stages[5:]
        copies = copies + more
    greet([core, across, beside] + (other_shards() if product else []))
    if product:
        shard_sum = ShardSum(product_ref, *product_refs)
        shard_sum.start()
    run_stages(stages, chunks, 1 if extra or left_ref.shape[3] > 1024 else 2)
    if product:
        product_out[...] = shard_sum.total()
        shard_sum.end()
    for k in range(chunks):
        for one in copies:
            one(k).wait_send()


def exchange(
    finish,
    left,
    matrix,
    turned,
    row_ins,
    shared_ins,
    row_outs,
    sum_outs,
    gather,
    number,
    product=None,
    extra=None,
    chunks=4,
):
    _, units, rows, _ = left.shape
    width = matrix.shape[0] if turned else matrix.shape[1]
    if not kernels_fit():
        return exchange_plainly(
            finish, left, matrix, turned, row_ins, shared_ins, row_outs, gather, product, extra
        )
    bf16 = jnp.bfloat16
    shapes = [jax.ShapeDtypeStruct((rows, width), dtype) for dtype in row_outs]
    shapes += [jax.ShapeDtypeStruct((1, width), jnp.float32)] * sum_outs
    shapes += [] if product is None else [jax.ShapeDtypeStruct(product.shape[1:], product.dtype)]
    shapes += [] if extra is None else [jax.ShapeDtypeStruct((rows, width), bf16)]
    shapes += [jax.ShapeDtypeStruct((2, units, rows, width), bf16)] * gather
    more = ([] if product is None else [product]) + list(extra or ())
    place, anywhere = pl.BlockSpec(memory_space=pltpu.VMEM), pl.BlockSpec(memory_space=pl.ANY)
    result = pl.pallas_call(
        functools.partial(
            exchange_kernel,
            finish,
            turned,
            len(row_ins),
            len(shared_ins),
            len(row_outs),
            sum_outs,
            gather,
            product is not None,
            extra is not None,
            chunks,
        ),
        out_shape=shapes,
        in_specs=[anywhere] * 2
        + [place] * (len(row_ins) + len(shared_ins))
        + ([] if product is None else [anywhere])
        + ([] if extra is None else [anywhere, anywhere, place]),
        out_specs=[place] * len(shapes),
        scratch_shapes=sum_scratch(left, matrix, turned, chunks)
        + [pltpu.SemaphoreType.DMA((4, chunks))] * 2
        + ([] if product is None else shard_sum_scratch(product))
        + ([] if extra is None else sum_scratch(extra[0], extra[1], False, chunks)),
        compiler_params=pltpu.CompilerParams(
            collective_id=number, has_side_effects=True, vmem_limit_bytes=VMEM_BYTES
        ),
        cost_estimate=lasting(66 if gather else 38),
        name=("exchange_%d" % number),
    )(left, matrix, *row_ins, *shared_ins, *more)
    result = list(result)
    rows_done = [result.pop(0) for _ in row_outs]
    sums = [result.pop(0) for _ in range(sum_outs)]
    product = None if product is None else result.pop(0)
    extra = None if extra is None else result.pop(0)
    return rows_done, sums, (result.pop(0) if gather else None), product, extra


def plane_total(left, matrix, turned):
    multiply = times_transposed if turned else times
    matrix = matrix[:, : left.shape[3]] if turned else matrix
    near, far = [multiply(half.reshape(-1, half.shape[2]), matrix).astype(jnp.bfloat16) for half in left]
    total = near.astype(jnp.float32) + flip(far, 1).astype(jnp.float32)
    return collect(total, (lax.axis_index("seq") % 2) == 1)


def exchange_plainly(finish, left, matrix, turned, row_ins, shared_ins, row_outs, gather, product, extra):
    total = plane_total(left, matrix, turned)
    rows, sums, sent = finish(total, *[value.astype(jnp.float32) for value in row_ins], *shared_ins)
    rows = [value.astype(dtype) for value, dtype in zip(rows, row_outs)]
    if product is not None:
        product = lax.psum_scatter(
            product.reshape(-1, product.shape[2]), "fsdp", scatter_dimension=0, tiled=True
        )
    if extra is not None:
        extra = (plane_total(extra[0], extra[1], False) + extra[2]).astype(jnp.bfloat16)
    if gather:
        odd = (lax.axis_index("seq") % 2) == 1
        sent = jnp.stack(spread(sent, odd)).reshape(*left.shape[:3], -1)
    return rows, sums, sent, product, extra


def finish_middle(total, stream, gain):
    middle = stream + total
    return [middle], [], (middle * rms_scale(middle) * gain).astype(jnp.bfloat16)


def finish_block(total, middle, gain):
    result = (middle + total).astype(jnp.bfloat16)
    stream = result.astype(jnp.float32)
    return [result], [], (stream * rms_scale(stream) * gain).astype(jnp.bfloat16)


def finish_gradient(total, upstream, stream, gain):
    scale = rms_scale(stream)
    weighted = gain * total
    grad = (
        upstream
        + scale * weighted
        - stream * scale**3 * jnp.mean(weighted * stream, -1, keepdims=True)
    )
    added = jnp.sum(total * stream * scale, 0, keepdims=True)
    return [grad], [added], grad.astype(jnp.bfloat16)


LAST_CHUNKS = 4
OWNER_CHUNKS = (6, 1, 1)


def last_kernel(
    left_ref,
    matrix_ref,
    upstream_ref,
    stream_ref,
    gain_ref,
    smalls_ref,
    later_ref,
    product_ref,
    down_product_ref,
    mixer_ref,
    down_ref,
    pair0_ref,
    pair1_ref,
    grad_ref,
    crossed_ref,
    smalls_out,
    pair_out,
    down_out,
    mixer_out,
    *scratch,
):
    sum_refs, scratch = scratch[:SUM_REFS], scratch[SUM_REFS:]
    pair_both, down_both, mixer_both, grad_low, gain_sum = scratch[:5]
    small_sum, small_sent, small_side, small_z = scratch[5:9]
    local, own_send, own_recv, small_send, small_recv, cross_send, cross_recv = scratch[9:16]
    mixer_sum = ShardSum(product_ref, *scratch[16:20])
    down_sum = ShardSum(down_product_ref, *scratch[20:])
    x, q, z = lax.axis_index("section"), lax.axis_index("seq"), lax.axis_index("fsdp")
    shards = lax.axis_size("fsdp")
    _, core, across, beside, _ = peers()
    f32, bf16 = jnp.float32, jnp.bfloat16
    others = other_shards()
    share = x * 4 + q
    share_across = (1 - x) * 4 + q
    beside_q = (1 - q // 2) * 2 + q % 2
    share_beside = x * 4 + beside_q
    share_corner = (1 - x) * 4 + beside_q

    def remote(source, target, send, recv, device):
        return pltpu.make_async_remote_copy(
            src_ref=source,
            dst_ref=target,
            send_sem=send,
            recv_sem=recv,
            device_id=device,
            device_id_type=MESH,
        )

    class Owners:
        def __init__(self, place, both, out):
            self.place, self.both, self.out = place, both, out
            self.step = both.shape[1] // OWNER_CHUNKS[place]
            self.chunks = range(OWNER_CHUNKS[place])

        def move(self, slot, k, source, target, device):
            part = pl.ds(k * self.step, self.step)
            place = self.place
            return remote(
                source.at[part],
                self.out.at[target, part],
                own_send.at[place, slot, k],
                own_recv.at[place, slot, k],
                device,
            )

        def cross(self, k):
            return self.move(0, k, self.both.at[1 - x], share, across)

        def side(self, k):
            return self.move(1, k, self.both.at[x], share, beside)

        def near(self, k):
            return self.move(2, k, self.both.at[x], share, core)

        def side_across(self, k):
            return self.move(3, k, self.out.at[share_across], share_across, beside)

        def near_across(self, k):
            return self.move(4, k, self.out.at[share_across], share_across, core)

        def near_beside(self, k):
            return self.move(5, k, self.out.at[share_beside], share_beside, core)

        def near_corner(self, k):
            return self.move(6, k, self.out.at[share_corner], share_corner, core)

        def keep(self):
            return pltpu.make_async_copy(self.both.at[x], self.out.at[share], local.at[4 + self.place])

        def first(self, k):
            self.cross(k).start()
            self.side(k).start()
            self.near(k).start()

        def second(self, k):
            self.cross(k).wait_recv()
            self.side_across(k).start()
            self.near_across(k).start()

        def third(self, k):
            self.side(k).wait_recv()
            self.near_beside(k).start()

        def fourth(self, k):
            self.side_across(k).wait_recv()
            self.near_corner(k).start()

        def end(self):
            for k in self.chunks:
                for one in (self.near, self.near_across, self.near_beside, self.near_corner):
                    one(k).wait_recv()
                for one in (
                    self.cross,
                    self.side,
                    self.near,
                    self.side_across,
                    self.near_across,
                    self.near_beside,
                    self.near_corner,
                ):
                    one(k).wait_send()
            self.keep().wait()

    pair = Owners(0, pair_both, pair_out)
    down = Owners(1, down_both, down_out)
    mixer = Owners(2, mixer_both, mixer_out)

    def finish_rows(k, rows, total):
        (grad,), (added,), sent = finish_gradient(
            total, upstream_ref[rows].astype(f32), stream_ref[rows].astype(f32), gain_ref[...]
        )
        grad_ref[rows] = grad
        grad_low[rows] = sent
        gain_sum[...] = added if k == 0 else gain_sum[...] + added

    stages, copies, load_all = sum_stages(left_ref, matrix_ref, True, finish_rows, sum_refs, LAST_CHUNKS)
    load_all()
    loads = [
        pltpu.make_async_copy(pair0_ref, pair_both.at[0], local.at[0]),
        pltpu.make_async_copy(pair1_ref, pair_both.at[1], local.at[1]),
        pltpu.make_async_copy(down_ref, down_both.at[1], local.at[2]),
        pltpu.make_async_copy(mixer_ref, mixer_both.at[1], local.at[3]),
    ]
    for one in loads:
        one.start()
    greet([core, across, beside] + others)
    mixer_sum.start()
    later = remote(later_ref, crossed_ref.at[1], cross_send.at[1], cross_recv.at[1], across)
    later.start()
    for one in loads[:2]:
        one.wait()
    pair.keep().start()
    for tick in range(ticks_of(stages, LAST_CHUNKS, 1)):
        run_tick(stages, LAST_CHUNKS, 1, tick)
        if tick in pair.chunks:
            pair.first(tick)
        if tick == 1:
            down_sum.start()

    small_rows = smalls_ref.shape[3]
    small_sum[...] = smalls_ref[...]
    for shard in range(shards):
        small_sum[0, shard, 0:1] += gain_sum[:, shard * small_rows : (shard + 1) * small_rows]

    def small_move(step, device):
        return remote(small_sent.at[step], small_side.at[step], small_send.at[step], small_recv.at[step], device)

    for step, device in enumerate((core, across, beside)):
        small_sent[step] = small_sum[...]
        small_move(step, device).start()
        pair.second(step)
        small_move(step, device).wait()
        small_sum[...] += small_side[step]
    small_moves = [
        remote(
            small_sum.at[x, (z + step + 1) % shards],
            small_z.at[step],
            small_send.at[3 + step],
            small_recv.at[3 + step],
            device,
        )
        for step, device in enumerate(others)
    ]
    for one in small_moves:
        one.start()

    mixer_both[0] = mixer_sum.total()
    loads[3].wait()
    mixer.keep().start()
    mixer.first(0)
    for k in pair.chunks[3:]:
        pair.second(k)
    mixer.second(0)
    down_both[0] = down_sum.total()
    loads[2].wait()
    down.keep().start()
    down.first(0)
    cross = remote(grad_low, crossed_ref.at[0], cross_send.at[0], cross_recv.at[0], across)
    cross.start()
    for k in pair.chunks:
        pair.third(k)
    mixer.third(0)
    down.second(0)
    for k in pair.chunks:
        pair.fourth(k)
    mixer.fourth(0)
    down.third(0)
    down.fourth(0)
    small_total = small_sum[x, z]
    for step, one in enumerate(small_moves):
        one.wait()
        small_total = small_total + small_z[step]
    smalls_out[...] = small_total
    for owners in (pair, down, mixer):
        owners.end()
    cross.wait()
    later.wait()
    mixer_sum.end()
    down_sum.end()
    for k in range(LAST_CHUNKS):
        for one in copies:
            one(k).wait_send()


def last_exchange(left, matrix, upstream, stream, gain, smalls, later, product, down_product, mixer, down, pairs):
    _, units, rows, _ = left.shape
    width = matrix.shape[0]
    shards, shard_rows, mixer_columns = product.shape
    bf16, f32 = jnp.bfloat16, jnp.float32
    count = 2 * units
    vmem = pl.BlockSpec(memory_space=pltpu.VMEM)
    anywhere = pl.BlockSpec(memory_space=pl.ANY)
    return pl.pallas_call(
        last_kernel,
        out_shape=[
            jax.ShapeDtypeStruct((rows, width), f32),
            jax.ShapeDtypeStruct((2, rows, width), bf16),
            jax.ShapeDtypeStruct(smalls.shape[2:], f32),
            jax.ShapeDtypeStruct((count, *pairs[0].shape), bf16),
            jax.ShapeDtypeStruct((count, *down.shape), bf16),
            jax.ShapeDtypeStruct((count, shard_rows, mixer_columns), bf16),
        ],
        in_specs=[anywhere] * 2 + [vmem] * 5 + [anywhere] * 6,
        out_specs=[vmem] * 3 + [anywhere] * 3,
        scratch_shapes=sum_scratch(left, matrix, True, LAST_CHUNKS)
        + [
            pltpu.VMEM((2, *pairs[0].shape), bf16),
            pltpu.VMEM((2, *down.shape), bf16),
            pltpu.VMEM((2, shard_rows, mixer_columns), bf16),
            pltpu.VMEM((rows, width), bf16),
            pltpu.VMEM((1, width), f32),
            pltpu.VMEM(smalls.shape, f32),
            pltpu.VMEM((3, *smalls.shape), f32),
            pltpu.VMEM((3, *smalls.shape), f32),
            pltpu.VMEM((shards - 1, *smalls.shape[2:]), f32),
            pltpu.SemaphoreType.DMA((7,)),
            pltpu.SemaphoreType.DMA((3, 7, max(OWNER_CHUNKS))),
            pltpu.SemaphoreType.DMA((3, 7, max(OWNER_CHUNKS))),
            pltpu.SemaphoreType.DMA((2 + shards,)),
            pltpu.SemaphoreType.DMA((2 + shards,)),
            pltpu.SemaphoreType.DMA((2,)),
            pltpu.SemaphoreType.DMA((2,)),
        ]
        + shard_sum_scratch(product)
        + shard_sum_scratch(down_product),
        compiler_params=pltpu.CompilerParams(
            collective_id=20, has_side_effects=True, vmem_limit_bytes=VMEM_BYTES
        ),
        cost_estimate=lasting(130),
        name="last_exchange",
    )(left, matrix, upstream, stream, gain, smalls, later, product, down_product, mixer, down, *pairs)


def place_kernel(blocks, width, stride, stack_ref, *outs):
    shards = lax.axis_size("fsdp")
    count = stack_ref.shape[0]
    part = width // shards // count
    for block in range(blocks):
        pieces = []
        for shard in range(shards):
            start = block * stride + shard * part
            pieces += [stack_ref[share, :, start : start + part] for share in range(count)]
        value = jnp.concatenate(pieces, 1).astype(jnp.float32)
        if len(outs) == 1:
            outs[0][:, block * width : (block + 1) * width] = value
        else:
            outs[block][...] = value


def place_rows_kernel(first, stack_ref, out_ref):
    channels = stack_ref.shape[2] - first
    blocks = out_ref.shape[1] // channels
    part = stack_ref.shape[1] // blocks
    for share in range(stack_ref.shape[0]):
        pieces = [stack_ref[share, block * part : (block + 1) * part, first:] for block in range(blocks)]
        out_ref[share * part : (share + 1) * part] = jnp.concatenate(pieces, 1).astype(jnp.float32)


def place_rows(stack, first, width):
    (value,) = local_call(
        functools.partial(place_rows_kernel, first),
        [((stack.shape[1], width), jnp.float32)],
        [],
        5,
        "place_rows",
        stack,
    )
    return value


def place_columns(stack, blocks, width, stride, together):
    count, rows, columns = stack.shape
    step = 96 if rows % 96 == 0 else rows
    widths = [blocks * width] if together else [width] * blocks
    return pl.pallas_call(
        functools.partial(place_kernel, blocks, width, stride),
        grid=(rows // step,),
        out_shape=[jax.ShapeDtypeStruct((rows, each), jnp.float32) for each in widths],
        in_specs=[pl.BlockSpec((count, step, columns), lambda i: (0, i, 0))],
        out_specs=[pl.BlockSpec((step, each), lambda i: (i, 0)) for each in widths],
        compiler_params=pltpu.CompilerParams(vmem_limit_bytes=VMEM_BYTES),
        cost_estimate=lasting(14),
        name="place_columns",
    )(stack)


def local_call(kernel, outs, scratch, us, name, *operands, far=()):
    place = pl.BlockSpec(memory_space=pltpu.VMEM)
    places = [pl.BlockSpec(memory_space=pl.ANY) if i in far else place for i in range(len(operands))]
    return pl.pallas_call(
        kernel,
        out_shape=[jax.ShapeDtypeStruct(shape, dtype) for shape, dtype in outs],
        in_specs=places,
        out_specs=[place] * len(outs),
        scratch_shapes=scratch,
        compiler_params=pltpu.CompilerParams(vmem_limit_bytes=VMEM_BYTES),
        cost_estimate=lasting(us),
        name=name,
    )(*operands)


def unit_place(difference):
    return difference // 4 + (difference // 2 % 2) * 2 + (difference % 2) * 4


def unit_bits(place):
    return (place % 2) * 4 + (place // 2 % 2) * 2 + place // 4


def either(left, right):
    total = 0
    for bit in (1, 2, 4):
        one, two = left // bit % 2, right // bit % 2
        total = total + bit * (one + two - 2 * one * two)
    return total


def neighbour(place, step):
    share = lax.axis_index("section") * 4 + lax.axis_index("seq")
    device = either(share, unit_bits(place))
    seq = device % 4 + step
    inside = jnp.where((seq >= 0) & (seq < 4), 1.0, 0.0)
    seq = (seq + 4) % 4
    return unit_place(either(share, device // 4 * 4 + seq)), inside


def conv_parts(held_ref, place):
    f32 = jnp.float32
    before, inside = neighbour(place, -1)
    here = held_ref[place]
    rows = here.shape[0]
    edge = held_ref[before, rows - 2 : rows] * inside
    whole = jnp.concatenate([edge.astype(f32), here], 0)
    return whole[:rows], whole[1 : rows + 1], here


def load_units(source, target, sems):
    def load(place):
        return pltpu.make_async_copy(source.at[place], target.at[place], sems.at[place])

    for place in range(8):
        load(place).start()
    return lambda place: load(place).wait()


def mixer_forward_kernel(
    channels, normed_far, matrix_ref, taps_ref, projected_ref, held_ref, gated_ref, normed_ref, sems
):
    f32, bf16 = jnp.float32, jnp.bfloat16
    wait_unit = load_units(normed_far, normed_ref, sems)

    def project(place, carry):
        wait_unit(place)
        value = jnp.dot(
            normed_ref[place], matrix_ref[:, : 3 * channels], preferred_element_type=f32
        )
        projected_ref[place] = value
        held_ref[place] = (value[:, :channels] * value[:, 2 * channels :]).astype(bf16).astype(f32)
        return carry

    lax.fori_loop(0, 8, project, 0)

    def convolve(place, carry):
        first, second, third = conv_parts(held_ref, place)
        value = taps_ref[0:1] * first + taps_ref[1:2] * second + taps_ref[2:3] * third
        gated_ref[place] = (projected_ref[place, :, channels : 2 * channels] * value).astype(bf16)
        return carry

    lax.fori_loop(0, 8, convolve, 0)


def mixer_forward(normed, matrix, taps):
    rows = normed.shape[2]
    channels = taps.shape[1]
    f32, bf16 = jnp.float32, jnp.bfloat16
    return local_call(
        functools.partial(mixer_forward_kernel, channels),
        [((8, rows, 3 * channels), f32), ((8, rows, channels), f32), ((8, rows, channels), bf16)],
        [pltpu.VMEM((8, *normed.shape[2:]), bf16), pltpu.SemaphoreType.DMA((8,))],
        10,
        "mixer_forward",
        normed.reshape(8, rows, -1),
        matrix,
        taps,
        far=(0,),
    )


def mixer_backward_kernel(
    channels,
    grad_far,
    matrix_ref,
    projected_far,
    held_ref,
    taps_ref,
    out_ref,
    taps_out,
    conv_grad,
    gate_grad,
    grad_ref,
    projected_ref,
    grad_sems,
    projected_sems,
):
    f32, bf16 = jnp.float32, jnp.bfloat16
    wait_grad = load_units(grad_far, grad_ref, grad_sems)
    wait_projected = load_units(projected_far, projected_ref, projected_sems)

    def to_gates(place, carry):
        wait_grad(place)
        wait_projected(place)
        grad = lax.dot_general(
            grad_ref[place], matrix_ref[...], (((1,), (1,)), ((), ())), preferred_element_type=f32
        )
        first, second, third = conv_parts(held_ref, place)
        value = taps_ref[0:1] * first + taps_ref[1:2] * second + taps_ref[2:3] * third
        back = grad * projected_ref[place, :, channels : 2 * channels]
        gate_grad[place] = grad * value
        conv_grad[place] = back
        added = [jnp.sum(back * shifted, 0, keepdims=True) for shifted in (first, second, third)]
        return carry + jnp.concatenate(added + [jnp.zeros((5, channels), f32)], 0)

    taps_out[...] = lax.fori_loop(0, 8, to_gates, jnp.zeros((8, channels), f32))

    def to_inputs(place, carry):
        after, inside = neighbour(place, 1)
        here = conv_grad[place]
        rows = here.shape[0]
        whole = jnp.concatenate([here, conv_grad[after, 0:2] * inside], 0)
        grad = (
            taps_ref[0:1] * whole[2:] + taps_ref[1:2] * whole[1 : rows + 1] + taps_ref[2:3] * here
        )
        out_ref[place] = jnp.concatenate(
            [
                grad * projected_ref[place, :, 2 * channels :],
                gate_grad[place],
                grad * projected_ref[place, :, :channels],
            ],
            1,
        ).astype(bf16)
        return carry

    lax.fori_loop(0, 8, to_inputs, 0)


def mixer_backward(grads, matrix, projected, held, taps):
    rows = grads.shape[2]
    channels = taps.shape[1]
    f32, bf16 = jnp.float32, jnp.bfloat16
    return local_call(
        functools.partial(mixer_backward_kernel, channels),
        [((8, rows, 3 * channels), bf16), ((8, channels), f32)],
        [
            pltpu.VMEM((8, rows, channels), f32),
            pltpu.VMEM((8, rows, channels), f32),
            pltpu.VMEM((8, *grads.shape[2:]), bf16),
            pltpu.VMEM(projected.shape, f32),
            pltpu.SemaphoreType.DMA((8,)),
            pltpu.SemaphoreType.DMA((8,)),
        ],
        12,
        "mixer_backward",
        grads.reshape(8, rows, -1),
        matrix,
        projected,
        held,
        taps,
        far=(0, 2),
    )


def ffn_forward_kernel(pad, normed_ref, matrix_ref, pairs_ref, hidden_ref):
    pairs = jnp.dot(normed_ref[...], matrix_ref[:, : 2 * pad], preferred_element_type=jnp.float32)
    pairs_ref[...] = pairs
    gate, up = pairs[:, :pad], pairs[:, pad:]
    hidden = gate * jax.nn.sigmoid(gate) * up
    hidden_ref[...] = hidden[:, : hidden_ref.shape[1]].astype(jnp.bfloat16)


def ffn_forward(normed, matrix, pad, columns):
    count, width = normed.shape
    step = 512
    return pl.pallas_call(
        functools.partial(ffn_forward_kernel, pad),
        grid=(count // step,),
        out_shape=[
            jax.ShapeDtypeStruct((count, 2 * pad), jnp.float32),
            jax.ShapeDtypeStruct((count, columns), jnp.bfloat16),
        ],
        in_specs=[
            pl.BlockSpec((step, width), lambda i: (i, 0)),
            pl.BlockSpec(matrix.shape, lambda i: (0, 0)),
        ],
        out_specs=[
            pl.BlockSpec((step, 2 * pad), lambda i: (i, 0)),
            pl.BlockSpec((step, columns), lambda i: (i, 0)),
        ],
        compiler_params=pltpu.CompilerParams(vmem_limit_bytes=VMEM_BYTES),
        cost_estimate=lasting(16),
        name="ffn_forward",
    )(normed, matrix)


def ffn_backward_kernel(pad, grad_ref, matrix_ref, pairs_ref, out_ref):
    grad = lax.dot_general(
        grad_ref[...], matrix_ref[...], (((1,), (1,)), ((), ())), preferred_element_type=jnp.float32
    )
    extra = pad - grad.shape[1]
    if extra:
        grad = jnp.concatenate([grad, jnp.zeros((grad.shape[0], extra), jnp.float32)], 1)
    gate, up = pairs_ref[:, :pad], pairs_ref[:, pad:]
    sigmoid = jax.nn.sigmoid(gate)
    out_ref[:, :pad] = (grad * up * sigmoid * (1.0 + gate * (1.0 - sigmoid))).astype(jnp.bfloat16)
    out_ref[:, pad:] = (grad * gate * sigmoid).astype(jnp.bfloat16)


def ffn_backward(grads, matrix, pairs, pad):
    count, width = grads.shape
    step = 512
    return pl.pallas_call(
        functools.partial(ffn_backward_kernel, pad),
        grid=(count // step,),
        out_shape=jax.ShapeDtypeStruct((count, 2 * pad), jnp.bfloat16),
        in_specs=[
            pl.BlockSpec((step, width), lambda i: (i, 0)),
            pl.BlockSpec(matrix.shape, lambda i: (0, 0)),
            pl.BlockSpec((step, 2 * pad), lambda i: (i, 0)),
        ],
        out_specs=pl.BlockSpec((step, 2 * pad), lambda i: (i, 0)),
        compiler_params=pltpu.CompilerParams(vmem_limit_bytes=VMEM_BYTES),
        cost_estimate=lasting(16),
        name="ffn_backward",
    )(grads, matrix, pairs)


def mixer_product_kernel(
    shards, normed_far, projected_ref, gated_ref, grad_far, out_ref, normed_ref, grad_ref, sems
):
    f32, bf16 = jnp.float32, jnp.bfloat16
    blocks = normed_ref.shape[0]
    step = normed_ref.shape[2]
    loads = [
        pltpu.make_async_copy(normed_far.at[:, pl.ds(i * step, step)], normed_ref.at[i], sems.at[i])
        for i in range(blocks)
    ]
    loads.append(pltpu.make_async_copy(grad_far, grad_ref, sems.at[blocks]))
    for one in loads:
        one.start()
    turned = (((0,), (0,)), ((), ()))
    columns = projected_ref.shape[1]
    width, channels = grad_ref.shape[1], gated_ref.shape[1]
    for i in range(blocks):
        loads[i].wait()
        out_ref[i * step : (i + 1) * step, :columns] = lax.dot_general(
            normed_ref[i], projected_ref[...], turned, preferred_element_type=f32
        ).astype(bf16)
    loads[blocks].wait()
    value = lax.dot_general(gated_ref[...], grad_ref[...], turned, preferred_element_type=f32)
    part = channels // shards
    pieces = width // channels
    for shard in range(shards):
        for block in range(pieces):
            row = (shard * pieces + block) * part
            out_ref[row : row + part, columns:] = value[
                shard * part : (shard + 1) * part, block * channels : (block + 1) * channels
            ].astype(bf16)


def mixer_products(normed, projected_grad, gated, grad):
    width, columns, channels = normed.shape[1], projected_grad.shape[1], gated.shape[1]
    shards = lax.axis_size("fsdp")
    blocks = width // 256
    (value,) = local_call(
        functools.partial(mixer_product_kernel, shards),
        [((width, columns + channels), jnp.bfloat16)],
        [
            pltpu.VMEM((blocks, normed.shape[0], width // blocks), jnp.bfloat16),
            pltpu.VMEM(grad.shape, jnp.bfloat16),
            pltpu.SemaphoreType.DMA((blocks + 1,)),
        ],
        14,
        "mixer_products",
        normed,
        projected_grad,
        gated,
        grad,
        far=(0, 3),
    )
    return value


def flip(value, bits):
    count = lax.axis_size("section") * lax.axis_size("seq")
    return lax.ppermute(value, PLANE, [(source, source ^ bits) for source in range(count)])


def flip_by_core(value, even_bits, odd_bits):
    count = lax.axis_size("section") * lax.axis_size("seq")
    pairs = [(source, source ^ (odd_bits if source & 1 else even_bits)) for source in range(count)]
    return lax.ppermute(value, PLANE, pairs)


def chip_bits():
    bits = [lax.axis_size("seq")]
    step = lax.axis_size("seq") // 2
    while step > 1:
        bits.append(step)
        step //= 2
    return bits


def half_units():
    units = [0]
    for bits in chip_bits():
        units = units + [unit | bits for unit in units]
    return units


def spread_chips(own, odd):
    bits = chip_bits()
    if len(bits) == 2:
        first = flip(own, bits[0])
        second = flip(own, bits[1])
        third = flip_by_core(jnp.where(odd, second, first), bits[1], bits[0])
        return jnp.concatenate([own, first, second, third], 0)
    held = own
    for step in bits:
        held = jnp.concatenate([held, flip(held, step)], 0)
    return held


def spread(own, odd):
    near = spread_chips(own, odd)
    return near, flip(near, 1)


def collect(near, odd):
    bits = chip_bits()
    if len(bits) == 2:
        rows = near.shape[0] // 4
        held = near
        third = flip_by_core(held[3 * rows :].astype(jnp.bfloat16), bits[1], bits[0]).astype(jnp.float32)
        first = held[rows : 2 * rows] + jnp.where(odd, 0.0, third)
        second = held[2 * rows : 3 * rows] + jnp.where(odd, third, 0.0)
        first = flip(first.astype(jnp.bfloat16), bits[0]).astype(jnp.float32)
        second = flip(second.astype(jnp.bfloat16), bits[1]).astype(jnp.float32)
        return held[:rows] + first + second
    held = near
    for step in reversed(bits):
        rows = held.shape[0] // 2
        held = held[:rows] + flip(held[rows:].astype(jnp.bfloat16), step).astype(jnp.float32)
    return held


def rms_scale(stream):
    return lax.rsqrt(jnp.mean(stream * stream, -1, keepdims=True) + EPSILON)


def times(left, matrix):
    return jnp.dot(left, matrix, preferred_element_type=jnp.float32)


def times_transposed(left, matrix):
    return lax.dot_general(
        left, matrix, (((1,), (1,)), ((), ())), preferred_element_type=jnp.float32
    )


def by_rows(value):
    return with_layout_constraint(value, Layout(major_to_minor=tuple(range(value.ndim))))


def row_products(left, right):
    return lax.dot_general(
        left, right, (((0,), (0,)), ((), ())), preferred_element_type=jnp.float32
    ).astype(jnp.bfloat16)


def normed_with(stream, gain):
    return (stream * rms_scale(stream) * gain).astype(jnp.bfloat16)


def pick_columns(matrix, share, width, count):
    shards = lax.axis_size("fsdp")
    part = width // shards // count
    return jnp.concatenate(
        [
            lax.dynamic_slice(
                matrix, (0, start + shard * (width // shards) + share * part), (matrix.shape[0], part)
            )
            for start in range(0, matrix.shape[1], width)
            for shard in range(shards)
        ],
        1,
    )


def pick_rows(matrix, share, count):
    part = matrix.shape[0] // count
    return lax.dynamic_slice(matrix, (share * part, 0), (part, matrix.shape[1]))


SPREAD_CHUNKS = 4
SPREAD_MOVES = 3 * SPREAD_CHUNKS + 1
FFN_CHUNKS = 2 * SPREAD_CHUNKS


class Spread:
    def __init__(self, rows_of, out_ref, send, recv):
        self.rows_of, self.out_ref, self.send, self.recv = rows_of, out_ref, send, recv
        _, self.core, _, self.beside, _ = peers()
        step = out_ref.shape[2] // SPREAD_CHUNKS
        self.parts = [pl.ds(k * step, step) for k in range(SPREAD_CHUNKS)]

    def side(self, k, slot):
        number = 2 * k + slot
        return remote_copy(
            self.rows_of(slot, self.parts[k]),
            self.out_ref.at[0, 2 + slot, self.parts[k]],
            self.send.at[number],
            self.recv.at[number],
            self.beside,
        )

    def over(self, k):
        number = 2 * SPREAD_CHUNKS + 1 + k
        part = self.parts[k]
        return remote_copy(
            self.out_ref.at[0, 2:4, part],
            self.out_ref.at[1, 2:4, part],
            self.send.at[number],
            self.recv.at[number],
            self.core,
        )

    def near(self):
        number = 2 * SPREAD_CHUNKS
        return remote_copy(
            self.out_ref.at[0, 0:2],
            self.out_ref.at[1, 0:2],
            self.send.at[number],
            self.recv.at[number],
            self.core,
        )

    def first(self, k):
        self.side(k, 0).start()
        self.side(k, 1).start()

    def second(self, k):
        self.side(k, 0).wait_recv()
        self.side(k, 1).wait_recv()
        self.over(k).start()

    def end(self):
        self.near().wait()
        for k in range(SPREAD_CHUNKS):
            self.over(k).wait()
            self.side(k, 0).wait_send()
            self.side(k, 1).wait_send()


def start_kernel(
    small_ref,
    tokens_ref,
    ffn_sent,
    small_out,
    normed_out,
    ffn_out,
    local,
    small_send,
    small_recv,
    spread_send,
    spread_recv,
    cross_send,
    cross_recv,
):
    x, z = lax.axis_index("section"), lax.axis_index("fsdp")
    shards = lax.axis_size("fsdp")
    _, core, across, beside, _ = peers()
    others = [
        {"section": (x + step // shards) % 2, "fsdp": (z + step) % shards} for step in range(1, 2 * shards)
    ]
    greet([core, beside] + others)
    smalls = [
        remote_copy(small_ref, small_out.at[x, z], small_send.at[step], small_recv.at[step], device)
        for step, device in enumerate(others)
    ]
    step = ffn_sent.shape[0] // FFN_CHUNKS
    crossing = []
    for k in range(FFN_CHUNKS):
        part = pl.ds(k * step, step)
        crossing.append(
            remote_copy(
                ffn_sent.at[part], ffn_out.at[part], cross_send.at[k], cross_recv.at[k], across
            )
        )
    keep = pltpu.make_async_copy(small_ref, small_out.at[x, z], local.at[0])
    normed = Spread(lambda slot, part: normed_out.at[0, slot, part], normed_out, spread_send, spread_recv)
    for one in smalls + [keep]:
        one.start()
    crossing[0].start()
    for one in smalls:
        one.wait_recv()
    keep.wait()
    gain = jnp.concatenate([small_out[0, shard, 0:1] for shard in range(shards)], 1)
    for k in range(SPREAD_CHUNKS):
        for slot, place in ((x, 0), (1 - x, 1)):
            part = normed.parts[k]
            normed_out[0, place, part] = normed_with(tokens_ref[slot, part].astype(jnp.float32), gain)
        normed.first(k)
        if k >= 1:
            crossing[k].start()
    normed.near().start()
    for k in range(SPREAD_CHUNKS):
        crossing[SPREAD_CHUNKS + k].start()
        normed.second(k)
    normed.end()
    for one in crossing:
        one.wait()
    for one in smalls:
        one.wait_send()


def start(small, tokens, ffn_sent):
    shards = lax.axis_size("fsdp")
    _, rows, width = tokens.shape
    f32, bf16 = jnp.float32, jnp.bfloat16
    if not kernels_fit():
        seq_count = lax.axis_size("seq")
        every = lax.all_gather(small, ("section", "fsdp"), axis=0).reshape(2, shards, *small.shape)
        gain = every[0, :, 0].reshape(width)
        return (
            every,
            normed_with(spread_plainly(tokens).astype(f32), gain),
            flip(ffn_sent, seq_count),
        )
    place = pl.BlockSpec(memory_space=pltpu.VMEM)
    anywhere = pl.BlockSpec(memory_space=pl.ANY)
    return pl.pallas_call(
        start_kernel,
        out_shape=[
            jax.ShapeDtypeStruct((2, shards, *small.shape), f32),
            jax.ShapeDtypeStruct((2, 4, rows, width), bf16),
            jax.ShapeDtypeStruct(ffn_sent.shape, bf16),
        ],
        in_specs=[place] * 2 + [anywhere],
        out_specs=[place] * 2 + [anywhere],
        scratch_shapes=[
            pltpu.SemaphoreType.DMA((1,)),
            pltpu.SemaphoreType.DMA((2 * shards - 1,)),
            pltpu.SemaphoreType.DMA((2 * shards - 1,)),
            pltpu.SemaphoreType.DMA((SPREAD_MOVES,)),
            pltpu.SemaphoreType.DMA((SPREAD_MOVES,)),
            pltpu.SemaphoreType.DMA((FFN_CHUNKS,)),
            pltpu.SemaphoreType.DMA((FFN_CHUNKS,)),
        ],
        compiler_params=pltpu.CompilerParams(
            collective_id=21, has_side_effects=True, vmem_limit_bytes=VMEM_BYTES
        ),
        cost_estimate=lasting(55),
        name="start",
    )(small, tokens, ffn_sent)


def spread_kernel(rows_ref, out_ref, local, send, recv):
    x = lax.axis_index("section")
    _, core, _, beside, _ = peers()
    greet([core, beside])
    keeps = [
        pltpu.make_async_copy(rows_ref.at[x], out_ref.at[0, 0], local.at[0]),
        pltpu.make_async_copy(rows_ref.at[1 - x], out_ref.at[0, 1], local.at[1]),
    ]
    for one in keeps:
        one.start()
    move = Spread(lambda slot, part: rows_ref.at[x if slot == 0 else 1 - x, part], out_ref, send, recv)
    for k in range(SPREAD_CHUNKS):
        move.first(k)
    for one in keeps:
        one.wait()
    move.near().start()
    for k in range(SPREAD_CHUNKS):
        move.second(k)
    move.end()


def spread_slots(tokens):
    _, rows, width = tokens.shape
    if not kernels_fit():
        return spread_plainly(tokens)
    place = pl.BlockSpec(memory_space=pltpu.VMEM)
    return pl.pallas_call(
        spread_kernel,
        out_shape=jax.ShapeDtypeStruct((2, 4, rows, width), tokens.dtype),
        in_specs=[place],
        out_specs=place,
        scratch_shapes=[
            pltpu.SemaphoreType.DMA((2,)),
            pltpu.SemaphoreType.DMA((SPREAD_MOVES,)),
            pltpu.SemaphoreType.DMA((SPREAD_MOVES,)),
        ],
        compiler_params=pltpu.CompilerParams(
            collective_id=22, has_side_effects=True, vmem_limit_bytes=VMEM_BYTES
        ),
        cost_estimate=lasting(42),
        name="spread_slots",
    )(tokens)


def spread_plainly(tokens):
    x = lax.axis_index("section")
    _, rows, width = tokens.shape
    near = jnp.concatenate(
        [lax.dynamic_index_in_dim(tokens, x, 0, False), lax.dynamic_index_in_dim(tokens, 1 - x, 0, False)], 0
    )
    for step in chip_bits()[1:]:
        near = jnp.concatenate([near, flip(near, step)], 0)
    return jnp.stack([near, flip(near, 1)]).reshape(2, -1, rows, width)


def body(
    tokens,
    in_weight,
    conv_kernel,
    out_weight,
    gate_weight,
    up_weight,
    down_weight,
    mixer_gain,
    ffn_gain,
    cotangent,
):
    bf16, f32 = jnp.bfloat16, jnp.float32
    x_index = lax.axis_index("section")
    q_index = lax.axis_index("seq")
    seq_count = lax.axis_size("seq")
    count = lax.axis_size("section") * seq_count
    shards = lax.axis_size("fsdp")
    share = x_index * seq_count + q_index
    first_plane = x_index == 0
    width = tokens.shape[3]
    rows = tokens.shape[2]
    hidden_width = gate_weight.shape[2]
    shard_rows = width // shards
    in_columns = 3 * width // count
    channels = width // count
    ffn_columns = hidden_width // count
    ffn_pad = -(-ffn_columns // 128) * 128
    units = half_units()
    half = len(units)
    part = shard_rows // count

    other = share ^ seq_count

    def in_share(index):
        return pick_columns(in_weight[0], index, width, count)

    def out_share(index):
        return pick_rows(out_weight[0], index, count)

    def ffn_share(index):
        nothing = jnp.zeros((shard_rows, ffn_pad - ffn_columns), bf16)
        return jnp.concatenate(
            [
                pick_columns(gate_weight[0], index, hidden_width, count),
                nothing,
                pick_columns(up_weight[0], index, hidden_width, count),
                nothing,
                pick_rows(down_weight[0], index, count).reshape(shard_rows, -1),
            ],
            1,
        )

    small = jnp.concatenate(
        [
            mixer_gain.astype(f32),
            ffn_gain.astype(f32),
            conv_kernel[0].T.astype(f32),
            jnp.zeros((3, shard_rows), f32),
        ],
        0,
    )
    def over_fsdp(value):
        return lax.all_gather(value, "fsdp", axis=0, tiled=True)

    def pack_rows(value):
        return value.reshape(part, count, channels).transpose(1, 0, 2).reshape(shard_rows, channels)

    def unpack_rows(value):
        return value.reshape(-1, count, part, channels).transpose(0, 2, 1, 3).reshape(-1, width)

    def mixer_share(index):
        return jnp.concatenate([in_share(index), pack_rows(out_share(index))], 1)

    def over_mixers(value):
        value = over_fsdp(value)
        return value[:, :in_columns], unpack_rows(value[:, in_columns:])

    mixer_own = over_mixers(mixer_share(share))
    mixer_sent = flip(mixer_share(other), seq_count)
    mixer_sent, ffn_kept, ffn_sent = tie(mixer_sent, ffn_share(share), ffn_share(other))
    small, mixer_sent = tie(small, mixer_sent)
    small, normed, ffn_sent = start(small, tokens[:, 0], ffn_sent)
    mixer_across = over_mixers(mixer_sent)
    mixer_matrices = [
        [jnp.where(first_plane == kept, own, across) for own, across in zip(mixer_own, mixer_across)]
        for kept in (True, False)
    ]
    ffn_parts = [
        jnp.where(first_plane, ffn_kept, ffn_sent),
        jnp.where(first_plane, ffn_sent, ffn_kept),
    ]
    small = small.transpose(0, 2, 1, 3)
    whole = small.reshape(2, 8, width)
    taps_all = lax.dynamic_slice(
        small[:, 2:5].reshape(2, 3, shards, count, part), (0, 0, 0, share, 0), (2, 3, shards, 1, part)
    ).reshape(2, 3, shards * part)

    pair_columns = 2 * ffn_pad
    pair = over_fsdp(ffn_parts[0][:, :pair_columns])
    normed, grad_rows = tie(normed, cotangent[:, 0])
    normed, grad_units, down_part = tie(normed, spread_slots(grad_rows), ffn_parts[0][:, pair_columns:])
    down = over_fsdp(down_part.reshape(-1, width))
    ids = jnp.stack([share ^ unit ^ side for side in (0, 1) for unit in units])
    has_before = (ids % seq_count) > 0
    has_after = (ids % seq_count) < seq_count - 1
    before_pick = (ids[None, :] == (ids - 1)[:, None]) & has_before[:, None]
    after_pick = (ids[None, :] == (ids + 1)[:, None]) & has_after[:, None]

    def pick_units(mask, edge):
        return jnp.sum(jnp.where(mask[:, :, None, None], edge[None].astype(f32), 0.0), 1)

    def flat(value):
        return value.reshape(2 * half * rows, value.shape[-1])

    def in_units(value):
        return value.reshape(2, half, rows, value.shape[-1])

    def gain_row(block, kind):
        return whole[block, kind : kind + 1]

    stream = lax.dynamic_index_in_dim(tokens[:, 0], x_index, 0, False)
    saved = []
    outputs = []
    for block in range(2):
        in_matrix, out_matrix = mixer_matrices[block]
        taps = taps_all[block]
        if kernels_fit():
            projected, held, gated = mixer_forward(normed, in_matrix, taps)
            gated = flat(gated)
            if block == 1:
                gated, crossed_out = tie(gated, crossed_out)
        else:
            projected = times(flat(normed), in_matrix[:, :in_columns])
            b_gate = projected[:, :channels]
            c_gate = projected[:, channels : 2 * channels]
            x_value = projected[:, 2 * channels :]
            conv_input = (b_gate * x_value).astype(bf16).reshape(2 * half, rows, channels)
            earlier = pick_units(before_pick, conv_input[:, -2:])
            held = jnp.concatenate([earlier, conv_input.astype(f32)], 1)
            conv_out = taps[0] * held[:, :-2] + taps[1] * held[:, 1:-1] + taps[2] * held[:, 2:]
            gated = flat((c_gate.reshape(conv_out.shape) * conv_out).astype(bf16))
        (middle,), _, normed_ffn, _, _ = exchange(
            finish_middle,
            in_units(gated),
            out_matrix,
            False,
            [stream],
            [gain_row(block, 1)],
            [f32],
            0,
            True,
            1 + 2 * block,
        )
        if block == 0:
            ffn_matrices = [(pair, down), None]
        pair_matrix, down_matrix = ffn_matrices[block]
        if kernels_fit():
            pairs, hidden = ffn_forward(flat(normed_ffn), pair_matrix, ffn_pad, ffn_columns)
        else:
            pairs = times(flat(normed_ffn), pair_matrix[:, :pair_columns])
            hidden = (jax.nn.silu(pairs[:, :ffn_pad]) * pairs[:, ffn_pad:]).astype(bf16)[:, :ffn_columns]
        if block == 0:
            hidden, down, pair_value, down_value = tie(
                hidden, down, ffn_parts[1][:, :pair_columns], ffn_parts[1][:, pair_columns:].reshape(-1, width)
            )
            down_matrix = down
            ffn_matrices = [(pair, down), (over_fsdp(pair_value), over_fsdp(down_value))]
        saved.append((stream, normed, projected, held, gated, middle, normed_ffn, pairs, hidden))
        if block == 0:
            (stream,), _, normed, _, _ = exchange(
                finish_block,
                in_units(hidden),
                down_matrix,
                False,
                [middle],
                [gain_row(1, 0)],
                [bf16],
                0,
                True,
                2,
            )
            outputs.append(stream)
            crossed_out = flip(stream, seq_count)
        else:
            last_sum = (in_units(hidden), down_matrix, middle)

    upstream = lax.dynamic_index_in_dim(cotangent[:, 0], x_index, 0, False)
    stream_grads = [None, None]
    small_grads = [None, None]
    matrix_grads = [None, None]

    def over_z(value):
        return lax.psum_scatter(value, "fsdp", scatter_dimension=0, tiled=True)

    def product(left, right):
        return by_rows(row_products(left, right))

    def small_rows(mixer_gain_part, ffn_gain_part, taps_placed):
        return jnp.concatenate(
            [
                mixer_gain_part.reshape(1, width),
                ffn_gain_part.reshape(1, width),
                taps_placed,
                jnp.zeros((3, width), f32),
            ],
            0,
        )

    def small_values():
        return jnp.stack(small_grads).reshape(2, 8, shards, shard_rows).transpose(0, 2, 1, 3)

    def to_section(value, block):
        over = [((1 - block) * seq_count + seq, block * seq_count + seq) for seq in range(seq_count)]
        return lax.ppermute(value, PLANE, over)

    inside = chip_bits()[1:] + [1]
    relative = [0, seq_count]
    for bits in inside:
        relative = relative + [unit | bits for unit in relative]

    def to_owners(value, block):
        held = [value, to_section(value, block)]
        for bits in inside:
            over = [
                (block * seq_count + seq, block * seq_count + (seq ^ bits)) for seq in range(seq_count)
            ]
            held = held + [lax.ppermute(unit, PLANE, over) for unit in held]
        return held

    mixer_sum = jnp.zeros((), f32)
    for block in (1, 0):
        in_matrix, out_matrix = mixer_matrices[block]
        pair_matrix, down_matrix = ffn_matrices[block]
        taps = taps_all[block]
        (stream, normed, projected, held, gated, middle, normed_ffn, pairs, hidden) = saved[block]
        down_product = product(hidden, flat(grad_units))
        if block == 1:
            down_product, grad_units = tie(down_product, grad_units)
        else:
            grad_units, mixer_sum = tie(grad_units, mixer_sum)
        if block == 0:
            matrix_grads[1] = (down_grad, pair_grad, mixer_sum)
        down_product = down_product.reshape(shards, -1, width)
        if kernels_fit():
            grad_pairs = ffn_backward(flat(grad_units), down_matrix, pairs, ffn_pad)
            if block == 0:
                grad_pairs, crossed = tie(grad_pairs, crossed)
        else:
            gate_value, up_value = pairs[:, :ffn_pad], pairs[:, ffn_pad:]
            grad_hidden = times_transposed(flat(grad_units), down_matrix)
            grad_hidden = jnp.pad(grad_hidden, ((0, 0), (0, ffn_pad - ffn_columns)))
            sigmoid_gate = jax.nn.sigmoid(gate_value)
            grad_gate = grad_hidden * up_value * sigmoid_gate * (1.0 + gate_value * (1.0 - sigmoid_gate))
            grad_up = grad_hidden * gate_value * sigmoid_gate
            grad_pairs = jnp.concatenate([grad_gate, grad_up], 1).astype(bf16)
        grad_pairs, pair_product = tie(grad_pairs, product(flat(normed_ffn), grad_pairs))
        pair_grad = over_z(pair_product)
        (grad_middle,), (ffn_gain_part,), mixer_grad, _, _ = exchange(
            finish_gradient,
            in_units(grad_pairs),
            pair_matrix,
            True,
            [upstream, middle],
            [gain_row(block, 1)],
            [f32],
            1,
            True,
            8 - 2 * block,
        )
        if kernels_fit():
            grad_projected, taps_part = mixer_backward(mixer_grad, out_matrix, projected, held, taps)
            grad_projected, taps_part = flat(grad_projected), taps_part[:3]
            mixer_product = mixer_products(flat(normed), grad_projected, gated, flat(mixer_grad))
        else:
            grad_gated = times_transposed(flat(mixer_grad), out_matrix).reshape(2 * half, rows, channels)
            b_gate = projected[:, :channels].reshape(2 * half, rows, channels)
            c_gate = projected[:, channels : 2 * channels].reshape(2 * half, rows, channels)
            x_value = projected[:, 2 * channels :].reshape(2 * half, rows, channels)
            conv_out = taps[0] * held[:, :-2] + taps[1] * held[:, 1:-1] + taps[2] * held[:, 2:]
            grad_cgate = grad_gated * conv_out
            grad_conv = grad_gated * c_gate
            later = pick_units(after_pick, grad_conv[:, :2])
            grad_extended = jnp.concatenate([grad_conv, later], 1)
            grad_input = (
                taps[0] * grad_extended[:, 2:]
                + taps[1] * grad_extended[:, 1:-1]
                + taps[2] * grad_extended[:, :-2]
            )
            taps_part = jnp.stack(
                [jnp.sum(grad_conv * held[:, tap : tap + rows], (0, 1)) for tap in range(3)], 0
            )
            grad_projected = flat(
                jnp.concatenate([grad_input * x_value, grad_cgate, grad_input * b_gate], 2).astype(bf16)
            )
            in_grad = row_products(flat(normed), grad_projected)
            out_grad = row_products(gated, flat(mixer_grad)).reshape(shards, part, count, channels)
            out_grad = out_grad.transpose(0, 2, 1, 3).reshape(width, channels)
            mixer_product = jnp.concatenate([in_grad, out_grad], 1)
        grad_projected, mixer_product, pair_grad = tie(
            grad_projected, mixer_product, pair_grad
        )
        if block == 1 or not kernels_fit():
            mixer_sum = over_z(mixer_product)
        own_mask = (jnp.arange(count) == share)[None, None, :, None]
        taps_placed = jnp.where(own_mask, taps_part.reshape(3, shards, 1, part), 0.0).reshape(3, width)
        if block == 0 and kernels_fit():
            break
        (grad_stream,), (mixer_gain_part,), sent, down_grad, result = exchange(
            finish_gradient,
            in_units(grad_projected),
            in_matrix,
            True,
            [grad_middle, stream],
            [gain_row(block, 0)],
            [f32],
            1,
            block == 1,
            9 - 2 * block,
            product=down_product,
            extra=last_sum if block else None,
        )
        if block == 1:
            outputs.append(result)
        stream_grads[block] = grad_stream
        small_grads[block] = small_rows(mixer_gain_part, ffn_gain_part, taps_placed)
        if block == 0:
            matrix_grads[0] = (down_grad, pair_grad, mixer_sum)
        if block == 1:
            upstream = sent[0, 0]
            grad_units = sent
            crossed = flip(result, seq_count)

    def in_order(index):
        second = to_owners(matrix_grads[1][index], 1)
        first = to_owners(matrix_grads[0][index], 0)
        ordered = jnp.zeros((count, *first[0].shape), bf16)
        for unit, one, two in zip(relative, first, second):
            ordered = lax.dynamic_update_index_in_dim(
                ordered, jnp.where(first_plane, one, two), share ^ unit, 0
            )
        return ordered

    def columns_of(value, blocks):
        piece = value.reshape(count, shard_rows, blocks, shards, -1)
        return piece.transpose(1, 2, 3, 0, 4).reshape(shard_rows, -1).astype(f32)

    if kernels_fit():
        small_grads[0] = small_rows(jnp.zeros((1, width), f32), ffn_gain_part, taps_placed)
        later = matrix_grads[1]
        stream_grads[0], crossed_last, smalls, pair_grad, down_grad, mixer_sum = last_exchange(
            in_units(grad_projected),
            in_matrix,
            grad_middle,
            stream,
            gain_row(0, 0),
            small_values(),
            upstream,
            mixer_product.reshape(shards, shard_rows, -1),
            down_product,
            later[2],
            later[0],
            (pair_grad, later[1]),
        )
        gate_grad, up_grad = place_columns(pair_grad, 2, hidden_width, ffn_pad, False)
        (in_grad,) = place_columns(mixer_sum, 3, width, channels, True)
    else:
        crossed_last = flip(jnp.stack([grad.astype(bf16) for grad in stream_grads]), seq_count)
        smalls = lax.psum(small_values(), ("section", "seq", "fsdp"))
        smalls = lax.dynamic_slice(
            smalls, (x_index, lax.axis_index("fsdp"), 0, 0), (1, 1, *smalls.shape[2:])
        )[0, 0]
        down_grad, pair_grad, mixer_sum = in_order(0), in_order(1), in_order(2)
        gate_grad = columns_of(pair_grad[..., :ffn_columns], 1)
        up_grad = columns_of(pair_grad[..., ffn_pad : ffn_pad + ffn_columns], 1)
        in_grad = columns_of(mixer_sum[..., :in_columns], 3)
    down_grad = down_grad.reshape(-1, width).astype(f32)
    if kernels_fit():
        out_grad = place_rows(mixer_sum, in_columns, width)
    else:
        out_grad = unpack_rows(mixer_sum[..., in_columns:]).astype(f32)

    def by_slot(values, crossed, dtype):
        kept = jnp.where(first_plane, values[0], values[1]).astype(dtype)
        other = jnp.where(first_plane, crossed[0], crossed[1]).astype(dtype)
        return jnp.stack(
            [jnp.where(first_plane, kept, other), jnp.where(first_plane, other, kept)], 0
        )

    return (
        by_slot(outputs, (crossed_out, crossed), bf16)[None, :, None],
        by_slot(stream_grads, (crossed_last[0], crossed_last[1]), f32)[None, :, None],
        in_grad[None],
        smalls[2:5].T[None],
        out_grad[None],
        gate_grad[None],
        up_grad[None],
        down_grad[None],
        smalls[0][None],
        smalls[1][None],
    )


def solution(mesh):
    placed = (
        P(None, "fsdp", "seq", None),
        P("section", "fsdp", None),
        P("section", "fsdp", None),
        P("section", "fsdp", None),
        P("section", "fsdp", None),
        P("section", "fsdp", None),
        P("section", "fsdp", None),
        P("section", "fsdp"),
        P("section", "fsdp"),
        P(None, "fsdp", "seq", None),
    )
    return jax.shard_map(
        body,
        mesh=mesh,
        in_specs=placed,
        out_specs=(
            P("section", None, "fsdp", "seq", None),
            P("section", None, "fsdp", "seq", None),
            P("section", "fsdp", None),
            P("section", "fsdp", None),
            P("section", "fsdp", None),
            P("section", "fsdp", None),
            P("section", "fsdp", None),
            P("section", "fsdp", None),
            P("section", "fsdp"),
            P("section", "fsdp"),
        ),
        check_vma=False,
    )
```
